32 devices in a mesh: groups: 2 (over x), pts: 4 (over y, core), feat: 4 (over z).
Axes of the slice: x: 2, y: 2, z: 4, core: 2. Of those that a mesh axis runs over, the one named last changes fastest.
Arguments:
- points: bfloat16 [16384, 256], P(('groups', 'pts')), parts along dimension 0, may hold values from -6 to 6
- picks: int32 [2, 4096], P(None, ('groups', 'pts')), parts along dimension 1, may hold values from 0 to 2047, as said below
- omega: bfloat16 [256, 32768], P(None, 'feat'), may hold values from -1 to 1
- phase: float32 [32768], P('feat'), may hold values from -3.140625 to 3.140625
- weights: bfloat16 [65536, 256], P(('groups', 'feat')), parts along dimension 0, may hold values from -3 to 3
- counts: int32 [2, 4096, 256], P(None, ('groups', 'pts')), parts along dimension 1, may hold values from 0 to 2
- master: float32 [8, 8192, 256], P(('groups', 'feat'), 'pts'), parts along dimension 0, may hold values from -0.06 to 0.06
- moment_one: float32 [8, 8192, 256], P(('groups', 'feat'), 'pts'), parts along dimension 0, may hold values from -1.8 to 1.8
- moment_two: float32 [8, 8192, 256], P(('groups', 'feat'), 'pts'), parts along dimension 0, may hold values from 1 to 20
- task_cov: bfloat16 [256, 256], replicated, may hold values from -1 to 3, as said below
Outputs:
- log_rates: float32 [2, 4096, 256], P(None, ('groups', 'pts')), parts along dimension 1
- new_master: float32 [8, 8192, 256], P(('groups', 'feat'), 'pts'), parts along dimension 0
- new_first: float32 [8, 8192, 256], P(('groups', 'feat'), 'pts'), parts along dimension 0
- new_second: float32 [8, 8192, 256], P(('groups', 'feat'), 'pts'), parts along dimension 0
- new_working: bfloat16 [65536, 256], P(('groups', 'feat')), parts along dimension 0
The draws below stay inside these ranges and needn't reach their ends.
There are 2 independent parts, one for each index of `groups`. The reference program is written for one: setup_inputs(seed, part) draws one part's arguments, and reference() takes and returns one part's arrays. A program takes and returns all parts, laid end to end along the dimension named above; an argument that names none is the same for every part. Nothing has to cross between parts.
Inputs may be any that keep to these rules, and one draw needn't show every extreme that they name: picks[m, i] names a point among the 2048 points of the same pts index as point i. `task_cov`: symmetric, diagonal entries between 1 and 3, entries off the diagonal at most 1 in magnitude.
All inputs are finite; a program needn't handle non-finite values.
Results may differ from the reference program's by a relative error of at most 0.0055.
Values may be sent and summed in bfloat16 or wider, within the bound.
No kernel may reach another device: no remote copies, remote signals or barrier semaphores. Data moves between devices by JAX's collectives and lax.ppermute only.
A program may use at most 128 MiB of HBM per device.

```python
import math
import jax
import jax.numpy as jnp
from jax import lax

F = 32768
K = 256
IN = 256
STEP = 20
BATCH_DEV = 512
POOL_DEV = 2048
BATCH = 2048
POOL = 8192
FEAT_DEV = 8192
N_FEAT = 4


def draw_picks(key, part):
    key = jax.random.fold_in(key, 11)
    chosen = jax.random.randint(key, (2, BATCH), 0, POOL_DEV, dtype=jnp.int32)
    chosen = chosen.at[:, ::BATCH_DEV].set(POOL_DEV - 1)
    return chosen.at[:, 1::BATCH_DEV].set(0)


def draw_task_cov(key, part):
    key = jax.random.fold_in(key, 7)
    noise = jax.random.normal(key, (K, K), jnp.float32) * (0.5 / math.sqrt(K))
    return (noise + noise.T + 2.0 * jnp.eye(K, dtype=jnp.float32)).astype(jnp.bfloat16)


def touch_ends(entries, key, low, top_value):
    extent = entries.shape
    place = [jax.random.randint(jax.random.fold_in(key, axis), (), 0, extent[axis]) for axis in range(len(extent))]
    entries = entries.at[tuple(place)].set(low)
    longest = extent.index(max(extent))
    place[longest] = (place[longest] + 1) % extent[longest]
    return entries.at[tuple(place)].set(top_value)


def levels(stream_key, extent, split, smallest, largest):
    def one(dim, shards_of):
        draws = jax.random.uniform(jax.random.fold_in(jax.random.fold_in(stream_key, 6), dim), (shards_of,), jnp.float32, smallest / len(split), largest / len(split))
        return jnp.repeat(jnp.exp(draws), extent[dim] // shards_of).reshape((-1,) + (1,) * (len(extent) - dim - 1))

    gain = one(*split[0])
    for cut in split[1:]:
        gain = gain * one(*cut)
    return gain


def gaussian(rng, shape, scale, reach, split=(), held_as=jnp.bfloat16):
    array = jax.random.normal(rng, shape, jnp.float32) * scale
    if len(split) > 0:
        array = levels(rng, shape, split, -0.22, 0.18) * array
    return jnp.clip(array, min=-reach, max=reach).astype(held_as)


def setup_inputs(seed: int = 0, part: int = 0) -> dict:
    seeds = jax.random.split(jax.random.key(seed), 11)
    own_keys = jax.random.split(jax.random.fold_in(seeds[10], part), 11)
    return {
        "points": gaussian(own_keys[0], (POOL, IN), 1.0, 6.0, ((0, 4),)),
        "picks": draw_picks(jax.random.fold_in(jax.random.fold_in(seeds[10], part), 71), part),
        "omega": gaussian(seeds[2], (IN, F), (IN // 9) ** -0.5, 1.0, ((1, 4),)),
        "phase": jnp.clip(jax.random.uniform(seeds[3], (F,), jnp.float32, -3.140625, 3.140625), -3.140625, 3.140625),
        "weights": gaussian(own_keys[4], (F, K), 0.5, 3.0, ((0, 4),)),
        "counts": touch_ends(jax.random.randint(own_keys[5], (2, BATCH, K), 0, 3), jax.random.fold_in(own_keys[5], 1), 0, 2).astype(jnp.int32),
        "master": gaussian(own_keys[6], (N_FEAT, FEAT_DEV, K), 0.01, 0.06, ((0, 4), (1, 4)), jnp.float32),
        "moment_one": gaussian(own_keys[7], (N_FEAT, FEAT_DEV, K), 0.3, 1.8, ((0, 4), (1, 4)), jnp.float32),
        "moment_two": jnp.clip(jnp.exp(math.log(20.0) - 2.9957323 * jax.random.uniform(own_keys[8], (N_FEAT, FEAT_DEV, K), jnp.float32) ** levels(own_keys[8], (N_FEAT, FEAT_DEV, K), ((0, 4), (1, 4)), -0.2, 0.2)), 1.0, 20.0),
        "task_cov": draw_task_cov(jax.random.fold_in(seeds[10], 71), part),
    }


beta_one = 0.9
beta_two = 0.999
learn_rate = 0.2

def feature_block(chosen, block_omega, block_phase):
    angle = jnp.dot(chosen, block_omega, preferred_element_type=jnp.float32) + block_phase
    return (math.sqrt(2.0 / F) * jnp.cos(angle)).astype(jnp.bfloat16)

def reference(points, picks, omega, phase, weights, counts, master, moment_one, moment_two, task_cov):
    offsets = jnp.arange(BATCH, dtype=jnp.int32) // BATCH_DEV * POOL_DEV
    omega_blocks = jnp.transpose(omega.reshape(IN, N_FEAT, FEAT_DEV), (1, 0, 2))
    phase_blocks = phase.reshape(N_FEAT, FEAT_DEV)
    weight_blocks = weights.reshape(N_FEAT, FEAT_DEV, K)
    rate_list = []
    gradient = master
    for minibatch in range(2):
        chosen = points[offsets + picks[minibatch].astype(jnp.int32)]

        def add_block(running, pieces):
            feature_rows = feature_block(chosen, pieces[0], pieces[1])
            return (running + jnp.dot(feature_rows, pieces[2], preferred_element_type=jnp.float32), None)
        log_rate, unused = lax.scan(add_block, jnp.zeros((BATCH, K), jnp.float32), (omega_blocks, phase_blocks, weight_blocks))
        residual = (jnp.exp(log_rate) - counts[minibatch].astype(jnp.float32)).astype(jnp.bfloat16)

        def block_gradient(pieces):
            feature_rows = feature_block(chosen, pieces[0], pieces[1])
            return lax.dot_general(feature_rows, residual, (((0,), (0,)), ((), ())), preferred_element_type=jnp.float32)
        gradient = gradient + lax.map(block_gradient, (omega_blocks, phase_blocks))
        rate_list.append(log_rate)
    flat_gradient = gradient.reshape(F, K).astype(jnp.bfloat16)
    conditioned = jnp.dot(flat_gradient, task_cov, preferred_element_type=jnp.float32).reshape(N_FEAT, FEAT_DEV, K)
    correction_one = 1.0 - beta_one ** STEP
    correction_two = 1.0 - beta_two ** STEP
    new_first = beta_one * moment_one + (1.0 - beta_one) * conditioned
    new_second = beta_two * moment_two + (1.0 - beta_two) * conditioned * conditioned
    new_master = master - learn_rate * (new_first / correction_one) / (jnp.sqrt(new_second / correction_two) + 1e-08)
    new_working = new_master.reshape(F, K).astype(jnp.bfloat16)
    return (jnp.stack(rate_list), new_master, new_first, new_second, new_working)
```

```python
import functools
import math

import jax
import jax.numpy as jnp
from jax import lax
from jax.experimental import pallas as pl
from jax.experimental.pallas import tpu as pltpu
from jax.sharding import PartitionSpec as P

F = 32768
STEP = 20
CORES = 2

beta_one = 0.9
beta_two = 0.999
learn_rate = 0.2

SINE = tuple(
    c / 8.0
    for c in (3.141582022078924, -5.167142793540227, 2.541899000696469, -0.5546361258792201)
)
ROUNDER = 12582912.0
TURN = 1.0 / (2.0 * math.pi)
VMEM = 56 * 1024 * 1024

f32 = jnp.float32
bf16 = jnp.bfloat16


def scaled_cos(product, phase_turns):
    turns = product * TURN + phase_turns
    r = turns - ((turns + ROUNDER) - ROUNDER)
    s = r * r
    w = ((SINE[3] * s + SINE[2]) * s + SINE[1]) * s + SINE[0]
    w = w * r
    return (math.sqrt(2.0 / F) - w * w).astype(bf16)


def cost(seconds, moved):
    return pl.CostEstimate(flops=int(seconds * 1.0e15), bytes_accessed=int(moved), transcendentals=0)


def params(*semantics):
    return pltpu.CompilerParams(vmem_limit_bytes=VMEM, dimension_semantics=semantics or None)


def rates_kernel(n, tile, place, chosen, omega, phase, weights, own, *rest):
    others, feats, total = rest[: n - 1], rest[n - 1], rest[n]
    step = pl.program_id(0)
    width = omega.shape[1]
    for c in range(width // tile):
        cols = slice(c * tile, (c + 1) * tile)
        product = jnp.dot(chosen[...], omega[:, cols], preferred_element_type=f32)
        feats[:, cols] = scaled_cos(product, phase[:, cols])
    part = jnp.dot(feats[...], weights[...], preferred_element_type=f32)

    @pl.when(step == 0)
    def _():
        total[...] = part

    @pl.when(step > 0)
    def _():
        total[...] += part

    @pl.when(step == pl.num_programs(0) - 1)
    def _():
        rows = own.shape[0]
        me = place[0]
        own[...] = total[pl.ds(pl.multiple_of(me * rows, rows), rows), :]
        for d in range(1, n):
            c = lax.rem(me + d, n)
            others[d - 1][...] = total[pl.ds(pl.multiple_of(c * rows, rows), rows), :].astype(bf16)


def rates(place, chosen, m, omega, phase, weights, n):
    ins, feat_dev = omega.shape
    k = weights.shape[1]
    batch = chosen.shape[0] // 2
    width = min(1024, feat_dev)
    rows = batch // n
    grid = feat_dev // width
    return pl.pallas_call(
        functools.partial(rates_kernel, n, min(256, width)),
        grid_spec=pltpu.PrefetchScalarGridSpec(
            num_scalar_prefetch=1,
            grid=(grid,),
            in_specs=[
                pl.BlockSpec((batch, ins), lambda i, _: (m, 0)),
                pl.BlockSpec((ins, width), lambda i, _: (0, i)),
                pl.BlockSpec((1, width), lambda i, _: (0, i)),
                pl.BlockSpec((width, k), lambda i, _: (i, 0)),
            ],
            out_specs=[pl.BlockSpec((rows, k), lambda i, _: (0, 0))] * n,
            scratch_shapes=[pltpu.VMEM((batch, width), bf16), pltpu.VMEM((batch, k), f32)],
        ),
        out_shape=[jax.ShapeDtypeStruct((rows, k), f32)]
        + [jax.ShapeDtypeStruct((rows, k), bf16)] * (n - 1),
        compiler_params=params("arbitrary"),
        cost_estimate=cost(9e-6, 8 << 20),
        name="partial_log_rates",
    )(place, chosen, omega, phase, weights)


def features_kernel(tile, omega_rows, phase, chosen, out):
    for c in range(chosen.shape[0] // tile):
        cols = slice(c * tile, (c + 1) * tile)
        product = lax.dot_general(
            omega_rows[...], chosen[cols, :], (((1,), (1,)), ((), ())), preferred_element_type=f32
        )
        out[:, cols] = scaled_cos(product, phase[...])


def owned_features(omega_rows, phase, chosen):
    owned, ins = omega_rows.shape
    points = chosen.shape[0]
    rows = min(256, owned)
    return pl.pallas_call(
        functools.partial(features_kernel, min(256, points)),
        grid=(owned // rows,),
        in_specs=[
            pl.BlockSpec((rows, ins), lambda i: (i, 0)),
            pl.BlockSpec((rows, 1), lambda i: (i, 0)),
            pl.BlockSpec((points, ins), lambda i: (0, 0)),
        ],
        out_specs=pl.BlockSpec((rows, points), lambda i: (i, 0)),
        out_shape=jax.ShapeDtypeStruct((owned, points), bf16),
        compiler_params=params("arbitrary"),
        cost_estimate=cost(4.5e-6, 8 << 20),
        name="owned_features",
    )(omega_rows, phase, chosen)


def residual_kernel(n, has_out, place, *refs):
    chunks, observed = refs[:n], refs[n]
    rate_out, residual_out = refs[-2], refs[-1]
    rows = chunks[0].shape[0]
    me = place[0]
    for d in range(n):
        c = lax.rem(me + n - d, n)
        at = pl.ds(pl.multiple_of(c * rows, rows), rows)
        rate = chunks[d][...].astype(f32)
        rate_out[0, at, :] = rate
        residual_out[at, :] = (jnp.exp(rate) - observed[0, at, :].astype(f32)).astype(bf16)


def residuals(place, chunks, counts, m, before):
    n = len(chunks)
    rows, k = chunks[0].shape
    batch = counts.shape[1]
    args = [place, *chunks, counts]
    specs = [pl.BlockSpec((rows, k), lambda i, _: (0, 0))] * n + [
        pl.BlockSpec((1, batch, k), lambda i, _: (m, 0, 0))
    ]
    aliases = {}
    if before is not None:
        aliases = {len(args): 0}
        args.append(before)
        specs.append(pl.BlockSpec(memory_space=pl.ANY))
    return pl.pallas_call(
        functools.partial(residual_kernel, n, before is not None),
        grid_spec=pltpu.PrefetchScalarGridSpec(
            num_scalar_prefetch=1,
            grid=(1,),
            in_specs=specs,
            out_specs=[
                pl.BlockSpec((1, batch, k), lambda i, _: (m, 0, 0)),
                pl.BlockSpec((batch, k), lambda i, _: (0, 0)),
            ],
        ),
        out_shape=[
            jax.ShapeDtypeStruct(counts.shape, f32),
            jax.ShapeDtypeStruct((batch, k), bf16),
        ],
        input_output_aliases=aliases,
        compiler_params=params("arbitrary"),
        cost_estimate=cost(1e-6, 2 << 20),
        name="residuals",
    )(*args)


def update_kernel(n, features, residual, cov, master, first, second, *refs):
    new_master, new_first, new_second, sent, working = refs[-5:]
    batch = residual[0][0].shape[0]
    gradient = master[0]
    for s in range(n):
        for m in range(2):
            gradient += jnp.dot(
                features[s][:, m * batch : (m + 1) * batch],
                residual[s][m][...],
                preferred_element_type=f32,
            )
    conditioned = jnp.dot(gradient.astype(bf16), cov[...], preferred_element_type=f32)
    moved_first = beta_one * first[0] + (1.0 - beta_one) * conditioned
    moved_second = beta_two * second[0] + (1.0 - beta_two) * conditioned * conditioned
    correction_one = 1.0 - beta_one**STEP
    correction_two = 1.0 - beta_two**STEP
    moved = master[0] - learn_rate * (moved_first / correction_one) / (
        jnp.sqrt(moved_second / correction_two) + 1e-08
    )
    new_first[0] = moved_first
    new_second[0] = moved_second
    new_master[0] = moved
    rounded = moved.astype(bf16)
    sent[...] = rounded
    working[...] = rounded


def update(place, features, residual, cov, master, first, second, chunk, chunks, n_pts, before):
    n = len(features)
    owned, k = master.shape[1:]
    rows = min(256, owned // chunks)
    steps = owned // chunks // rows
    at = chunk * steps
    points = features[0].shape[1]
    batch = points // 2
    flat = [r for pair in residual for r in pair]
    state = pl.BlockSpec((1, rows, k), lambda i, _: (0, at + i, 0))
    args = [place, *features, *flat, cov, master, first, second]
    specs = (
        [pl.BlockSpec((rows, points), lambda i, _: (at + i, 0))] * n
        + [pl.BlockSpec((batch, k), lambda i, _: (0, 0))] * (2 * n)
        + [pl.BlockSpec(cov.shape, lambda i, _: (0, 0)), state, state, state]
    )
    aliases = {}
    if before is not None:
        aliases = {len(args) + j: o for j, o in enumerate((0, 1, 2, 4))}
        args += list(before)
        specs += [pl.BlockSpec(memory_space=pl.ANY)] * 4
    blocks = owned // rows

    def kernel(place, *refs):
        fs = refs[:n]
        rs = [refs[n + 2 * s : n + 2 * s + 2] for s in range(n)]
        update_kernel(n, fs, rs, *refs[3 * n :])

    return pl.pallas_call(
        kernel,
        grid_spec=pltpu.PrefetchScalarGridSpec(
            num_scalar_prefetch=1,
            grid=(steps,),
            in_specs=specs,
            out_specs=[
                state,
                state,
                state,
                pl.BlockSpec((rows, k), lambda i, _: (i, 0)),
                pl.BlockSpec((rows, k), lambda i, pt: (pt[1] * blocks + at + i, 0)),
            ],
        ),
        out_shape=[jax.ShapeDtypeStruct(master.shape, f32)] * 3
        + [
            jax.ShapeDtypeStruct((owned // chunks, k), bf16),
            jax.ShapeDtypeStruct((owned * n_pts, k), bf16),
        ],
        input_output_aliases=aliases,
        compiler_params=params("arbitrary"),
        cost_estimate=cost(4e-6, 8 << 20),
        name="update",
    )(*args)


def put_kernel(n, place, *refs):
    pieces, out, sems = refs[:n], refs[n + 1], refs[n + 2]
    copies = []
    for j in range(n):
        rows = pieces[j].shape[0]
        at = pl.ds(pl.multiple_of(place[j] * rows, rows), rows)
        copies.append(pltpu.make_async_copy(pieces[j], out.at[at, :], sems.at[j]))
    for copy in copies:
        copy.start()
    for copy in copies:
        copy.wait()


def put(working, pieces, blocks):
    n = len(pieces)
    any_spec = pl.BlockSpec(memory_space=pl.ANY)
    return pl.pallas_call(
        functools.partial(put_kernel, n),
        grid_spec=pltpu.PrefetchScalarGridSpec(
            num_scalar_prefetch=1,
            grid=(1,),
            in_specs=[any_spec] * (n + 1),
            out_specs=any_spec,
            scratch_shapes=[pltpu.SemaphoreType.DMA((n,))],
        ),
        out_shape=jax.ShapeDtypeStruct(working.shape, working.dtype),
        input_output_aliases={n + 1: 0},
        compiler_params=params("arbitrary"),
        cost_estimate=cost(1e-6, 1 << 20),
        name="put_rows",
    )(jnp.stack(blocks).astype(jnp.int32), *pieces, working)


def ring(x, axis, n, distance):
    return lax.ppermute(x, axis, [(i, (i + distance) % n) for i in range(n)])


def mate(x, n):
    return lax.ppermute(x, "pts", [(i, i ^ 1) for i in range(n)])


def across(x, n, distance):
    return ring(x, "pts", n, distance * CORES)


def spread(x, n):
    chips = n // CORES
    got = [x if d == 0 else across(x, n, d) for d in range(chips)]
    return [y for g in got for y in (g, mate(g, n))]


def body(n_feat, n_pts, points, picks, omega, phase, weights, counts, master, first, second, cov):
    f, p = lax.axis_index("feat"), lax.axis_index("pts")
    place = jnp.stack([f, p]).astype(jnp.int32)
    owned, k = master.shape[1:]
    chosen = points.at[picks.reshape(-1)].get(mode="promise_in_bounds")
    everyone = spread(chosen, n_pts)
    turns = phase * TURN
    omega_rows = lax.dynamic_slice_in_dim(omega, p * owned, owned, 1).T
    own_turns = lax.dynamic_slice_in_dim(turns, p * owned, owned, 0)[:, None]
    turns = turns[None, :]

    out_rates = None
    residual = []
    partial = [rates(place, chosen, m, omega, turns, weights, n_feat) for m in range(2)]
    omega_rows, own_turns, _ = lax.optimization_barrier((omega_rows, own_turns, partial[1][0]))
    for m in range(2):
        own, others = partial[m][0], partial[m][1:]
        total = own
        for d in range(1, n_feat):
            total = total + ring(others[d - 1], "feat", n_feat, d).astype(f32)
        chunk = total.astype(bf16)
        chunks = [chunk] + [ring(chunk, "feat", n_feat, d) for d in range(1, n_feat)]
        out_rates, res = residuals(place, chunks, counts, m, out_rates)
        residual.append(spread(res, n_pts))
    features = [owned_features(omega_rows, own_turns, e) for e in everyone]

    pairs = [(residual[0][s], residual[1][s]) for s in range(n_pts)]
    chunks = 4
    state = None
    sent = []
    for c in range(chunks):
        done = update(
            place, features, pairs, cov, master, first, second, c, chunks, n_pts, state
        )
        state = (done[0], done[1], done[2], done[4])
        sent.append(done[3])
    working = state[3]
    for c in range(chunks):
        pieces = spread(sent[c], n_pts)[1:]
        blocks = []
        for j in range(1, n_pts):
            d, other = j // CORES, j % CORES
            home = lax.rem(p + n_pts - d * CORES, n_pts)
            home = home + other * (1 - 2 * lax.rem(home, 2))
            blocks.append(home * chunks + c)
        working = put(working, pieces, blocks)
    return out_rates, state[0], state[1], state[2], working


def solution(mesh):
    placed = (
        P(("groups", "pts"), None),
        P(None, ("groups", "pts")),
        P(None, "feat"),
        P("feat"),
        P(("groups", "feat"), None),
        P(None, ("groups", "pts"), None),
        P(("groups", "feat"), "pts", None),
        P(("groups", "feat"), "pts", None),
        P(("groups", "feat"), "pts", None),
        P(),
    )
    return jax.shard_map(
        functools.partial(body, mesh.shape["feat"], mesh.shape["pts"]),
        mesh=mesh,
        in_specs=placed,
        out_specs=(
            P(None, ("groups", "pts"), None),
            P(("groups", "feat"), "pts", None),
            P(("groups", "feat"), "pts", None),
            P(("groups", "feat"), "pts", None),
            P(("groups", "feat"), None),
        ),
        check_vma=False,
    )
```

```python
import functools
import math

import jax
import jax.numpy as jnp
from jax import lax
from jax.experimental import pallas as pl
from jax.experimental.pallas import tpu as pltpu
from jax.sharding import PartitionSpec as P

F = 32768
STEP = 20
CORES = 2

beta_one = 0.9
beta_two = 0.999
learn_rate = 0.2

SINE = tuple(
    c / 8.0
    for c in (3.141582022078924, -5.167142793540227, 2.541899000696469, -0.5546361258792201)
)
ROUNDER = 12582912.0
TURN = 1.0 / (2.0 * math.pi)
VMEM = 30 * 1024 * 1024

f32 = jnp.float32
bf16 = jnp.bfloat16
IN_VMEM = pl.BlockSpec(memory_space=pltpu.VMEM)
ANYWHERE = pl.BlockSpec(memory_space=pl.ANY)


def scaled_cos(product, phase_turns):
    turns = product * TURN + phase_turns
    r = turns - ((turns + ROUNDER) - ROUNDER)
    s = r * r
    w = ((SINE[3] * s + SINE[2]) * s + SINE[1]) * s + SINE[0]
    w = w * r
    return (math.sqrt(2.0 / F) - w * w).astype(bf16)


TOKEN = jax.ShapeDtypeStruct((8, 128), f32)


def cost(microseconds):
    return pl.CostEstimate(
        flops=int(microseconds * 1.0e9), bytes_accessed=1 << 10, transcendentals=0
    )


def params():
    return pltpu.CompilerParams(vmem_limit_bytes=VMEM)


def rates_kernel(n, m, owned_blocks, f, p, picks, points, omega, phase, weights, *refs):
    chosen, owned, own, *others, token, feats, total = refs[-(n + 5) :]
    token[...] = jnp.zeros_like(token)
    step = pl.program_id(0)
    width = omega.shape[1]
    tile = min(256, width)
    pair = min(512, width)

    @pl.when(step == 0)
    def _():
        batch, pool = chosen.shape[0], points.shape[0]
        wanted = jnp.broadcast_to(picks[m : m + 1, :], (128, batch)).T
        lane = lax.broadcasted_iota(jnp.int32, (batch, 128), 1)
        hot = [
            jnp.where(wanted == lane + 128 * j, 1.0, 0.0).astype(bf16) for j in range(pool // 128)
        ]
        chosen[...] = jnp.dot(
            jnp.concatenate(hot, axis=1), points[...], preferred_element_type=f32
        ).astype(bf16)
        total[...] = jnp.zeros_like(total)

    turns = phase[...] * TURN
    part = None
    for c in range(width // tile):
        cols = slice(c * tile, (c + 1) * tile)
        product = jnp.dot(chosen[...], omega[:, cols], preferred_element_type=f32)
        feats[:, cols] = scaled_cos(product, turns[:, cols])
        if (c + 1) * tile % pair == 0:
            rows = slice((c + 1) * tile - pair, (c + 1) * tile)
            term = jnp.dot(feats[:, rows], weights[rows, :], preferred_element_type=f32)
            part = term if part is None else part + term
    total[...] += part

    @pl.when(step < owned_blocks)
    def _():
        owned[...] = feats[...]

    @pl.when(step == pl.num_programs(0) - 1)
    def _():
        rows = own.shape[0]
        me = f[0]
        own[...] = total[pl.ds(pl.multiple_of(me * rows, rows), rows), :]
        for d in range(1, n):
            c = lax.rem(me + d, n)
            others[d - 1][...] = total[pl.ds(pl.multiple_of(c * rows, rows), rows), :].astype(bf16)


def rates(f, p, picks, points, omega, phase, weights, m, n, owned, deps):
    ins, feat_dev = omega.shape
    k = weights.shape[1]
    batch = picks.shape[1]
    width = min(1024, owned)
    rows = batch // n
    grid = feat_dev // width
    blocks = owned // width

    def turned(i, p):
        return lax.rem(i + p[0] * blocks, grid)

    return pl.pallas_call(
        functools.partial(rates_kernel, n, m, blocks),
        grid_spec=pltpu.PrefetchScalarGridSpec(
            num_scalar_prefetch=2,
            grid=(grid,),
            in_specs=[
                IN_VMEM,
                IN_VMEM,
                pl.BlockSpec((ins, width), lambda i, f, p: (0, turned(i, p))),
                pl.BlockSpec((1, width), lambda i, f, p: (0, turned(i, p))),
                pl.BlockSpec((width, k), lambda i, f, p: (turned(i, p), 0)),
            ]
            + [IN_VMEM] * len(deps),
            out_specs=[
                IN_VMEM,
                pl.BlockSpec((batch, width), lambda i, f, p: (0, jnp.minimum(i, blocks - 1))),
            ]
            + [IN_VMEM] * (n + 1),
            scratch_shapes=[pltpu.VMEM((batch, width), bf16), pltpu.VMEM((batch, k), f32)],
        ),
        out_shape=[
            jax.ShapeDtypeStruct((batch, ins), bf16),
            jax.ShapeDtypeStruct((batch, owned), bf16),
            jax.ShapeDtypeStruct((rows, k), f32),
        ]
        + [jax.ShapeDtypeStruct((rows, k), bf16)] * (n - 1)
        + [TOKEN],
        compiler_params=params(),
        cost_estimate=cost(12),
        name="partial_log_rates",
    )(f, p, picks, points, omega, phase, weights, *deps)


def features_kernel(tile, p, chosen, omega, phase, *refs):
    out, token = refs[-2:]
    token[...] = jnp.zeros_like(token)
    turns = phase[...] * TURN
    for c in range(omega.shape[1] // tile):
        cols = slice(c * tile, (c + 1) * tile)
        product = jnp.dot(chosen[...], omega[:, cols], preferred_element_type=f32)
        out[:, cols] = scaled_cos(product, turns[:, cols])


def owned_features(p, chosen, omega, phase, owned, deps):
    points, ins = chosen.shape
    width = min(512, owned)
    blocks = owned // width
    return pl.pallas_call(
        functools.partial(features_kernel, min(256, width)),
        grid_spec=pltpu.PrefetchScalarGridSpec(
            num_scalar_prefetch=1,
            grid=(blocks,),
            in_specs=[
                IN_VMEM,
                pl.BlockSpec((ins, width), lambda i, p: (0, p[0] * blocks + i)),
                pl.BlockSpec((1, width), lambda i, p: (0, p[0] * blocks + i)),
            ]
            + [IN_VMEM] * len(deps),
            out_specs=[pl.BlockSpec((points, width), lambda i, p: (0, i)), IN_VMEM],
        ),
        out_shape=[jax.ShapeDtypeStruct((points, owned), bf16), TOKEN],
        compiler_params=params(),
        cost_estimate=cost(4),
        name="owned_features",
    )(p, chosen, omega, phase, *deps)


def total_kernel(n, *refs):
    out, token = refs[-2:]
    token[...] = jnp.zeros_like(token)
    value = refs[0][...]
    for r in refs[1:n]:
        value = value + r[...].astype(f32)
    out[...] = value.astype(bf16)


def total(terms, deps):
    return pl.pallas_call(
        functools.partial(total_kernel, len(terms)),
        in_specs=[IN_VMEM] * (len(terms) + len(deps)),
        out_specs=[IN_VMEM] * 2,
        out_shape=[jax.ShapeDtypeStruct(terms[0].shape, bf16), TOKEN],
        compiler_params=params(),
        cost_estimate=cost(0.5),
        name="total_rates",
    )(*terms, *deps)


def residual_kernel(n, m, f, *refs):
    chunks, observed = refs[:n], refs[n]
    rate_out, residual_out, token, held = refs[-4:]
    token[...] = jnp.zeros_like(token)
    rows = chunks[0].shape[0]
    me = f[0]
    for d in range(n):
        c = lax.rem(me + n - d, n)
        at = pl.ds(pl.multiple_of(c * rows, rows), rows)
        rate = chunks[d][...].astype(f32)
        rate_out[0, at, :] = rate
        held[at, :] = jnp.exp(rate) - observed[0, at, :].astype(f32)
    residual_out[...] = held[...].T.astype(bf16)


def residuals(f, chunks, counts, m, before, deps):
    n = len(chunks)
    k = chunks[0].shape[1]
    batch = counts.shape[1]
    args = [f, *chunks, counts, *deps]
    specs = [IN_VMEM] * n + [pl.BlockSpec((1, batch, k), lambda i, _: (m, 0, 0))]
    specs += [IN_VMEM] * len(deps)
    aliases = {}
    if before is not None:
        aliases = {len(args): 0}
        args.append(before)
        specs.append(ANYWHERE)
    return pl.pallas_call(
        functools.partial(residual_kernel, n, m),
        grid_spec=pltpu.PrefetchScalarGridSpec(
            num_scalar_prefetch=1,
            grid=(1,),
            in_specs=specs,
            out_specs=[pl.BlockSpec((1, batch, k), lambda i, _: (m, 0, 0)), IN_VMEM, IN_VMEM],
            scratch_shapes=[pltpu.VMEM((batch, k), f32)],
        ),
        out_shape=[
            jax.ShapeDtypeStruct(counts.shape, f32),
            jax.ShapeDtypeStruct((k, batch), bf16),
            TOKEN,
        ],
        input_output_aliases=aliases,
        compiler_params=params(),
        cost_estimate=cost(1),
        name="residuals",
    )(*args)


def update_kernel(n, *refs):
    features, residual = refs[:n], refs[n : 2 * n]
    cov, master, first, second = refs[2 * n : 2 * n + 4]
    new_master, new_first, new_second, sent = refs[-4:]
    rows = master.shape[1]
    gradient = None
    for j in range(n):
        term = jnp.dot(residual[j][...], features[j][...], preferred_element_type=f32)
        gradient = term if gradient is None else gradient + term
    gradient = gradient.T + master[0]
    conditioned = jnp.dot(gradient.astype(bf16), cov[...], preferred_element_type=f32)
    moved_first = beta_one * first[0] + (1.0 - beta_one) * conditioned
    moved_second = beta_two * second[0] + (1.0 - beta_two) * conditioned * conditioned
    correction_one = 1.0 - beta_one**STEP
    correction_two = 1.0 - beta_two**STEP
    moved = master[0] - learn_rate * (moved_first / correction_one) / (
        jnp.sqrt(moved_second / correction_two) + 1e-08
    )
    new_first[0] = moved_first
    new_second[0] = moved_second
    new_master[0] = moved
    sent[pl.ds(pl.multiple_of(pl.program_id(0) * rows, rows), rows), :] = moved.astype(bf16)


def update(features, residual, cov, master, first, second, chunk, chunks, before, deps):
    n = len(features)
    owned, k = master.shape[1:]
    rows = min(256, owned // chunks)
    steps = owned // chunks // rows
    at = chunk * steps
    batch = features[0].shape[0]
    state = pl.BlockSpec((1, rows, k), lambda i: (0, at + i, 0))
    args = [*features, *residual, cov, master, first, second]
    specs = (
        [pl.BlockSpec((batch, rows), lambda i: (0, at + i))] * n
        + [IN_VMEM] * n
        + [pl.BlockSpec(cov.shape, lambda i: (0, 0)), state, state, state]
    )
    aliases = {}
    if before is not None:
        aliases = {len(args) + j: j for j in range(3)}
        args += list(before)
        specs += [ANYWHERE] * 3
    args += deps
    specs += [IN_VMEM] * len(deps)
    return pl.pallas_call(
        functools.partial(update_kernel, n),
        grid=(steps,),
        in_specs=specs,
        out_specs=[state, state, state, IN_VMEM],
        out_shape=[jax.ShapeDtypeStruct(master.shape, f32)] * 3
        + [jax.ShapeDtypeStruct((owned // chunks, k), bf16)],
        input_output_aliases=aliases,
        compiler_params=params(),
        cost_estimate=cost(4),
        name="update",
    )(*args)


def put_kernel(n, n_pts, chunk, chunks, p, *refs):
    pieces, out, sems = refs[:n], refs[-2], refs[-1]
    me = p[0]
    copies = []
    for j in range(n):
        rows = pieces[j].shape[0]
        distance, other = j // CORES, j % CORES
        home = lax.rem(me + n_pts - distance * CORES, n_pts)
        home = home + other * (1 - 2 * lax.rem(home, 2))
        at = pl.ds(pl.multiple_of((home * chunks + chunk) * rows, rows), rows)
        copies.append(pltpu.make_async_copy(pieces[j], out.at[at, :], sems.at[j]))
    for copy in copies:
        copy.start()
    for copy in copies:
        copy.wait()


def put(p, working, pieces, chunk, chunks, n_pts, shape):
    n = len(pieces)
    args = [p, *pieces]
    specs = [IN_VMEM] * n
    aliases = {}
    if working is not None:
        aliases = {len(args): 0}
        args.append(working)
        specs.append(ANYWHERE)
    return pl.pallas_call(
        functools.partial(put_kernel, n, n_pts, chunk, chunks),
        grid_spec=pltpu.PrefetchScalarGridSpec(
            num_scalar_prefetch=1,
            grid=(1,),
            in_specs=specs,
            out_specs=ANYWHERE,
            scratch_shapes=[pltpu.SemaphoreType.DMA((n,))],
        ),
        out_shape=jax.ShapeDtypeStruct(shape, bf16),
        input_output_aliases=aliases,
        compiler_params=params(),
        cost_estimate=cost(1),
        name="put_rows",
    )(*args)


def ring(x, axis, n, distance):
    return lax.ppermute(x, axis, [(i, (i + distance) % n) for i in range(n)])


def mate(x, n):
    return lax.ppermute(x, "pts", [(i, i ^ 1) for i in range(n)])


def across(x, n, distance):
    return ring(x, "pts", n, distance * CORES)


def spread(x, n):
    chips = n // CORES
    got = [x if d == 0 else across(x, n, d) for d in range(chips)]
    return [y for g in got for y in (g, mate(g, n))]


def body(n_feat, n_pts, points, picks, omega, phase, weights, counts, master, first, second, cov):
    f = lax.axis_index("feat").astype(jnp.int32).reshape(1)
    p = lax.axis_index("pts").astype(jnp.int32).reshape(1)
    owned, k = master.shape[1:]
    phase = phase[None, :]

    terms, chosen, features = [], [], []
    deps = []
    for m in range(2):
        picked, feats, own, *others, token = rates(
            f, p, picks, points, omega, phase, weights, m, n_feat, owned, deps
        )
        deps = [token]
        features.append([feats])
        chosen.append(spread(picked, n_pts)[1:])
        terms.append([own] + [ring(others[d - 1], "feat", n_feat, d) for d in range(1, n_feat)])

    def whole(chunk):
        return [chunk] + [ring(chunk, "feat", n_feat, d) for d in range(1, n_feat)]

    pieces = [(m, j) for m in range(2) for j in range(n_pts - 1)]
    marks = [len(pieces) * i // 6 for i in range(6)]
    residual = []
    for i, (m, j) in enumerate(pieces):
        if i == marks[0]:
            chunk, token = total(terms[0], deps)
            rows_zero = whole(chunk)
            deps = [token]
        if i == marks[2]:
            chunk, first_token = total(terms[1], deps)
            rows_one = whole(chunk)
            out_rates, res, token = residuals(f, rows_zero, counts, 0, None, deps + [first_token])
            residual.append(spread(res, n_pts))
            deps = [token]
        if i == marks[4]:
            out_rates, res, token = residuals(f, rows_one, counts, 1, out_rates, deps)
            residual.append(spread(res, n_pts))
            deps = [token]
        feats, token = owned_features(p, chosen[m][j], omega, phase, owned, deps)
        deps = [token]
        features[m].append(feats)

    flat_features = features[0] + features[1]
    flat_residual = residual[0] + residual[1]
    state = None
    arrived = []
    chunks = max(1, min(4, owned // 256))
    for c in range(chunks):
        deps = [arrived[c - 2][CORES]] if c >= 2 and n_pts > CORES else []
        *state, sent = update(
            flat_features, flat_residual, cov, master, first, second, c, chunks, state, deps
        )
        arrived.append(spread(sent, n_pts))
    working = None
    for c in range(chunks):
        working = put(p, working, arrived[c], c, chunks, n_pts, (owned * n_pts, k))
    return out_rates, *state, working


def solution(mesh):
    placed = (
        P(("groups", "pts"), None),
        P(None, ("groups", "pts")),
        P(None, "feat"),
        P("feat"),
        P(("groups", "feat"), None),
        P(None, ("groups", "pts"), None),
        P(("groups", "feat"), "pts", None),
        P(("groups", "feat"), "pts", None),
        P(("groups", "feat"), "pts", None),
        P(),
    )
    return jax.shard_map(
        functools.partial(body, mesh.shape["feat"], mesh.shape["pts"]),
        mesh=mesh,
        in_specs=placed,
        out_specs=(
            P(None, ("groups", "pts"), None),
            P(("groups", "feat"), "pts", None),
            P(("groups", "feat"), "pts", None),
            P(("groups", "feat"), "pts", None),
            P(("groups", "feat"), None),
        ),
        check_vma=False,
    )
```

```python
import functools
import math

import jax
import jax.numpy as jnp
from jax import lax
from jax.experimental import pallas as pl
from jax.experimental.pallas import tpu as pltpu
from jax.sharding import PartitionSpec as P

F = 32768
STEP = 20
CORES = 2

beta_one = 0.9
beta_two = 0.999
learn_rate = 0.2

SINE = tuple(
    c / 8.0
    for c in (3.141582022078924, -5.167142793540227, 2.541899000696469, -0.5546361258792201)
)
ROUNDER = 12582912.0
TURN = 1.0 / (2.0 * math.pi)
VMEM = 30 * 1024 * 1024
WIDE = 58 * 1024 * 1024

f32 = jnp.float32
bf16 = jnp.bfloat16
IN_VMEM = pl.BlockSpec(memory_space=pltpu.VMEM)
ANYWHERE = pl.BlockSpec(memory_space=pl.ANY)


def scaled_cos(product, phase_turns):
    turns = product * TURN + phase_turns
    r = turns - ((turns + ROUNDER) - ROUNDER)
    s = r * r
    w = ((SINE[3] * s + SINE[2]) * s + SINE[1]) * s + SINE[0]
    w = w * r
    return (math.sqrt(2.0 / F) - w * w).astype(bf16)


TOKEN = jax.ShapeDtypeStruct((8, 128), f32)


def cost(microseconds):
    return pl.CostEstimate(
        flops=int(microseconds * 1.0e9), bytes_accessed=1 << 10, transcendentals=0
    )


def params(limit=None):
    return pltpu.CompilerParams(vmem_limit_bytes=limit or VMEM)


def gather_kernel(picks, points, chosen, token):
    batch, pool = chosen.shape[0], points.shape[0]
    m = pl.program_id(0)
    wanted = jnp.broadcast_to(picks[pl.ds(m, 1), :], (128, batch)).T
    lane = lax.broadcasted_iota(jnp.int32, (batch, 128), 1)
    hot = [jnp.where(wanted == lane + 128 * j, 1.0, 0.0).astype(bf16) for j in range(pool // 128)]
    chosen[...] = jnp.dot(
        jnp.concatenate(hot, axis=1), points[...], preferred_element_type=f32
    ).astype(bf16)


def gather(picks, points):
    batch = picks.shape[1]
    pool, ins = points.shape
    return pl.pallas_call(
        gather_kernel,
        grid=(2,),
        in_specs=[
            pl.BlockSpec(picks.shape, lambda i: (0, 0)),
            pl.BlockSpec((pool, ins), lambda i: (0, 0)),
        ],
        out_specs=[pl.BlockSpec((batch, ins), lambda i: (i, 0)), ANYWHERE],
        out_shape=[jax.ShapeDtypeStruct((2 * batch, ins), bf16), TOKEN],
        compiler_params=params(WIDE),
        cost_estimate=cost(3),
        name="chosen_points",
    )(picks, points)


def rates_kernel(owned_blocks, f, p, chosen, omega, phase, weights, *refs):
    owned, *outs, token, feats, total = refs
    step = pl.program_id(0)
    width = omega.shape[1]
    tile = min(256, width)
    pair = min(512, width)

    @pl.when(step == 0)
    def _():
        total[...] = jnp.zeros_like(total)

    turns = phase[...] * TURN
    part = None
    for c in range(width // tile):
        cols = slice(c * tile, (c + 1) * tile)
        product = jnp.dot(chosen[...], omega[:, cols], preferred_element_type=f32)
        feats[:, cols] = scaled_cos(product, turns[:, cols])
        if (c + 1) * tile % pair == 0:
            rows = slice((c + 1) * tile - pair, (c + 1) * tile)
            term = jnp.dot(feats[:, rows], weights[rows, :], preferred_element_type=f32)
            part = term if part is None else part + term
    total[...] += part

    @pl.when(step < owned_blocks)
    def _():
        owned[...] = feats[...]

    @pl.when(step == pl.num_programs(0) - 1)
    def _():
        if len(outs) == 1:
            outs[0][...] = total[...].astype(bf16)
        else:
            split(total, f[0], 0, *outs)


def split(value, f, bit, kept, sent):
    rows = kept.shape[0]
    side = lax.rem(f // 2**bit, 2)
    kept[...] = value[pl.ds(pl.multiple_of(side * rows, rows), rows), :]
    sent[...] = value[pl.ds(pl.multiple_of((1 - side) * rows, rows), rows), :].astype(bf16)


def rates(f, p, chosen, omega, phase, weights, m, owned, halves, deps):
    ins, feat_dev = omega.shape
    k = weights.shape[1]
    batch = chosen.shape[0] // 2
    width = min(1024, owned)
    grid = feat_dev // width
    blocks = owned // width

    def turned(i, p):
        return lax.rem(i + p[0] * blocks, grid)

    if halves:
        outs = [
            jax.ShapeDtypeStruct((batch // 2, k), f32),
            jax.ShapeDtypeStruct((batch // 2, k), bf16),
        ]
    else:
        outs = [jax.ShapeDtypeStruct((batch, k), bf16)]
    n_refs = len(outs) + 4

    def kernel(f, p, chosen, omega, phase, weights, *refs):
        rates_kernel(blocks, f, p, chosen, omega, phase, weights, *refs[-n_refs:])

    return pl.pallas_call(
        kernel,
        grid_spec=pltpu.PrefetchScalarGridSpec(
            num_scalar_prefetch=2,
            grid=(grid,),
            in_specs=[
                pl.BlockSpec((batch, ins), lambda i, f, p: (m, 0)),
                pl.BlockSpec((ins, width), lambda i, f, p: (0, turned(i, p))),
                pl.BlockSpec((1, width), lambda i, f, p: (0, turned(i, p))),
                pl.BlockSpec((width, k), lambda i, f, p: (turned(i, p), 0)),
            ]
            + [ANYWHERE] * len(deps),
            out_specs=[pl.BlockSpec((batch, width), lambda i, f, p: (0, jnp.minimum(i, blocks - 1)))]
            + [IN_VMEM] * len(outs)
            + [ANYWHERE],
            scratch_shapes=[pltpu.VMEM((batch, width), bf16), pltpu.VMEM((batch, k), f32)],
        ),
        out_shape=[jax.ShapeDtypeStruct((batch, owned), bf16), *outs, TOKEN],
        compiler_params=params(WIDE),
        cost_estimate=cost(12),
        name="partial_log_rates",
    )(f, p, chosen, omega, phase, weights, *deps)


def features_kernel(tile, p, chosen, omega, phase, *refs):
    out, token = refs[-2:]
    turns = phase[...] * TURN
    for c in range(omega.shape[1] // tile):
        cols = slice(c * tile, (c + 1) * tile)
        product = jnp.dot(chosen[0], omega[:, cols], preferred_element_type=f32)
        out[:, cols] = scaled_cos(product, turns[:, cols])


def owned_features(p, everyone, omega, phase, owned, m, j, deps):
    n, points, ins = everyone.shape
    points //= 2
    width = min(512, owned)
    blocks = owned // width
    return pl.pallas_call(
        functools.partial(features_kernel, min(256, width)),
        grid_spec=pltpu.PrefetchScalarGridSpec(
            num_scalar_prefetch=1,
            grid=(blocks,),
            in_specs=[
                pl.BlockSpec((1, points, ins), lambda i, p: (lax.rem(p[0] + j, n), m, 0)),
                pl.BlockSpec((ins, width), lambda i, p: (0, p[0] * blocks + i)),
                pl.BlockSpec((1, width), lambda i, p: (0, p[0] * blocks + i)),
            ]
            + [ANYWHERE] * len(deps),
            out_specs=[pl.BlockSpec((points, width), lambda i, p: (0, i)), ANYWHERE],
        ),
        out_shape=[jax.ShapeDtypeStruct((points, owned), bf16), TOKEN],
        compiler_params=params(),
        cost_estimate=cost(4),
        name="owned_features",
    )(p, everyone, omega, phase, *deps)


def total_kernel(bit, halves, f, a, b, *refs):
    value = a[...].astype(f32) + b[...].astype(f32)
    if halves:
        kept, sent, token, held = refs[-4:]
        held[...] = value
        split(held, f[0], bit, kept, sent)
    else:
        out, token = refs[-2:]
        out[...] = value.astype(bf16)


def total(f, a, b, bit, halves, deps):
    rows, k = a.shape
    if halves:
        outs = [
            jax.ShapeDtypeStruct((rows // 2, k), f32),
            jax.ShapeDtypeStruct((rows // 2, k), bf16),
        ]
    else:
        outs = [jax.ShapeDtypeStruct((rows, k), bf16)]
    return pl.pallas_call(
        functools.partial(total_kernel, bit, halves),
        grid_spec=pltpu.PrefetchScalarGridSpec(
            num_scalar_prefetch=1,
            grid=(1,),
            in_specs=[IN_VMEM] * 2 + [ANYWHERE] * len(deps),
            out_specs=[IN_VMEM] * len(outs) + [ANYWHERE],
            scratch_shapes=[pltpu.VMEM((rows, k), f32)] if halves else [],
        ),
        out_shape=[*outs, TOKEN],
        compiler_params=params(),
        cost_estimate=cost(0.5),
        name="total_rates",
    )(f, a, b, *deps)


def residual_kernel(masks, m, f, *refs):
    chunks, observed = refs[: len(masks)], refs[len(masks)]
    rate_out, residual_out, token, held = refs[-4:]
    batch = held.shape[0]
    for j, mask in enumerate(masks):
        rows = chunks[j].shape[0]
        start, bit = 0, 0
        while batch >> (bit + 1) >= rows:
            side = lax.rem(f[0] // 2**bit, 2)
            side = 1 - side if mask >> bit & 1 else side
            start = start + side * (batch >> (bit + 1))
            bit += 1
        at = pl.ds(pl.multiple_of(start, rows), rows) if bit else slice(None)
        rate = chunks[j][...].astype(f32)
        rate_out[0, at, :] = rate
        held[at, :] = jnp.exp(rate) - observed[0, at, :].astype(f32)
    residual_out[...] = held[...].T.astype(bf16)


def residuals(f, chunks, masks, counts, m, before, deps):
    n = len(chunks)
    k = chunks[0].shape[1]
    batch = counts.shape[1]
    args = [f, *chunks, counts, *deps]
    specs = [IN_VMEM] * n + [pl.BlockSpec((1, batch, k), lambda i, _: (m, 0, 0))]
    specs += [ANYWHERE] * len(deps)
    aliases = {}
    if before is not None:
        aliases = {len(args): 0}
        args.append(before)
        specs.append(ANYWHERE)
    return pl.pallas_call(
        functools.partial(residual_kernel, masks, m),
        grid_spec=pltpu.PrefetchScalarGridSpec(
            num_scalar_prefetch=1,
            grid=(1,),
            in_specs=specs,
            out_specs=[pl.BlockSpec((1, batch, k), lambda i, _: (m, 0, 0)), IN_VMEM, ANYWHERE],
            scratch_shapes=[pltpu.VMEM((batch, k), f32)],
        ),
        out_shape=[
            jax.ShapeDtypeStruct(counts.shape, f32),
            jax.ShapeDtypeStruct((k, batch), bf16),
            TOKEN,
        ],
        input_output_aliases=aliases,
        compiler_params=params(),
        cost_estimate=cost(1),
        name="residuals",
    )(*args)


def gradient_part(n, p, features, residual):
    value = None
    for j in range(n):
        term = jnp.dot(
            residual[lax.rem(p[0] + j, n)], features[j][...], preferred_element_type=f32
        )
        value = term if value is None else value + term
    return value


def first_part_kernel(n, p, *refs):
    features, residual, master = refs[:n], refs[n], refs[n + 1]
    out, token = refs[-2:]
    out[...] = gradient_part(n, p, features, residual).T + master[0]


def first_part(p, features, residual, master, deps):
    n = len(features)
    owned, k = master.shape[1:]
    rows = min(512, owned)
    batch = features[0].shape[0]
    return pl.pallas_call(
        functools.partial(first_part_kernel, n),
        grid_spec=pltpu.PrefetchScalarGridSpec(
            num_scalar_prefetch=1,
            grid=(owned // rows,),
            in_specs=[pl.BlockSpec((batch, rows), lambda i, p: (0, i))] * n
            + [IN_VMEM, pl.BlockSpec((1, rows, k), lambda i, p: (0, i, 0))]
            + [ANYWHERE] * len(deps),
            out_specs=[pl.BlockSpec((rows, k), lambda i, p: (i, 0)), ANYWHERE],
        ),
        out_shape=[jax.ShapeDtypeStruct((owned, k), f32), TOKEN],
        compiler_params=params(),
        cost_estimate=cost(5),
        name="first_part",
    )(p, *features, residual, master, *deps)


def update_kernel(n, p, *refs):
    features, residual = refs[:n], refs[n]
    begun, cov, master, first, second = refs[n + 1 : n + 6]
    new_master, new_first, new_second, kept, sent = refs[-5:]
    rows = master.shape[1]
    gradient = gradient_part(n, p, features, residual).T + begun[...]
    conditioned = jnp.dot(gradient.astype(bf16), cov[...], preferred_element_type=f32)
    moved_first = beta_one * first[0] + (1.0 - beta_one) * conditioned
    moved_second = beta_two * second[0] + (1.0 - beta_two) * conditioned * conditioned
    correction_one = 1.0 - beta_one**STEP
    correction_two = 1.0 - beta_two**STEP
    moved = master[0] - learn_rate * (moved_first / correction_one) / (
        jnp.sqrt(moved_second / correction_two) + 1e-08
    )
    new_first[0] = moved_first
    new_second[0] = moved_second
    new_master[0] = moved
    rounded = moved.astype(bf16)
    kept[...] = rounded
    sent[pl.ds(pl.multiple_of(pl.program_id(0) * rows, rows), rows), :] = rounded


def update(p, features, residual, begun, cov, master, first, second, at, steps, before, deps):
    n = len(features)
    owned, k = master.shape[1:]
    rows = min(256, owned)
    batch = features[0].shape[0]
    state = pl.BlockSpec((1, rows, k), lambda i, p: (0, at + i, 0))
    flat = pl.BlockSpec((rows, k), lambda i, p: (at + i, 0))
    args = [p, *features, residual, begun, cov, master, first, second]
    specs = (
        [pl.BlockSpec((batch, rows), lambda i, p: (0, at + i))] * n
        + [IN_VMEM, flat]
        + [pl.BlockSpec(cov.shape, lambda i, p: (0, 0)), state, state, state]
    )
    aliases = {}
    if before is not None:
        aliases = {len(args) + j: j for j in range(4)}
        args += list(before)
        specs += [ANYWHERE] * 4
    args += deps
    specs += [ANYWHERE] * len(deps)
    return pl.pallas_call(
        functools.partial(update_kernel, n),
        grid_spec=pltpu.PrefetchScalarGridSpec(
            num_scalar_prefetch=1,
            grid=(steps,),
            in_specs=specs,
            out_specs=[state, state, state, flat, IN_VMEM],
        ),
        out_shape=[jax.ShapeDtypeStruct(master.shape, f32)] * 3
        + [
            jax.ShapeDtypeStruct((owned, k), bf16),
            jax.ShapeDtypeStruct((steps * rows, k), bf16),
        ],
        input_output_aliases=aliases,
        compiler_params=params(),
        cost_estimate=cost(4),
        name="update",
    )(*args)


def put_kernel(blocks, owned, n_pts, p, *refs):
    n = len(blocks)
    pieces, out, sems = refs[:n], refs[-2], refs[-1]
    me = p[0]
    copies = []
    for j, (distance, other, start) in enumerate(blocks):
        rows = pieces[j].shape[0]
        home = lax.rem(me + n_pts - distance * CORES, n_pts)
        home = home + other * (1 - 2 * lax.rem(home, 2))
        at = pl.ds(pl.multiple_of(home * owned + start, rows), rows)
        copies.append(pltpu.make_async_copy(pieces[j], out.at[at, :], sems.at[j]))
    for copy in copies:
        copy.start()
    for copy in copies:
        copy.wait()


def put(p, pieces, blocks, owned, n_pts):
    n = len(pieces)
    k = pieces[0].shape[1]
    return pl.pallas_call(
        functools.partial(put_kernel, blocks, owned, n_pts),
        grid_spec=pltpu.PrefetchScalarGridSpec(
            num_scalar_prefetch=1,
            grid=(1,),
            in_specs=[IN_VMEM] * n,
            out_specs=ANYWHERE,
            scratch_shapes=[pltpu.SemaphoreType.DMA((n,))],
        ),
        out_shape=jax.ShapeDtypeStruct((owned * n_pts, k), bf16),
        compiler_params=params(),
        cost_estimate=cost(2),
        name="put_rows",
    )(p, *pieces)


def ring(x, axis, n, distance):
    return lax.ppermute(x, axis, [(i, (i + distance) % n) for i in range(n)])


def mate(x, n):
    return lax.ppermute(x, "pts", [(i, i ^ 1) for i in range(n)])


def across(x, n, distance):
    return ring(x, "pts", n, distance * CORES)


def swap(x, n, bit):
    return lax.ppermute(x, "feat", [(i, i ^ 2**bit) for i in range(n)])


def body(n_feat, n_pts, points, picks, omega, phase, weights, counts, master, first, second, cov):
    f = lax.axis_index("feat").astype(jnp.int32).reshape(1)
    p = lax.axis_index("pts").astype(jnp.int32).reshape(1)
    owned, k = master.shape[1:]
    phase = phase[None, :]
    bits = n_feat.bit_length() - 1

    chosen, token = gather(picks, points)
    everyone = lax.all_gather(chosen, "pts")
    feats_zero, part, token = rates(
        f, p, chosen, omega, phase, weights, 0, owned, False, [token]
    )
    rate_zero = lax.psum(part, "feat")
    feats_one, kept, sent, token = rates(
        f, p, chosen, omega, phase, weights, 1, owned, True, [token]
    )
    features = [[feats_zero], [feats_one]]

    todo = [(m, j) for m in range(2) for j in range(1, n_pts)]
    share = len(todo) // 6

    def some(token, pieces):
        for _ in range(pieces * share):
            m, j = todo.pop(0)
            feats, token = owned_features(p, everyone, omega, phase, owned, m, j, [token])
            features[m].append(feats)
        return token

    got = swap(sent, n_feat, 0)
    token = some(token, 1)
    for bit in range(1, bits):
        *out, token = total(f, kept, got, bit, bit < bits - 1, [token])
        if bit < bits - 1:
            kept, sent = out
        else:
            kept = sent = out[0]
        got = swap(sent, n_feat, bit)
        if bit == 1:
            out_rates, res_zero, token = residuals(f, [rate_zero], [0], counts, 0, None, [token])
            res_zero = lax.all_gather(res_zero, "pts")
            token = some(token, 2)
    chunk, token = total(f, kept, got, 0, False, [token])
    rows, masks = [chunk], [0]
    for bit in reversed(range(bits - 1)):
        rows = rows + [swap(r, n_feat, bit) for r in rows]
        masks = masks + [q ^ 2**bit for q in masks]
    token = some(token, 1)
    out_rates, res_one, token = residuals(f, rows, masks, counts, 1, out_rates, [token])
    res_one = lax.all_gather(res_one, "pts")
    token = some(token, 2)
    begun, token = first_part(p, features[0], res_zero, master, [token])

    steps = max(1, owned // 256)
    sizes = [2, 3, 2, 1] if steps == 8 else [1] * steps
    chips = n_pts // CORES
    state = None
    pieces, blocks = [], []
    at = 0
    early = []
    for c, size in enumerate(sizes):
        deps = early if c == 2 else []
        *state, sent = update(
            p, features[1], res_one, begun, cov, master, first, second, at, size, state, deps
        )
        come = [across(sent, n_pts, d) for d in range(1, chips)]
        early = early or come[:1]
        pieces += come + [mate(x, n_pts) for x in come]
        start = at * (owned // steps)
        blocks += [(d, other, start) for other in (0, 1) for d in range(1, chips)]
        at += size
    *state, kept = state
    pieces += [kept, mate(kept, n_pts)]
    blocks += [(0, 0, 0), (0, 1, 0)]
    working = put(p, pieces, blocks, owned, n_pts)
    return out_rates, *state, working


def solution(mesh):
    placed = (
        P(("groups", "pts"), None),
        P(None, ("groups", "pts")),
        P(None, "feat"),
        P("feat"),
        P(("groups", "feat"), None),
        P(None, ("groups", "pts"), None),
        P(("groups", "feat"), "pts", None),
        P(("groups", "feat"), "pts", None),
        P(("groups", "feat"), "pts", None),
        P(),
    )
    return jax.shard_map(
        functools.partial(body, mesh.shape["feat"], mesh.shape["pts"]),
        mesh=mesh,
        in_specs=placed,
        out_specs=(
            P(None, ("groups", "pts"), None),
            P(("groups", "feat"), "pts", None),
            P(("groups", "feat"), "pts", None),
            P(("groups", "feat"), "pts", None),
            P(("groups", "feat"), None),
        ),
        check_vma=False,
    )
```

```python
import functools
import math

import jax
import jax.numpy as jnp
from jax import lax
from jax.experimental import pallas as pl
from jax.experimental.pallas import tpu as pltpu
from jax.sharding import PartitionSpec as P

F = 32768
STEP = 20
CORES = 2

beta_one = 0.9
beta_two = 0.999
learn_rate = 0.2

SINE = tuple(
    c / 8.0
    for c in (3.141582022078924, -5.167142793540227, 2.541899000696469, -0.5546361258792201)
)
ROUNDER = 12582912.0
TURN = 1.0 / (2.0 * math.pi)
VMEM = 24 * 1024 * 1024

f32 = jnp.float32
bf16 = jnp.bfloat16
IN_VMEM = pl.BlockSpec(memory_space=pltpu.VMEM)
ANYWHERE = pl.BlockSpec(memory_space=pl.ANY)


def scaled_cos(product, phase_turns):
    turns = product * TURN + phase_turns
    r = turns - ((turns + ROUNDER) - ROUNDER)
    s = r * r
    w = ((SINE[3] * s + SINE[2]) * s + SINE[1]) * s + SINE[0]
    w = w * r
    return (math.sqrt(2.0 / F) - w * w).astype(bf16)


TOKEN = jax.ShapeDtypeStruct((8, 128), f32)


def cost(microseconds):
    return pl.CostEstimate(
        flops=int(microseconds * 1.0e9), bytes_accessed=1 << 10, transcendentals=0
    )


def params():
    return pltpu.CompilerParams(vmem_limit_bytes=VMEM)


def in_hbm(x):
    return pltpu.with_memory_space_constraint(x, pltpu.HBM)


def gather_kernel(picks, points, chosen, token):
    batch, pool = chosen.shape[0], points.shape[0]
    m = pl.program_id(0)
    wanted = jnp.broadcast_to(picks[pl.ds(m, 1), :], (128, batch)).T
    lane = lax.broadcasted_iota(jnp.int32, (batch, 128), 1)
    hot = [jnp.where(wanted == lane + 128 * j, 1.0, 0.0).astype(bf16) for j in range(pool // 128)]
    chosen[...] = jnp.dot(
        jnp.concatenate(hot, axis=1), points[...], preferred_element_type=f32
    ).astype(bf16)


def gather(picks, points):
    batch = picks.shape[1]
    pool, ins = points.shape
    return pl.pallas_call(
        gather_kernel,
        grid=(2,),
        in_specs=[
            pl.BlockSpec(picks.shape, lambda i: (0, 0)),
            pl.BlockSpec((pool, ins), lambda i: (0, 0)),
        ],
        out_specs=[pl.BlockSpec((batch, ins), lambda i: (i, 0)), ANYWHERE],
        out_shape=[jax.ShapeDtypeStruct((2 * batch, ins), bf16), TOKEN],
        compiler_params=params(),
        cost_estimate=cost(3),
        name="chosen_points",
    )(picks, points)


def cosines(chosen, omega, turns, width, store, between=None):
    tile = min(256, width)
    count = width // tile

    def product(c):
        return jnp.dot(chosen, omega[:, c * tile : (c + 1) * tile], preferred_element_type=f32)

    ready = product(0)
    for c in range(count):
        coming = product(c + 1) if c + 1 < count else None
        if between is not None and c > 0:
            between(slice((c - 1) * tile, c * tile))
        cols = slice(c * tile, (c + 1) * tile)
        store(cols, scaled_cos(ready, turns[:, cols]))
        ready = coming
    if between is not None:
        between(slice((count - 1) * tile, count * tile))


def rates_kernel(start, size, begun, keep, ends, blocks, f, p, chosen, omega, phase, weights, *refs):
    refs = list(refs)
    total, feats = refs.pop(), refs.pop()
    before = refs.pop(0) if begun else None
    refs.pop()
    step = pl.program_id(0)
    width = omega.shape[1]

    @pl.when(step == 0)
    def _():
        total[...] = before[...] if begun else jnp.zeros_like(total)

    turns = phase[...] * TURN
    parts = []

    def store(cols, value):
        feats[:, cols] = value

    def between(cols):
        parts.append(jnp.dot(feats[:, cols], weights[cols, :], preferred_element_type=f32))

    cosines(chosen[start : start + size, :], omega, turns, width, store, between)
    part = parts[0]
    for q in parts[1:]:
        part = part + q
    total[...] += part

    if not begun:
        owned = refs.pop(0)

        @pl.when(step < blocks)
        def _():
            at = pl.ds(pl.multiple_of(step * width, width), width)
            owned[:, at] = feats[...]
            if keep:
                refs[0][:, at] = omega[...]
                refs[1][:, at] = turns

    @pl.when(step == pl.num_programs(0) - 1)
    def _():
        if ends:
            split(total, f[0], 0, *refs[-2:])
        else:
            refs[-1][...] = total[...]


def split(value, f, bit, kept, sent):
    rows = kept.shape[0]
    side = lax.rem(f // 2**bit, 2)
    kept[...] = value[pl.ds(pl.multiple_of(side * rows, rows), rows), :]
    sent[...] = value[pl.ds(pl.multiple_of((1 - side) * rows, rows), rows), :].astype(bf16)


def rates(f, p, chosen, omega, phase, weights, start, size, owned, blocks, before, keep, ends, deps):
    ins, feat_dev = omega.shape
    k = weights.shape[1]
    width = min(1024, owned)
    count = feat_dev // width
    own = owned // width
    low, high = blocks[0] * count // 2, blocks[1] * count // 2

    def turned(i, p):
        return lax.rem(i + low + p[0] * own, count)

    begun = before is not None
    outs = []
    if not begun:
        outs.append(jax.ShapeDtypeStruct((size, owned), bf16))
    if keep:
        outs += [jax.ShapeDtypeStruct((ins, owned), bf16), jax.ShapeDtypeStruct((1, owned), f32)]
    if ends:
        outs += [jax.ShapeDtypeStruct((size // 2, k), t) for t in (f32, bf16)]
    else:
        outs.append(jax.ShapeDtypeStruct((size, k), f32))
    args = [f, p, chosen, omega, phase, weights] + ([before] if begun else []) + deps

    def kernel(*refs):
        inputs = len(args) - len(deps)
        rates_kernel(
            start, size, begun, keep, ends, own, *refs[:inputs], *refs[inputs + len(deps) :]
        )

    return pl.pallas_call(
        kernel,
        grid_spec=pltpu.PrefetchScalarGridSpec(
            num_scalar_prefetch=2,
            grid=(high - low,),
            in_specs=[
                IN_VMEM,
                pl.BlockSpec((ins, width), lambda i, f, p: (0, turned(i, p))),
                pl.BlockSpec((1, width), lambda i, f, p: (0, turned(i, p))),
                pl.BlockSpec((width, k), lambda i, f, p: (turned(i, p), 0)),
            ]
            + [IN_VMEM] * begun
            + [ANYWHERE] * len(deps),
            out_specs=[IN_VMEM] * len(outs) + [ANYWHERE],
            scratch_shapes=[pltpu.VMEM((size, width), bf16), pltpu.VMEM((size, k), f32)],
        ),
        out_shape=[*outs, TOKEN],
        compiler_params=params(),
        cost_estimate=cost(12 * (high - low) / count),
        name="partial_log_rates",
    )(*args)


def features_kernel(start, size, chosen, omega, turns, *refs):
    out = refs[-2]

    def store(cols, value):
        out[:, cols] = value

    cosines(chosen[start : start + size, :], omega, turns, omega.shape[1], store)


def owned_features(chosen, omega, turns, start, size, deps):
    owned = omega.shape[1]
    return pl.pallas_call(
        functools.partial(features_kernel, start, size),
        in_specs=[IN_VMEM] * 3 + [ANYWHERE] * len(deps),
        out_specs=[IN_VMEM, ANYWHERE],
        out_shape=[jax.ShapeDtypeStruct((size, owned), bf16), TOKEN],
        compiler_params=params(),
        cost_estimate=cost(1),
        name="owned_features",
    )(chosen, omega, turns, *deps)


def total_kernel(bit, halves, f, a, b, *refs):
    value = a[...].astype(f32) + b[...].astype(f32)
    if halves:
        kept, sent, token, held = refs[-4:]
        held[...] = value
        split(held, f[0], bit, kept, sent)
    else:
        out, token = refs[-2:]
        out[...] = value.astype(bf16)


def total(f, a, b, bit, halves, deps):
    rows, k = a.shape
    if halves:
        outs = [
            jax.ShapeDtypeStruct((rows // 2, k), f32),
            jax.ShapeDtypeStruct((rows // 2, k), bf16),
        ]
    else:
        outs = [jax.ShapeDtypeStruct((rows, k), bf16)]
    return pl.pallas_call(
        functools.partial(total_kernel, bit, halves),
        grid_spec=pltpu.PrefetchScalarGridSpec(
            num_scalar_prefetch=1,
            grid=(1,),
            in_specs=[IN_VMEM] * 2 + [ANYWHERE] * len(deps),
            out_specs=[IN_VMEM] * len(outs) + [ANYWHERE],
            scratch_shapes=[pltpu.VMEM((rows, k), f32)] if halves else [],
        ),
        out_shape=[*outs, TOKEN],
        compiler_params=params(),
        cost_estimate=cost(0.5),
        name="total_rates",
    )(f, a, b, *deps)


def residual_kernel(masks, m, f, *refs):
    chunks, observed = refs[: len(masks)], refs[len(masks)]
    rate_out, residual_out, token, held = refs[-4:]
    batch = held.shape[0]
    for j, mask in enumerate(masks):
        rows = chunks[j].shape[0]
        start, bit = 0, 0
        while batch >> (bit + 1) >= rows:
            side = lax.rem(f[0] // 2**bit, 2)
            side = 1 - side if mask >> bit & 1 else side
            start = start + side * (batch >> (bit + 1))
            bit += 1
        at = pl.ds(pl.multiple_of(start, rows), rows) if bit else slice(None)
        rate = chunks[j][...].astype(f32)
        rate_out[0, at, :] = rate
        held[at, :] = jnp.exp(rate) - observed[0, at, :].astype(f32)
    residual_out[...] = held[...].T.astype(bf16)


def residuals(f, chunks, masks, counts, m, before, deps):
    n = len(chunks)
    k = chunks[0].shape[1]
    batch = counts.shape[1]
    args = [f, *chunks, counts, *deps]
    specs = [IN_VMEM] * n + [pl.BlockSpec((1, batch, k), lambda i, _: (m, 0, 0))]
    specs += [ANYWHERE] * len(deps)
    aliases = {}
    if before is not None:
        aliases = {len(args): 0}
        args.append(before)
        specs.append(ANYWHERE)
    return pl.pallas_call(
        functools.partial(residual_kernel, masks, m),
        grid_spec=pltpu.PrefetchScalarGridSpec(
            num_scalar_prefetch=1,
            grid=(1,),
            in_specs=specs,
            out_specs=[pl.BlockSpec((1, batch, k), lambda i, _: (m, 0, 0)), IN_VMEM, ANYWHERE],
            scratch_shapes=[pltpu.VMEM((batch, k), f32)],
        ),
        out_shape=[
            jax.ShapeDtypeStruct(counts.shape, f32),
            jax.ShapeDtypeStruct((k, batch), bf16),
            TOKEN,
        ],
        input_output_aliases=aliases,
        compiler_params=params(),
        cost_estimate=cost(1),
        name="residuals",
    )(*args)


def gradient_part(n, features, residual, start, rows):
    at = pl.ds(pl.multiple_of(start, rows), rows)
    value = None
    for j in range(n):
        term = jnp.dot(residual[j][...], features[j][:, at], preferred_element_type=f32)
        value = term if value is None else value + term
    return value


def first_part_kernel(n, *refs):
    features, residual, master = refs[:n], refs[n : 2 * n], refs[2 * n]
    out = refs[-2]
    rows = out.shape[0]
    out[...] = gradient_part(n, features, residual, pl.program_id(0) * rows, rows).T + master[0]


def first_part(features, residual, master, deps):
    n = len(features)
    owned, k = master.shape[1:]
    rows = min(512, owned)
    return pl.pallas_call(
        functools.partial(first_part_kernel, n),
        grid=(owned // rows,),
        in_specs=[IN_VMEM] * (2 * n)
        + [pl.BlockSpec((1, rows, k), lambda i: (0, i, 0))]
        + [ANYWHERE] * len(deps),
        out_specs=[pl.BlockSpec((rows, k), lambda i: (i, 0)), ANYWHERE],
        out_shape=[jax.ShapeDtypeStruct((owned, k), f32), TOKEN],
        compiler_params=params(),
        cost_estimate=cost(5),
        name="first_part",
    )(*features, *residual, master, *deps)


def update_kernel(n, begin, *refs):
    features, residual = refs[:n], refs[n : 2 * n]
    begun, cov, master, first, second = refs[2 * n : 2 * n + 5]
    new_master, new_first, new_second, sent = refs[-4:]
    rows = master.shape[1]
    step = pl.program_id(0)
    gradient = gradient_part(n, features, residual, (begin + step) * rows, rows).T + begun[...]
    conditioned = jnp.dot(gradient.astype(bf16), cov[...], preferred_element_type=f32)
    moved_first = beta_one * first[0] + (1.0 - beta_one) * conditioned
    moved_second = beta_two * second[0] + (1.0 - beta_two) * conditioned * conditioned
    correction_one = 1.0 - beta_one**STEP
    correction_two = 1.0 - beta_two**STEP
    moved = master[0] - learn_rate * (moved_first / correction_one) / (
        jnp.sqrt(moved_second / correction_two) + 1e-08
    )
    new_first[0] = moved_first
    new_second[0] = moved_second
    new_master[0] = moved
    sent[pl.ds(pl.multiple_of(step * rows, rows), rows), :] = moved.astype(bf16)


def update(features, residual, begun, cov, master, first, second, at, steps, before, deps):
    n = len(features)
    owned, k = master.shape[1:]
    rows = min(256, owned)
    state = pl.BlockSpec((1, rows, k), lambda i: (0, at + i, 0))
    flat = pl.BlockSpec((rows, k), lambda i: (at + i, 0))
    args = [*features, *residual, begun, cov, master, first, second]
    specs = [IN_VMEM] * (2 * n) + [flat, pl.BlockSpec(cov.shape, lambda i: (0, 0))] + [state] * 3
    aliases = {}
    if before is not None:
        aliases = {len(args) + j: j for j in range(3)}
        args += list(before)
        specs += [ANYWHERE] * 3
    args += deps
    specs += [ANYWHERE] * len(deps)
    return pl.pallas_call(
        functools.partial(update_kernel, n, at),
        grid=(steps,),
        in_specs=specs,
        out_specs=[state, state, state, IN_VMEM],
        out_shape=[jax.ShapeDtypeStruct(master.shape, f32)] * 3
        + [jax.ShapeDtypeStruct((steps * rows, k), bf16)],
        input_output_aliases=aliases,
        compiler_params=params(),
        cost_estimate=cost(1),
        name="update",
    )(*args)


def put_kernel(blocks, owned, n_pts, p, *refs):
    n = len(blocks)
    pieces, out, sems = refs[:n], refs[-2], refs[-1]
    me = p[0]
    copies = []
    for j, (distance, other, start) in enumerate(blocks):
        rows = pieces[j].shape[0]
        home = lax.rem(me + n_pts - distance * CORES, n_pts)
        home = home + other * (1 - 2 * lax.rem(home, 2))
        at = pl.ds(pl.multiple_of(home * owned + start, rows), rows)
        copies.append(pltpu.make_async_copy(pieces[j], out.at[at, :], sems.at[j]))
    for copy in copies:
        copy.start()
    for copy in copies:
        copy.wait()


def put(p, pieces, blocks, owned, n_pts):
    n = len(pieces)
    k = pieces[0].shape[1]
    return pl.pallas_call(
        functools.partial(put_kernel, blocks, owned, n_pts),
        grid_spec=pltpu.PrefetchScalarGridSpec(
            num_scalar_prefetch=1,
            grid=(1,),
            in_specs=[IN_VMEM] * n,
            out_specs=ANYWHERE,
            scratch_shapes=[pltpu.SemaphoreType.DMA((n,))],
        ),
        out_shape=jax.ShapeDtypeStruct((owned * n_pts, k), bf16),
        compiler_params=params(),
        cost_estimate=cost(2),
        name="put_rows",
    )(p, *pieces)


def ring(x, axis, n, distance):
    return lax.ppermute(x, axis, [(i, (i + distance) % n) for i in range(n)])


def mate(x, n):
    return lax.ppermute(x, "pts", [(i, i ^ 1) for i in range(n)])


def across(x, n, distance):
    return ring(x, "pts", n, distance * CORES)


def swap(x, n, bit):
    return lax.ppermute(x, "feat", [(i, i ^ 2**bit) for i in range(n)])


def spread(x, n):
    got = [x if d == 0 else across(x, n, d) for d in range(n // CORES)]
    return [y for g in got for y in (g, mate(g, n))]


def body(n_feat, n_pts, points, picks, omega, phase, weights, counts, master, first, second, cov):
    f = lax.axis_index("feat").astype(jnp.int32).reshape(1)
    p = lax.axis_index("pts").astype(jnp.int32).reshape(1)
    owned, k = master.shape[1:]
    batch = picks.shape[1]
    bits = n_feat.bit_length() - 1
    points, picks, omega, weights = map(in_hbm, (points, picks, omega, weights))
    phase, counts, cov = map(in_hbm, (phase[None, :], counts, cov))
    master, first, second = map(in_hbm, (master, first, second))

    chosen, token = gather(picks, points)
    everyone = spread(chosen, n_pts)

    def some_rates(m, blocks, before, keep, ends, token):
        return rates(
            f, p, chosen, omega, phase, weights, m * batch, batch, owned, blocks, before, keep, ends, [token]
        )

    def add_up(kept, got, bit, token):
        last = bit == bits - 1
        *out, token = total(f, kept, got, bit, not last, [token])
        kept, sent = (out[0], out[0]) if last else out
        return kept, swap(sent, n_feat, bit), token

    def give_back(chunk):
        rows, masks = [chunk], [0]
        for bit in reversed(range(bits - 1)):
            rows = rows + [swap(r, n_feat, bit) for r in rows]
            masks = masks + [q ^ 2**bit for q in masks]
        return rows, masks

    feats_zero, own_omega, own_turns, kept_zero, sent, token = some_rates(
        0, (0, 2), None, True, True, token
    )
    got_zero = swap(sent, n_feat, 0)
    feats_one, begun, token = some_rates(1, (0, 1), None, False, False, token)
    for bit in range(1, bits):
        kept_zero, got_zero, token = add_up(kept_zero, got_zero, bit, token)
    kept_one, sent, token = some_rates(1, (1, 2), begun, False, True, token)
    got_one = swap(sent, n_feat, 0)
    features = [[feats_zero], [feats_one]]

    todo = [(m, j) for m in range(2) for j in range(1, n_pts)]
    share = len(todo) // 6

    def some(token, pieces):
        for _ in range(pieces * share):
            m, j = todo.pop(0)
            feats, token = owned_features(
                everyone[j], own_omega, own_turns, m * batch, batch, [token]
            )
            features[m].append(feats)
        return token

    chunk, token = total(f, kept_zero, got_zero, 0, False, [token])
    rows_zero, masks = give_back(chunk)
    token = some(token, 1)
    for bit in range(1, bits):
        kept_one, got_one, token = add_up(kept_one, got_one, bit, token)
    token = some(token, 1)
    out_rates, res, token = residuals(f, rows_zero, masks, counts, 0, None, [token])
    res_zero = spread(res, n_pts)
    token = some(token, 1)
    chunk, token = total(f, kept_one, got_one, 0, False, [token])
    rows_one, masks = give_back(chunk)
    token = some(token, 1)
    out_rates, res, token = residuals(f, rows_one, masks, counts, 1, out_rates, [token])
    res_one = spread(res, n_pts)
    token = some(token, 2)
    begun, token = first_part(features[0], res_zero, master, [token])

    steps = max(1, owned // 256)
    sizes = [2, 3, 2, 1] if steps == 8 else [1] * steps
    chips = n_pts // CORES
    state = None
    pieces, blocks = [], []
    at = 0
    early = []
    for c, size in enumerate(sizes):
        *state, sent = update(
            features[1], res_one, begun, cov, master, first, second, at, size, state, [token]
        )
        come = [sent]
        if chips > 1:
            if c >= 2:
                sent, _ = lax.optimization_barrier((sent, early[c - 2]))
            come += [across(sent, n_pts, d) for d in range(1, chips)]
            early.append(come[1])
        pieces += come + [mate(x, n_pts) for x in come]
        start = at * (owned // steps)
        blocks += [(d, other, start) for other in (0, 1) for d in range(chips)]
        at += size
    working = put(p, pieces, blocks, owned, n_pts)
    return out_rates, *state, working


def solution(mesh):
    placed = (
        P(("groups", "pts"), None),
        P(None, ("groups", "pts")),
        P(None, "feat"),
        P("feat"),
        P(("groups", "feat"), None),
        P(None, ("groups", "pts"), None),
        P(("groups", "feat"), "pts", None),
        P(("groups", "feat"), "pts", None),
        P(("groups", "feat"), "pts", None),
        P(),
    )
    return jax.shard_map(
        functools.partial(body, mesh.shape["feat"], mesh.shape["pts"]),
        mesh=mesh,
        in_specs=placed,
        out_specs=(
            P(None, ("groups", "pts"), None),
            P(("groups", "feat"), "pts", None),
            P(("groups", "feat"), "pts", None),
            P(("groups", "feat"), "pts", None),
            P(("groups", "feat"), None),
        ),
        check_vma=False,
    )
```

```python
import functools
import math

import jax
import jax.numpy as jnp
from jax import lax
from jax.experimental import pallas as pl
from jax.experimental.pallas import tpu as pltpu
from jax.sharding import PartitionSpec as P

F = 32768
STEP = 20
CORES = 2

beta_one = 0.9
beta_two = 0.999
learn_rate = 0.2

SINE = tuple(
    c * math.sqrt(2.0 / F) for c in (6.2825055774072665, -41.16644056159234, 74.4523919857074)
)
ROUNDER = 12582912.0
TURN = 1.0 / (2.0 * math.pi)
VMEM = 24 * 1024 * 1024

f32 = jnp.float32
bf16 = jnp.bfloat16
IN_VMEM = pl.BlockSpec(memory_space=pltpu.VMEM)
ANYWHERE = pl.BlockSpec(memory_space=pl.ANY)
TOKEN = jax.ShapeDtypeStruct((8, 128), f32)


def scaled_cos(product, phase_turns):
    turns = product * TURN + phase_turns
    v = 0.25 - jnp.abs(turns - ((turns + ROUNDER) - ROUNDER))
    s = v * v
    return (((SINE[2] * s + SINE[1]) * s + SINE[0]) * v).astype(bf16)


def cost(microseconds):
    return pl.CostEstimate(
        flops=int(microseconds * 1.0e9), bytes_accessed=1 << 10, transcendentals=0
    )


def params():
    return pltpu.CompilerParams(vmem_limit_bytes=VMEM)


def in_hbm(x):
    return pltpu.with_memory_space_constraint(x, pltpu.HBM)


def gather_kernel(picks, points, chosen, token):
    batch, pool = chosen.shape[0], points.shape[0]
    m = pl.program_id(0)
    wanted = jnp.broadcast_to(picks[pl.ds(m, 1), :], (128, batch)).T
    lane = lax.broadcasted_iota(jnp.int32, (batch, 128), 1)
    hot = [jnp.where(wanted == lane + 128 * j, 1.0, 0.0).astype(bf16) for j in range(pool // 128)]
    chosen[...] = jnp.dot(
        jnp.concatenate(hot, axis=1), points[...], preferred_element_type=f32
    ).astype(bf16)


def gather(picks, points):
    batch = picks.shape[1]
    pool, ins = points.shape
    return pl.pallas_call(
        gather_kernel,
        grid=(2,),
        in_specs=[
            pl.BlockSpec(picks.shape, lambda i: (0, 0)),
            pl.BlockSpec((pool, ins), lambda i: (0, 0)),
        ],
        out_specs=[pl.BlockSpec((batch, ins), lambda i: (i, 0)), ANYWHERE],
        out_shape=[jax.ShapeDtypeStruct((2 * batch, ins), bf16), TOKEN],
        compiler_params=params(),
        cost_estimate=cost(3),
        name="chosen_points",
    )(picks, points)


def cosines(chosen, omega, turns, width, store, between=None):
    tile = min(256, width)
    count = width // tile
    group = min(512, width)

    def product(c):
        return jnp.dot(chosen, omega[:, c * tile : (c + 1) * tile], preferred_element_type=f32)

    ready = product(0)
    for c in range(count):
        coming = product(c + 1) if c + 1 < count else None
        if between is not None and c > 0 and c * tile % group == 0:
            between(slice(c * tile - group, c * tile))
        cols = slice(c * tile, (c + 1) * tile)
        store(cols, scaled_cos(ready, turns[:, cols]))
        ready = coming
    if between is not None:
        between(slice(width - group, width))


def rates_kernel(start, size, begun, keep, ends, blocks, f, p, chosen, omega, phase, weights, *refs):
    refs = list(refs)
    total, feats = refs.pop(), refs.pop()
    before = refs.pop(0) if begun else None
    refs.pop()
    step = pl.program_id(0)
    width = omega.shape[1]

    @pl.when(step == 0)
    def _():
        total[...] = before[...] if begun else jnp.zeros_like(total)

    turns = phase[...] * TURN
    parts = []

    def store(cols, value):
        feats[:, cols] = value

    def between(cols):
        parts.append(jnp.dot(feats[:, cols], weights[cols, :], preferred_element_type=f32))

    cosines(chosen[start : start + size, :], omega, turns, width, store, between)
    part = parts[0]
    for q in parts[1:]:
        part = part + q
    total[...] += part

    if not begun:
        owned = refs.pop(0)

        @pl.when(step < blocks)
        def _():
            at = pl.ds(pl.multiple_of(step * width, width), width)
            owned[:, at] = feats[...]
            if keep:
                refs[0][:, at] = omega[...]
                refs[1][:, at] = turns

    @pl.when(step == pl.num_programs(0) - 1)
    def _():
        if ends:
            split(total, f[0], 0, *refs[-2:])
        else:
            refs[-1][...] = total[...]


def split(value, f, bit, kept, sent):
    rows = kept.shape[0]
    side = lax.rem(f // 2**bit, 2)
    kept[...] = value[pl.ds(pl.multiple_of(side * rows, rows), rows), :]
    sent[...] = value[pl.ds(pl.multiple_of((1 - side) * rows, rows), rows), :].astype(bf16)


def rates(f, p, chosen, omega, phase, weights, start, size, owned, blocks, before, keep, ends, deps):
    ins, feat_dev = omega.shape
    k = weights.shape[1]
    width = min(2048, owned)
    count = feat_dev // width
    own = owned // width
    low, high = blocks[0] * count // 2, blocks[1] * count // 2

    def turned(i, p):
        return lax.rem(i + low + p[0] * own, count)

    begun = before is not None
    outs = []
    if not begun:
        outs.append(jax.ShapeDtypeStruct((size, owned), bf16))
    if keep:
        outs += [jax.ShapeDtypeStruct((ins, owned), bf16), jax.ShapeDtypeStruct((1, owned), f32)]
    if ends:
        outs += [jax.ShapeDtypeStruct((size // 2, k), t) for t in (f32, bf16)]
    else:
        outs.append(jax.ShapeDtypeStruct((size, k), f32))
    args = [f, p, chosen, omega, phase, weights] + ([before] if begun else []) + deps

    def kernel(*refs):
        inputs = len(args) - len(deps)
        rates_kernel(
            start, size, begun, keep, ends, own, *refs[:inputs], *refs[inputs + len(deps) :]
        )

    return pl.pallas_call(
        kernel,
        grid_spec=pltpu.PrefetchScalarGridSpec(
            num_scalar_prefetch=2,
            grid=(high - low,),
            in_specs=[
                IN_VMEM,
                pl.BlockSpec((ins, width), lambda i, f, p: (0, turned(i, p))),
                pl.BlockSpec((1, width), lambda i, f, p: (0, turned(i, p))),
                pl.BlockSpec((width, k), lambda i, f, p: (turned(i, p), 0)),
            ]
            + [IN_VMEM] * begun
            + [ANYWHERE] * len(deps),
            out_specs=[IN_VMEM] * len(outs) + [ANYWHERE],
            scratch_shapes=[pltpu.VMEM((size, width), bf16), pltpu.VMEM((size, k), f32)],
        ),
        out_shape=[*outs, TOKEN],
        compiler_params=params(),
        cost_estimate=cost(12 * (high - low) / count),
        name="partial_log_rates",
    )(*args)


def features_kernel(start, size, chosen, omega, turns, *refs):
    out = refs[-2]

    def store(cols, value):
        out[:, cols] = value

    cosines(chosen[start : start + size, :], omega, turns, omega.shape[1], store)


def owned_features(chosen, omega, turns, start, size, deps):
    owned = omega.shape[1]
    return pl.pallas_call(
        functools.partial(features_kernel, start, size),
        in_specs=[IN_VMEM] * 3 + [ANYWHERE] * len(deps),
        out_specs=[IN_VMEM, ANYWHERE],
        out_shape=[jax.ShapeDtypeStruct((size, owned), bf16), TOKEN],
        compiler_params=params(),
        cost_estimate=cost(1),
        name="owned_features",
    )(chosen, omega, turns, *deps)


def total_kernel(bit, halves, f, a, b, *refs):
    value = a[...].astype(f32) + b[...].astype(f32)
    if halves:
        kept, sent, token, held = refs[-4:]
        held[...] = value
        split(held, f[0], bit, kept, sent)
    else:
        out, token = refs[-2:]
        out[...] = value.astype(bf16)


def total(f, a, b, bit, halves, deps):
    rows, k = a.shape
    if halves:
        outs = [
            jax.ShapeDtypeStruct((rows // 2, k), f32),
            jax.ShapeDtypeStruct((rows // 2, k), bf16),
        ]
    else:
        outs = [jax.ShapeDtypeStruct((rows, k), bf16)]
    return pl.pallas_call(
        functools.partial(total_kernel, bit, halves),
        grid_spec=pltpu.PrefetchScalarGridSpec(
            num_scalar_prefetch=1,
            grid=(1,),
            in_specs=[IN_VMEM] * 2 + [ANYWHERE] * len(deps),
            out_specs=[IN_VMEM] * len(outs) + [ANYWHERE],
            scratch_shapes=[pltpu.VMEM((rows, k), f32)] if halves else [],
        ),
        out_shape=[*outs, TOKEN],
        compiler_params=params(),
        cost_estimate=cost(0.5),
        name="total_rates",
    )(f, a, b, *deps)


def residual_kernel(masks, m, f, *refs):
    chunks, observed = refs[: len(masks)], refs[len(masks)]
    rate_out, residual_out, token, held = refs[-4:]
    batch = held.shape[0]
    for j, mask in enumerate(masks):
        rows = chunks[j].shape[0]
        start, bit = 0, 0
        while batch >> (bit + 1) >= rows:
            side = lax.rem(f[0] // 2**bit, 2)
            side = 1 - side if mask >> bit & 1 else side
            start = start + side * (batch >> (bit + 1))
            bit += 1
        at = pl.ds(pl.multiple_of(start, rows), rows) if bit else slice(None)
        rate = chunks[j][...].astype(f32)
        rate_out[0, at, :] = rate
        held[at, :] = jnp.exp(rate) - observed[m, at, :].astype(f32)
    residual_out[...] = held[...].T.astype(bf16)


def residuals(f, chunks, masks, counts, m, before, deps):
    n = len(chunks)
    k = chunks[0].shape[1]
    batch = counts.shape[1]
    args = [f, *chunks, counts, *deps]
    specs = [IN_VMEM] * (n + 1) + [ANYWHERE] * len(deps)
    aliases = {}
    if before is not None:
        aliases = {len(args): 0}
        args.append(before)
        specs.append(ANYWHERE)
    return pl.pallas_call(
        functools.partial(residual_kernel, masks, m),
        grid_spec=pltpu.PrefetchScalarGridSpec(
            num_scalar_prefetch=1,
            grid=(1,),
            in_specs=specs,
            out_specs=[pl.BlockSpec((1, batch, k), lambda i, _: (m, 0, 0)), IN_VMEM, ANYWHERE],
            scratch_shapes=[pltpu.VMEM((batch, k), f32)],
        ),
        out_shape=[
            jax.ShapeDtypeStruct(counts.shape, f32),
            jax.ShapeDtypeStruct((k, batch), bf16),
            TOKEN,
        ],
        input_output_aliases=aliases,
        compiler_params=params(),
        cost_estimate=cost(1),
        name="residuals",
    )(*args)


def gradient_part(n, features, residual, start, rows):
    at = pl.ds(pl.multiple_of(start, rows), rows)
    value = None
    for j in range(n):
        term = jnp.dot(residual[j][...], features[j][:, at], preferred_element_type=f32)
        value = term if value is None else value + term
    return value


def first_part_kernel(n, *refs):
    features, residual, master = refs[:n], refs[n : 2 * n], refs[2 * n]
    out = refs[-2]
    rows = out.shape[0]
    out[...] = gradient_part(n, features, residual, pl.program_id(0) * rows, rows).T + master[0]


def first_part(features, residual, master, deps):
    n = len(features)
    owned, k = master.shape[1:]
    rows = min(512, owned)
    return pl.pallas_call(
        functools.partial(first_part_kernel, n),
        grid=(owned // rows,),
        in_specs=[IN_VMEM] * (2 * n)
        + [pl.BlockSpec((1, rows, k), lambda i: (0, i, 0))]
        + [ANYWHERE] * len(deps),
        out_specs=[pl.BlockSpec((rows, k), lambda i: (i, 0)), ANYWHERE],
        out_shape=[jax.ShapeDtypeStruct((owned, k), f32), TOKEN],
        compiler_params=params(),
        cost_estimate=cost(5),
        name="first_part",
    )(*features, *residual, master, *deps)


def update_kernel(n, begin, *refs):
    features, residual = refs[:n], refs[n : 2 * n]
    begun, cov, master, first, second = refs[2 * n : 2 * n + 5]
    new_master, new_first, new_second, sent = refs[-4:]
    rows = master.shape[1]
    step = pl.program_id(0)
    gradient = gradient_part(n, features, residual, (begin + step) * rows, rows).T + begun[...]
    conditioned = jnp.dot(gradient.astype(bf16), cov[...], preferred_element_type=f32)
    moved_first = beta_one * first[0] + (1.0 - beta_one) * conditioned
    moved_second = beta_two * second[0] + (1.0 - beta_two) * conditioned * conditioned
    correction_one = 1.0 - beta_one**STEP
    correction_two = 1.0 - beta_two**STEP
    moved = master[0] - (learn_rate / correction_one) * moved_first / (
        jnp.sqrt(moved_second * (1.0 / correction_two)) + 1e-08
    )
    new_first[0] = moved_first
    new_second[0] = moved_second
    new_master[0] = moved
    sent[pl.ds(pl.multiple_of(step * rows, rows), rows), :] = moved.astype(bf16)


def update(features, residual, begun, cov, master, first, second, at, steps, before, deps):
    n = len(features)
    owned, k = master.shape[1:]
    rows = min(256, owned)
    state = pl.BlockSpec((1, rows, k), lambda i: (0, at + i, 0))
    flat = pl.BlockSpec((rows, k), lambda i: (at + i, 0))
    args = [*features, *residual, begun, cov, master, first, second]
    specs = [IN_VMEM] * (2 * n) + [flat, pl.BlockSpec(cov.shape, lambda i: (0, 0))] + [state] * 3
    aliases = {}
    if before is not None:
        aliases = {len(args) + j: j for j in range(3)}
        args += list(before)
        specs += [ANYWHERE] * 3
    args += deps
    specs += [ANYWHERE] * len(deps)
    return pl.pallas_call(
        functools.partial(update_kernel, n, at),
        grid=(steps,),
        in_specs=specs,
        out_specs=[state, state, state, IN_VMEM],
        out_shape=[jax.ShapeDtypeStruct(master.shape, f32)] * 3
        + [jax.ShapeDtypeStruct((steps * rows, k), bf16)],
        input_output_aliases=aliases,
        compiler_params=params(),
        cost_estimate=cost(1),
        name="update",
    )(*args)


def put_kernel(blocks, owned, n_pts, p, *refs):
    n = len(blocks)
    pieces, out, sems = refs[:n], refs[-2], refs[-1]
    me = p[0]
    copies = []
    for j, (distance, other, start) in enumerate(blocks):
        rows = pieces[j].shape[0]
        home = lax.rem(me + n_pts - distance * CORES, n_pts)
        home = home + other * (1 - 2 * lax.rem(home, 2))
        at = pl.ds(pl.multiple_of(home * owned + start, rows), rows)
        copies.append(pltpu.make_async_copy(pieces[j], out.at[at, :], sems.at[j]))
    for copy in copies:
        copy.start()
    for copy in copies:
        copy.wait()


def put(p, pieces, blocks, owned, n_pts, before):
    n = len(pieces)
    k = pieces[0].shape[1]
    return pl.pallas_call(
        functools.partial(put_kernel, blocks, owned, n_pts),
        grid_spec=pltpu.PrefetchScalarGridSpec(
            num_scalar_prefetch=1,
            grid=(1,),
            in_specs=[IN_VMEM] * n + [ANYWHERE] * (before is not None),
            out_specs=ANYWHERE,
            scratch_shapes=[pltpu.SemaphoreType.DMA((n,))],
        ),
        out_shape=jax.ShapeDtypeStruct((owned * n_pts, k), bf16),
        input_output_aliases={} if before is None else {n + 1: 0},
        compiler_params=params(),
        cost_estimate=cost(2),
        name="put_rows",
    )(p, *pieces, *([] if before is None else [before]))


def ring(x, axis, n, distance):
    return lax.ppermute(x, axis, [(i, (i + distance) % n) for i in range(n)])


def mate(x, n):
    return lax.ppermute(x, "pts", [(i, i ^ 1) for i in range(n)])


def across(x, n, distance):
    return ring(x, "pts", n, distance * CORES)


def swap(x, n, bit):
    return lax.ppermute(x, "feat", [(i, i ^ 2**bit) for i in range(n)])


def spread(x, n):
    got = [x if d == 0 else across(x, n, d) for d in range(n // CORES)]
    return [y for g in got for y in (g, mate(g, n))]


def body(n_feat, n_pts, points, picks, omega, phase, weights, counts, master, first, second, cov):
    f = lax.axis_index("feat").astype(jnp.int32).reshape(1)
    p = lax.axis_index("pts").astype(jnp.int32).reshape(1)
    owned, k = master.shape[1:]
    batch = picks.shape[1]
    bits = n_feat.bit_length() - 1
    points, picks, omega, weights = map(in_hbm, (points, picks, omega, weights))
    phase, cov = map(in_hbm, (phase[None, :], cov))
    master, first, second = map(in_hbm, (master, first, second))

    chosen, token = gather(picks, points)
    everyone = spread(chosen, n_pts)

    def some_rates(m, blocks, before, keep, ends, token):
        return rates(
            f, p, chosen, omega, phase, weights, m * batch, batch, owned, blocks, before, keep, ends, [token]
        )

    def add_up(kept, got, bit, token):
        last = bit == bits - 1
        *out, token = total(f, kept, got, bit, not last, [token])
        kept, sent = (out[0], out[0]) if last else out
        return kept, swap(sent, n_feat, bit), token

    def give_back(chunk):
        rows, masks = [chunk], [0]
        for bit in reversed(range(bits - 1)):
            rows = rows + [swap(r, n_feat, bit) for r in rows]
            masks = masks + [q ^ 2**bit for q in masks]
        return rows, masks

    feats_zero, own_omega, own_turns, kept_zero, sent, token = some_rates(
        0, (0, 2), None, True, True, token
    )
    got_zero = swap(sent, n_feat, 0)
    feats_one, begun, token = some_rates(1, (0, 1), None, False, False, token)
    for bit in range(1, bits):
        kept_zero, got_zero, token = add_up(kept_zero, got_zero, bit, token)
    kept_one, sent, token = some_rates(1, (1, 2), begun, False, True, token)
    got_one = swap(sent, n_feat, 0)
    features = [[feats_zero], [feats_one]]

    todo = [(m, j) for m in range(2) for j in range(1, n_pts)]
    share = len(todo) // 6

    def some(token, pieces):
        for _ in range(pieces * share):
            m, j = todo.pop(0)
            feats, token = owned_features(
                everyone[j], own_omega, own_turns, m * batch, batch, [token]
            )
            features[m].append(feats)
        return token

    chunk, token = total(f, kept_zero, got_zero, 0, False, [token])
    rows_zero, masks = give_back(chunk)
    token = some(token, 1)
    for bit in range(1, bits):
        kept_one, got_one, token = add_up(kept_one, got_one, bit, token)
    token = some(token, 1)
    out_rates, res, token = residuals(f, rows_zero, masks, counts, 0, None, [token])
    res_zero = spread(res, n_pts)
    token = some(token, 1)
    chunk, token = total(f, kept_one, got_one, 0, False, [token])
    rows_one, masks = give_back(chunk)
    token = some(token, 1)
    out_rates, res, token = residuals(f, rows_one, masks, counts, 1, out_rates, [token])
    res_one = spread(res, n_pts)
    token = some(token, 2)
    begun, token = first_part(features[0], res_zero, master, [token])

    steps = max(1, owned // 256)
    sizes = [2, 3, 2, 1] if steps == 8 else [1] * steps
    chips = n_pts // CORES
    state = None
    at = 0
    sent, come, starts = [], [], []
    for c, size in enumerate(sizes):
        *state, rows = update(
            features[1], res_one, begun, cov, master, first, second, at, size, state, [token]
        )
        if c >= 2 and chips > 1:
            rows, _ = lax.optimization_barrier((rows, come[c - 2][0]))
        sent.append(rows)
        come.append([across(rows, n_pts, d) for d in range(1, chips)])
        starts.append(at * (owned // steps))
        at += size
    working = None
    for group in [range(len(sizes) - 1), [len(sizes) - 1]]:
        pieces, blocks = [], []
        for c in group:
            got = come[c]
            if c and got:
                fence = sent[-1] if working is None else working
                *got, fence = lax.optimization_barrier((*got, fence))
                working = None if working is None else fence
            pieces += [sent[c], mate(sent[c], n_pts)] + got + [mate(y, n_pts) for y in got]
            blocks += [(0, other, starts[c]) for other in (0, 1)]
            blocks += [(d, other, starts[c]) for other in (0, 1) for d in range(1, chips)]
        if pieces:
            working = put(p, pieces, blocks, owned, n_pts, working)
    return out_rates, *state, working


def solution(mesh):
    placed = (
        P(("groups", "pts"), None),
        P(None, ("groups", "pts")),
        P(None, "feat"),
        P("feat"),
        P(("groups", "feat"), None),
        P(None, ("groups", "pts"), None),
        P(("groups", "feat"), "pts", None),
        P(("groups", "feat"), "pts", None),
        P(("groups", "feat"), "pts", None),
        P(),
    )
    return jax.shard_map(
        functools.partial(body, mesh.shape["feat"], mesh.shape["pts"]),
        mesh=mesh,
        in_specs=placed,
        out_specs=(
            P(None, ("groups", "pts"), None),
            P(("groups", "feat"), "pts", None),
            P(("groups", "feat"), "pts", None),
            P(("groups", "feat"), "pts", None),
            P(("groups", "feat"), None),
        ),
        check_vma=False,
    )
```

```python
import functools
import math

import jax
import jax.numpy as jnp
from jax import lax
from jax.experimental import pallas as pl
from jax.experimental.pallas import tpu as pltpu
from jax.sharding import PartitionSpec as P

F = 32768
STEP = 20
CORES = 2

beta_one = 0.9
beta_two = 0.999
learn_rate = 0.2

SINE = tuple(
    c * math.sqrt(2.0 / F) for c in (6.2825055774072665, -41.16644056159234, 74.4523919857074)
)
ROUNDER = 12582912.0
TURN = 1.0 / (2.0 * math.pi)
VMEM = 24 * 1024 * 1024

f32 = jnp.float32
bf16 = jnp.bfloat16
IN_VMEM = pl.BlockSpec(memory_space=pltpu.VMEM)
ANYWHERE = pl.BlockSpec(memory_space=pl.ANY)
TOKEN = jax.ShapeDtypeStruct((8, 128), f32)


def scaled_cos(product, phase_turns):
    turns = product * TURN + phase_turns
    v = 0.25 - jnp.abs(turns - ((turns + ROUNDER) - ROUNDER))
    s = v * v
    return (((SINE[2] * s + SINE[1]) * s + SINE[0]) * v).astype(bf16)


def cost(microseconds):
    return pl.CostEstimate(
        flops=int(microseconds * 1.0e9), bytes_accessed=1 << 10, transcendentals=0
    )


def params():
    return pltpu.CompilerParams(vmem_limit_bytes=VMEM)


def in_hbm(x):
    return pltpu.with_memory_space_constraint(x, pltpu.HBM)


def gather_kernel(picks, points, chosen, token):
    batch, pool = chosen.shape[0], points.shape[0]
    m = pl.program_id(0)
    wanted = jnp.broadcast_to(picks[pl.ds(m, 1), :], (128, batch)).T
    lane = lax.broadcasted_iota(jnp.int32, (batch, 128), 1)
    hot = [jnp.where(wanted == lane + 128 * j, 1.0, 0.0).astype(bf16) for j in range(pool // 128)]
    chosen[...] = jnp.dot(
        jnp.concatenate(hot, axis=1), points[...], preferred_element_type=f32
    ).astype(bf16)


def gather(picks, points):
    batch = picks.shape[1]
    pool, ins = points.shape
    return pl.pallas_call(
        gather_kernel,
        grid=(2,),
        in_specs=[
            pl.BlockSpec(picks.shape, lambda i: (0, 0)),
            pl.BlockSpec((pool, ins), lambda i: (0, 0)),
        ],
        out_specs=[pl.BlockSpec((batch, ins), lambda i: (i, 0)), ANYWHERE],
        out_shape=[jax.ShapeDtypeStruct((2 * batch, ins), bf16), TOKEN],
        compiler_params=params(),
        cost_estimate=cost(3),
        name="chosen_points",
    )(picks, points)


def cosines(chosen, omega, turns, width, store, between=None):
    tile = min(256, width)
    count = width // tile
    group = min(512, width)

    def product(c):
        return jnp.dot(chosen, omega[:, c * tile : (c + 1) * tile], preferred_element_type=f32)

    ready = product(0)
    for c in range(count):
        coming = product(c + 1) if c + 1 < count else None
        if between is not None and c > 0 and c * tile % group == 0:
            between(slice(c * tile - group, c * tile))
        cols = slice(c * tile, (c + 1) * tile)
        store(cols, scaled_cos(ready, turns[:, cols]))
        ready = coming
    if between is not None:
        between(slice(width - group, width))


def rates_kernel(start, size, begun, keep, ends, blocks, f, p, chosen, omega, phase, weights, *refs):
    refs = list(refs)
    total, feats = refs.pop(), refs.pop()
    before = refs.pop(0) if begun else None
    refs.pop()
    step = pl.program_id(0)
    width = omega.shape[1]

    @pl.when(step == 0)
    def _():
        total[...] = before[...] if begun else jnp.zeros_like(total)

    turns = phase[...] * TURN
    parts = []

    def store(cols, value):
        feats[:, cols] = value

    def between(cols):
        parts.append(jnp.dot(feats[:, cols], weights[cols, :], preferred_element_type=f32))

    cosines(chosen[start : start + size, :], omega, turns, width, store, between)
    part = parts[0]
    for q in parts[1:]:
        part = part + q
    total[...] += part

    if not begun:
        owned = refs.pop(0)

        @pl.when(step < blocks)
        def _():
            at = pl.ds(pl.multiple_of(step * width, width), width)
            owned[:, at] = feats[...]
            if keep:
                refs[0][:, at] = omega[...]
                refs[1][:, at] = turns

    @pl.when(step == pl.num_programs(0) - 1)
    def _():
        if ends:
            split(total, f[0], 0, *refs[-2:])
        else:
            refs[-1][...] = total[...]


def split(value, f, bit, kept, sent):
    rows = kept.shape[0]
    side = lax.rem(f // 2**bit, 2)
    kept[...] = value[pl.ds(pl.multiple_of(side * rows, rows), rows), :]
    sent[...] = value[pl.ds(pl.multiple_of((1 - side) * rows, rows), rows), :].astype(bf16)


def rates(f, p, chosen, omega, phase, weights, start, size, owned, blocks, before, keep, ends, deps):
    ins, feat_dev = omega.shape
    k = weights.shape[1]
    width = min(2048, owned)
    count = feat_dev // width
    own = owned // width
    low, high = blocks[0] * count // 2, blocks[1] * count // 2

    def turned(i, p):
        return lax.rem(i + low + p[0] * own, count)

    begun = before is not None
    outs = []
    if not begun:
        outs.append(jax.ShapeDtypeStruct((size, owned), bf16))
    if keep:
        outs += [jax.ShapeDtypeStruct((ins, owned), bf16), jax.ShapeDtypeStruct((1, owned), f32)]
    if ends:
        outs += [jax.ShapeDtypeStruct((size // 2, k), t) for t in (f32, bf16)]
    else:
        outs.append(jax.ShapeDtypeStruct((size, k), f32))
    args = [f, p, chosen, omega, phase, weights] + ([before] if begun else []) + deps

    def kernel(*refs):
        inputs = len(args) - len(deps)
        rates_kernel(
            start, size, begun, keep, ends, own, *refs[:inputs], *refs[inputs + len(deps) :]
        )

    return pl.pallas_call(
        kernel,
        grid_spec=pltpu.PrefetchScalarGridSpec(
            num_scalar_prefetch=2,
            grid=(high - low,),
            in_specs=[
                IN_VMEM,
                pl.BlockSpec((ins, width), lambda i, f, p: (0, turned(i, p))),
                pl.BlockSpec((1, width), lambda i, f, p: (0, turned(i, p))),
                pl.BlockSpec((width, k), lambda i, f, p: (turned(i, p), 0)),
            ]
            + [IN_VMEM] * begun
            + [ANYWHERE] * len(deps),
            out_specs=[IN_VMEM] * len(outs) + [ANYWHERE],
            scratch_shapes=[pltpu.VMEM((size, width), bf16), pltpu.VMEM((size, k), f32)],
        ),
        out_shape=[*outs, TOKEN],
        compiler_params=params(),
        cost_estimate=cost(12 * (high - low) / count),
        name="partial_log_rates",
    )(*args)


def features_kernel(start, size, chosen, omega, turns, *refs):
    out = refs[-2]

    def store(cols, value):
        out[:, cols] = value

    cosines(chosen[start : start + size, :], omega, turns, omega.shape[1], store)


def owned_features(chosen, omega, turns, start, size, deps):
    owned = omega.shape[1]
    return pl.pallas_call(
        functools.partial(features_kernel, start, size),
        in_specs=[IN_VMEM] * 3 + [ANYWHERE] * len(deps),
        out_specs=[IN_VMEM, ANYWHERE],
        out_shape=[jax.ShapeDtypeStruct((size, owned), bf16), TOKEN],
        compiler_params=params(),
        cost_estimate=cost(1),
        name="owned_features",
    )(chosen, omega, turns, *deps)


def total_kernel(bit, halves, f, a, b, *refs):
    value = a[...].astype(f32) + b[...].astype(f32)
    if halves:
        kept, sent, token, held = refs[-4:]
        held[...] = value
        split(held, f[0], bit, kept, sent)
    else:
        out, token = refs[-2:]
        out[...] = value.astype(bf16)


def total(f, a, b, bit, halves, deps):
    rows, k = a.shape
    if halves:
        outs = [
            jax.ShapeDtypeStruct((rows // 2, k), f32),
            jax.ShapeDtypeStruct((rows // 2, k), bf16),
        ]
    else:
        outs = [jax.ShapeDtypeStruct((rows, k), bf16)]
    return pl.pallas_call(
        functools.partial(total_kernel, bit, halves),
        grid_spec=pltpu.PrefetchScalarGridSpec(
            num_scalar_prefetch=1,
            grid=(1,),
            in_specs=[IN_VMEM] * 2 + [ANYWHERE] * len(deps),
            out_specs=[IN_VMEM] * len(outs) + [ANYWHERE],
            scratch_shapes=[pltpu.VMEM((rows, k), f32)] if halves else [],
        ),
        out_shape=[*outs, TOKEN],
        compiler_params=params(),
        cost_estimate=cost(0.5),
        name="total_rates",
    )(f, a, b, *deps)


def residual_kernel(masks, start, f, *refs):
    chunks, observed = refs[: len(masks)], refs[len(masks)]
    rate_out, residual_out, token, rates, held, sem = refs[-6:]
    size = held.shape[0]
    for j, mask in enumerate(masks):
        rows = chunks[j].shape[0]
        first, bit = 0, 0
        while size >> (bit + 1) >= rows:
            side = lax.rem(f[0] // 2**bit, 2)
            side = 1 - side if mask >> bit & 1 else side
            first = first + side * (size >> (bit + 1))
            bit += 1
        at = pl.ds(pl.multiple_of(first, rows), rows) if bit else slice(None)
        rates[at, :] = chunks[j][...].astype(f32)
    copy = pltpu.make_async_copy(rates, rate_out.at[pl.ds(start, size), :], sem)
    copy.start()
    held[...] = jnp.exp(rates[...]) - observed[start : start + size, :].astype(f32)
    residual_out[...] = held[...].T.astype(bf16)
    copy.wait()


def residuals(f, chunks, masks, counts, start, size, before, deps):
    n = len(chunks)
    k = counts.shape[1]
    args = [f, *chunks, counts, *deps]
    specs = [IN_VMEM] * (n + 1) + [ANYWHERE] * len(deps)
    aliases = {}
    if before is not None:
        aliases = {len(args): 0}
        args.append(before)
        specs.append(ANYWHERE)
    return pl.pallas_call(
        functools.partial(residual_kernel, masks, start),
        grid_spec=pltpu.PrefetchScalarGridSpec(
            num_scalar_prefetch=1,
            grid=(1,),
            in_specs=specs,
            out_specs=[ANYWHERE, IN_VMEM, ANYWHERE],
            scratch_shapes=[pltpu.VMEM((size, k), f32)] * 2 + [pltpu.SemaphoreType.DMA],
        ),
        out_shape=[
            jax.ShapeDtypeStruct(counts.shape, f32),
            jax.ShapeDtypeStruct((k, size), bf16),
            TOKEN,
        ],
        input_output_aliases=aliases,
        compiler_params=params(),
        cost_estimate=cost(1),
        name="residuals",
    )(*args)


def gradient_part(n, features, residual, start, rows):
    at = slice(start, start + rows) if isinstance(start, int) else pl.ds(pl.multiple_of(start, rows), rows)
    value = None
    for j in range(n):
        term = jnp.dot(residual[j][...], features[j][:, at], preferred_element_type=f32)
        value = term if value is None else value + term
    return value


def first_part_kernel(n, *refs):
    features, residual, master = refs[:n], refs[n : 2 * n], refs[2 * n]
    out = refs[-2]
    rows = min(512, out.shape[0])
    for start in range(0, out.shape[0], rows):
        value = gradient_part(n, features, residual, start, rows).T
        out[start : start + rows, :] = value + master[0, start : start + rows, :]


def first_part(features, residual, master, deps):
    n = len(features)
    owned, k = master.shape[1:]
    return pl.pallas_call(
        functools.partial(first_part_kernel, n),
        in_specs=[IN_VMEM] * (2 * n + 1) + [ANYWHERE] * len(deps),
        out_specs=[IN_VMEM, ANYWHERE],
        out_shape=[jax.ShapeDtypeStruct((owned, k), f32), TOKEN],
        compiler_params=params(),
        cost_estimate=cost(5),
        name="first_part",
    )(*features, *residual, master, *deps)


def update_kernel(n, begin, *refs):
    features, residual = refs[:n], refs[n : 2 * n]
    begun, cov, master, first, second = refs[2 * n : 2 * n + 5]
    new_master, new_first, new_second, sent = refs[-4:]
    rows = new_master.shape[1]
    step = pl.program_id(0)
    start = pl.multiple_of((begin + step) * rows, rows)
    at = pl.ds(start, rows)
    gradient = gradient_part(n, features, residual, start, rows).T + begun[at, :]
    conditioned = jnp.dot(gradient.astype(bf16), cov[...], preferred_element_type=f32)
    moved_first = beta_one * first[0, at, :] + (1.0 - beta_one) * conditioned
    moved_second = beta_two * second[0, at, :] + (1.0 - beta_two) * conditioned * conditioned
    correction_one = 1.0 - beta_one**STEP
    correction_two = 1.0 - beta_two**STEP
    moved = master[0, at, :] - (learn_rate / correction_one) * moved_first / (
        jnp.sqrt(moved_second * (1.0 / correction_two)) + 1e-08
    )
    new_first[0] = moved_first
    new_second[0] = moved_second
    new_master[0] = moved
    sent[pl.ds(pl.multiple_of(step * rows, rows), rows), :] = moved.astype(bf16)


def update(features, residual, begun, cov, master, first, second, at, steps, before, deps):
    n = len(features)
    owned, k = master.shape[1:]
    rows = min(256, owned)
    state = pl.BlockSpec((1, rows, k), lambda i: (0, at + i, 0))
    args = [*features, *residual, begun, cov, master, first, second]
    specs = [IN_VMEM] * (2 * n + 5)
    aliases = {}
    if before is not None:
        aliases = {len(args) + j: j for j in range(3)}
        args += list(before)
        specs += [ANYWHERE] * 3
    args += deps
    specs += [ANYWHERE] * len(deps)
    return pl.pallas_call(
        functools.partial(update_kernel, n, at),
        grid=(steps,),
        in_specs=specs,
        out_specs=[state, state, state, IN_VMEM],
        out_shape=[jax.ShapeDtypeStruct(master.shape, f32)] * 3
        + [jax.ShapeDtypeStruct((steps * rows, k), bf16)],
        input_output_aliases=aliases,
        compiler_params=params(),
        cost_estimate=cost(1),
        name="update",
    )(*args)


def put_kernel(blocks, owned, n_pts, p, *refs):
    n = len(blocks)
    pieces, out, sems = refs[:n], refs[-2], refs[-1]
    me = p[0]
    copies = []
    for j, (distance, other, start) in enumerate(blocks):
        rows = pieces[j].shape[0]
        home = lax.rem(me + n_pts - distance * CORES, n_pts)
        home = home + other * (1 - 2 * lax.rem(home, 2))
        at = pl.ds(pl.multiple_of(home * owned + start, rows), rows)
        copies.append(pltpu.make_async_copy(pieces[j], out.at[at, :], sems.at[j]))
    for copy in copies:
        copy.start()
    for copy in copies:
        copy.wait()


def put(p, pieces, blocks, owned, n_pts, before):
    n = len(pieces)
    k = pieces[0].shape[1]
    return pl.pallas_call(
        functools.partial(put_kernel, blocks, owned, n_pts),
        grid_spec=pltpu.PrefetchScalarGridSpec(
            num_scalar_prefetch=1,
            grid=(1,),
            in_specs=[IN_VMEM] * n + [ANYWHERE] * (before is not None),
            out_specs=ANYWHERE,
            scratch_shapes=[pltpu.SemaphoreType.DMA((n,))],
        ),
        out_shape=jax.ShapeDtypeStruct((owned * n_pts, k), bf16),
        input_output_aliases={} if before is None else {n + 1: 0},
        compiler_params=params(),
        cost_estimate=cost(0.01),
        name="put_rows",
    )(p, *pieces, *([] if before is None else [before]))


def ring(x, axis, n, distance):
    return lax.ppermute(x, axis, [(i, (i + distance) % n) for i in range(n)])


def mate(x, n):
    return lax.ppermute(x, "pts", [(i, i ^ 1) for i in range(n)])


def across(x, n, distance):
    return ring(x, "pts", n, distance * CORES)


def swap(x, n, bit):
    return lax.ppermute(x, "feat", [(i, i ^ 2**bit) for i in range(n)])


def spread(x, n):
    got = [x if d == 0 else across(x, n, d) for d in range(n // CORES)]
    return [y for g in got for y in (g, mate(g, n))]


def body(n_feat, n_pts, points, picks, omega, phase, weights, counts, master, first, second, cov):
    f = lax.axis_index("feat").astype(jnp.int32).reshape(1)
    p = lax.axis_index("pts").astype(jnp.int32).reshape(1)
    owned, k = master.shape[1:]
    points_here = 2 * picks.shape[1]
    size_one = points_here * 3 // 8
    parts = [(0, points_here - size_one), (points_here - size_one, size_one)]
    bits = n_feat.bit_length() - 1
    points, picks, omega, weights = map(in_hbm, (points, picks, omega, weights))
    phase = in_hbm(phase[None, :])
    outer = counts.shape
    counts = counts.reshape(points_here, k)

    chosen, token = gather(picks, points)
    everyone = spread(chosen, n_pts)

    def some_rates(m, blocks, before, keep, ends, token):
        return rates(
            f, p, chosen, omega, phase, weights, *parts[m], owned, blocks, before, keep, ends, [token]
        )

    def add_up(kept, got, bit, token):
        last = bit == bits - 1
        *out, token = total(f, kept, got, bit, not last, [token])
        kept, sent = (out[0], out[0]) if last else out
        return kept, swap(sent, n_feat, bit), token

    def give_back(chunk):
        rows, masks = [chunk], [0]
        for bit in reversed(range(bits - 1)):
            rows = rows + [swap(r, n_feat, bit) for r in rows]
            masks = masks + [q ^ 2**bit for q in masks]
        return rows, masks

    feats_zero, own_omega, own_turns, kept_zero, sent, token = some_rates(
        0, (0, 2), None, True, True, token
    )
    got_zero = swap(sent, n_feat, 0)
    feats_one, begun, token = some_rates(1, (0, 1), None, False, False, token)
    for bit in range(1, bits):
        kept_zero, got_zero, token = add_up(kept_zero, got_zero, bit, token)
    kept_one, sent, token = some_rates(1, (1, 2), begun, False, True, token)
    got_one = swap(sent, n_feat, 0)
    features = [[feats_zero], [feats_one]]

    todo = [(m, j) for m in range(2) for j in range(1, n_pts)]
    share = len(todo) // 6

    def some(token, pieces):
        for _ in range(pieces * share):
            m, j = todo.pop(0)
            feats, token = owned_features(
                everyone[j], own_omega, own_turns, *parts[m], [token]
            )
            features[m].append(feats)
        return token

    chunk, token = total(f, kept_zero, got_zero, 0, False, [token])
    rows_zero, masks = give_back(chunk)
    token = some(token, 1)
    for bit in range(1, bits):
        kept_one, got_one, token = add_up(kept_one, got_one, bit, token)
    out_rates, res, token = residuals(f, rows_zero, masks, counts, *parts[0], None, [token])
    res_zero = spread(res, n_pts)
    token = some(token, 1)
    chunk, token = total(f, kept_one, got_one, 0, False, [token])
    rows_one, masks = give_back(chunk)
    token = some(token, 1)
    out_rates, res, token = residuals(
        f, rows_one, masks, counts, *parts[1], out_rates, [token]
    )
    res_one = spread(res, n_pts)
    token = some(token, 3)
    begun, token = first_part(features[0], res_zero, master, [token])

    steps = max(1, owned // 256)
    sizes = [1, 3, 4] if steps == 8 else [1] * steps
    chips = n_pts // CORES
    state = None
    at = 0
    sent, come, starts = [], [], []
    for c, size in enumerate(sizes):
        *state, rows = update(
            features[1], res_one, begun, cov, master, first, second, at, size, state, [token]
        )
        if c and chips > 1:
            rows, _ = lax.optimization_barrier((rows, come[max(0, c - 2)][0]))
        sent.append([rows, mate(rows, n_pts)])
        come.append([across(rows, n_pts, d) for d in range(1, chips)])
        starts.append(at * (owned // steps))
        at += size
    working = None
    for group in [range(len(sizes) - 1), [len(sizes) - 1]]:
        pieces, blocks = [], []
        for c in group:
            got = come[c]
            if c and got:
                fence = sent[-1][0] if working is None else working
                *got, fence = lax.optimization_barrier((*got, fence))
                working = None if working is None else fence
            pieces += sent[c] + got + [mate(y, n_pts) for y in got]
            blocks += [(0, other, starts[c]) for other in (0, 1)]
            blocks += [(d, other, starts[c]) for other in (0, 1) for d in range(1, chips)]
        if pieces:
            working = put(p, pieces, blocks, owned, n_pts, working)
    return out_rates.reshape(outer), *state, working


def solution(mesh):
    placed = (
        P(("groups", "pts"), None),
        P(None, ("groups", "pts")),
        P(None, "feat"),
        P("feat"),
        P(("groups", "feat"), None),
        P(None, ("groups", "pts"), None),
        P(("groups", "feat"), "pts", None),
        P(("groups", "feat"), "pts", None),
        P(("groups", "feat"), "pts", None),
        P(),
    )
    return jax.shard_map(
        functools.partial(body, mesh.shape["feat"], mesh.shape["pts"]),
        mesh=mesh,
        in_specs=placed,
        out_specs=(
            P(None, ("groups", "pts"), None),
            P(("groups", "feat"), "pts", None),
            P(("groups", "feat"), "pts", None),
            P(("groups", "feat"), "pts", None),
            P(("groups", "feat"), None),
        ),
        check_vma=False,
    )
```

```python
import functools
import math

import jax
import jax.numpy as jnp
from jax import lax
from jax.experimental import pallas as pl
from jax.experimental.pallas import tpu as pltpu
from jax.sharding import PartitionSpec as P

F = 32768
STEP = 20
CORES = 2

beta_one = 0.9
beta_two = 0.999
learn_rate = 0.2

SINE = tuple(
    c * math.sqrt(2.0 / F) for c in (6.2825055774072665, -41.16644056159234, 74.4523919857074)
)
ROUNDER = 12582912.0
TURN = 1.0 / (2.0 * math.pi)
VMEM = 24 * 1024 * 1024

f32 = jnp.float32
bf16 = jnp.bfloat16
IN_VMEM = pl.BlockSpec(memory_space=pltpu.VMEM)
ANYWHERE = pl.BlockSpec(memory_space=pl.ANY)
TOKEN = jax.ShapeDtypeStruct((8, 128), f32)


def scaled_cos(product, phase_turns):
    turns = product * TURN + phase_turns
    v = 0.25 - jnp.abs(turns - ((turns + ROUNDER) - ROUNDER))
    s = v * v
    return (((SINE[2] * s + SINE[1]) * s + SINE[0]) * v).astype(bf16)


def cost(microseconds):
    return pl.CostEstimate(
        flops=int(microseconds * 1.0e9), bytes_accessed=1 << 10, transcendentals=0
    )


def params():
    return pltpu.CompilerParams(vmem_limit_bytes=VMEM)


def in_hbm(x):
    return pltpu.with_memory_space_constraint(x, pltpu.HBM)


def gather_kernel(picks, points, chosen, token):
    batch, pool = chosen.shape[0], points.shape[0]
    m = pl.program_id(0)
    wanted = jnp.broadcast_to(picks[pl.ds(m, 1), :], (128, batch)).T
    lane = lax.broadcasted_iota(jnp.int32, (batch, 128), 1)
    hot = [jnp.where(wanted == lane + 128 * j, 1.0, 0.0).astype(bf16) for j in range(pool // 128)]
    chosen[...] = jnp.dot(
        jnp.concatenate(hot, axis=1), points[...], preferred_element_type=f32
    ).astype(bf16)


def gather(picks, points):
    batch = picks.shape[1]
    pool, ins = points.shape
    return pl.pallas_call(
        gather_kernel,
        grid=(2,),
        in_specs=[
            pl.BlockSpec(picks.shape, lambda i: (0, 0)),
            pl.BlockSpec((pool, ins), lambda i: (0, 0)),
        ],
        out_specs=[pl.BlockSpec((batch, ins), lambda i: (i, 0)), ANYWHERE],
        out_shape=[jax.ShapeDtypeStruct((2 * batch, ins), bf16), TOKEN],
        compiler_params=params(),
        cost_estimate=cost(3),
        name="chosen_points",
    )(picks, points)


def cosines(chosen, omega, turns, width, store, between=None):
    tile = min(256, width)
    count = width // tile
    group = min(512, width)

    def product(c):
        return jnp.dot(chosen, omega[:, c * tile : (c + 1) * tile], preferred_element_type=f32)

    ready = product(0)
    for c in range(count):
        coming = product(c + 1) if c + 1 < count else None
        if between is not None and c > 0 and c * tile % group == 0:
            between(slice(c * tile - group, c * tile))
        cols = slice(c * tile, (c + 1) * tile)
        store(cols, scaled_cos(ready, turns[:, cols]))
        ready = coming
    if between is not None:
        between(slice(width - group, width))


def rates_kernel(start, size, begun, keep, ends, blocks, f, p, chosen, omega, phase, weights, *refs):
    refs = list(refs)
    total, feats = refs.pop(), refs.pop()
    before = refs.pop(0) if begun else None
    refs.pop()
    step = pl.program_id(0)
    width = omega.shape[1]

    @pl.when(step == 0)
    def _():
        total[...] = before[...] if begun else jnp.zeros_like(total)

    turns = phase[...] * TURN
    parts = []

    def store(cols, value):
        feats[:, cols] = value

    def between(cols):
        parts.append(jnp.dot(feats[:, cols], weights[cols, :], preferred_element_type=f32))

    cosines(chosen[start : start + size, :], omega, turns, width, store, between)
    part = parts[0]
    for q in parts[1:]:
        part = part + q
    total[...] += part

    if not begun:
        owned = refs.pop(0)

        @pl.when(step < blocks)
        def _():
            at = pl.ds(pl.multiple_of(step * width, width), width)
            owned[:, at] = feats[...]
            if keep:
                refs[0][:, at] = omega[...]
                refs[1][:, at] = turns

    @pl.when(step == pl.num_programs(0) - 1)
    def _():
        if ends:
            split(total, f[0], 0, *refs[-2:])
        else:
            refs[-1][...] = total[...]


def split(value, f, bit, kept, sent):
    rows = kept.shape[0]
    side = lax.rem(f // 2**bit, 2)
    kept[...] = value[pl.ds(pl.multiple_of(side * rows, rows), rows), :]
    sent[...] = value[pl.ds(pl.multiple_of((1 - side) * rows, rows), rows), :].astype(bf16)


def rates(f, p, chosen, omega, phase, weights, start, size, owned, blocks, before, keep, ends, deps):
    ins, feat_dev = omega.shape
    k = weights.shape[1]
    width = min(2048, owned)
    count = feat_dev // width
    own = owned // width
    low, high = blocks[0] * count // 2, blocks[1] * count // 2

    def turned(i, p):
        return lax.rem(i + low + p[0] * own, count)

    begun = before is not None
    outs = []
    if not begun:
        outs.append(jax.ShapeDtypeStruct((size, owned), bf16))
    if keep:
        outs += [jax.ShapeDtypeStruct((ins, owned), bf16), jax.ShapeDtypeStruct((1, owned), f32)]
    if ends:
        outs += [jax.ShapeDtypeStruct((size // 2, k), t) for t in (f32, bf16)]
    else:
        outs.append(jax.ShapeDtypeStruct((size, k), f32))
    args = [f, p, chosen, omega, phase, weights] + ([before] if begun else []) + deps

    def kernel(*refs):
        inputs = len(args) - len(deps)
        rates_kernel(
            start, size, begun, keep, ends, own, *refs[:inputs], *refs[inputs + len(deps) :]
        )

    return pl.pallas_call(
        kernel,
        grid_spec=pltpu.PrefetchScalarGridSpec(
            num_scalar_prefetch=2,
            grid=(high - low,),
            in_specs=[
                IN_VMEM,
                pl.BlockSpec((ins, width), lambda i, f, p: (0, turned(i, p))),
                pl.BlockSpec((1, width), lambda i, f, p: (0, turned(i, p))),
                pl.BlockSpec((width, k), lambda i, f, p: (turned(i, p), 0)),
            ]
            + [IN_VMEM] * begun
            + [ANYWHERE] * len(deps),
            out_specs=[IN_VMEM] * len(outs) + [ANYWHERE],
            scratch_shapes=[pltpu.VMEM((size, width), bf16), pltpu.VMEM((size, k), f32)],
        ),
        out_shape=[*outs, TOKEN],
        compiler_params=params(),
        cost_estimate=cost(12 * (high - low) / count),
        name="partial_log_rates",
    )(*args)


def features_kernel(start, size, chosen, omega, turns, *refs):
    out = refs[-2]

    def store(cols, value):
        out[:, cols] = value

    cosines(chosen[start : start + size, :], omega, turns, omega.shape[1], store)


def owned_features(chosen, omega, turns, start, size, weight, deps):
    owned = omega.shape[1]
    return pl.pallas_call(
        functools.partial(features_kernel, start, size),
        in_specs=[IN_VMEM] * 3 + [ANYWHERE] * len(deps),
        out_specs=[IN_VMEM, ANYWHERE],
        out_shape=[jax.ShapeDtypeStruct((size, owned), bf16), TOKEN],
        compiler_params=params(),
        cost_estimate=cost(weight),
        name="owned_features",
    )(chosen, omega, turns, *deps)


def total_kernel(bit, halves, f, a, b, *refs):
    value = a[...].astype(f32) + b[...].astype(f32)
    if halves:
        kept, sent, token, held = refs[-4:]
        held[...] = value
        split(held, f[0], bit, kept, sent)
    else:
        out, token = refs[-2:]
        out[...] = value.astype(bf16)


def total(f, a, b, bit, halves, deps):
    rows, k = a.shape
    if halves:
        outs = [
            jax.ShapeDtypeStruct((rows // 2, k), f32),
            jax.ShapeDtypeStruct((rows // 2, k), bf16),
        ]
    else:
        outs = [jax.ShapeDtypeStruct((rows, k), bf16)]
    return pl.pallas_call(
        functools.partial(total_kernel, bit, halves),
        grid_spec=pltpu.PrefetchScalarGridSpec(
            num_scalar_prefetch=1,
            grid=(1,),
            in_specs=[IN_VMEM] * 2 + [ANYWHERE] * len(deps),
            out_specs=[IN_VMEM] * len(outs) + [ANYWHERE],
            scratch_shapes=[pltpu.VMEM((rows, k), f32)] if halves else [],
        ),
        out_shape=[*outs, TOKEN],
        compiler_params=params(),
        cost_estimate=cost(0.5),
        name="total_rates",
    )(f, a, b, *deps)


def residual_kernel(masks, start, f, *refs):
    chunks, observed = refs[: len(masks)], refs[len(masks)]
    rate_out, residual_out, token, rates, held, sem = refs[-6:]
    size = held.shape[0]
    for j, mask in enumerate(masks):
        rows = chunks[j].shape[0]
        first, bit = 0, 0
        while size >> (bit + 1) >= rows:
            side = lax.rem(f[0] // 2**bit, 2)
            side = 1 - side if mask >> bit & 1 else side
            first = first + side * (size >> (bit + 1))
            bit += 1
        at = pl.ds(pl.multiple_of(first, rows), rows) if bit else slice(None)
        rates[at, :] = chunks[j][...].astype(f32)
    copy = pltpu.make_async_copy(rates, rate_out.at[pl.ds(start, size), :], sem)
    copy.start()
    held[...] = jnp.exp(rates[...]) - observed[start : start + size, :].astype(f32)
    residual_out[...] = held[...].T.astype(bf16)
    copy.wait()


def residuals(f, chunks, masks, counts, start, size, before, deps):
    n = len(chunks)
    k = counts.shape[1]
    args = [f, *chunks, counts, *deps]
    specs = [IN_VMEM] * (n + 1) + [ANYWHERE] * len(deps)
    aliases = {}
    if before is not None:
        aliases = {len(args): 0}
        args.append(before)
        specs.append(ANYWHERE)
    return pl.pallas_call(
        functools.partial(residual_kernel, masks, start),
        grid_spec=pltpu.PrefetchScalarGridSpec(
            num_scalar_prefetch=1,
            grid=(1,),
            in_specs=specs,
            out_specs=[ANYWHERE, IN_VMEM, ANYWHERE],
            scratch_shapes=[pltpu.VMEM((size, k), f32)] * 2 + [pltpu.SemaphoreType.DMA],
        ),
        out_shape=[
            jax.ShapeDtypeStruct(counts.shape, f32),
            jax.ShapeDtypeStruct((k, size), bf16),
            TOKEN,
        ],
        input_output_aliases=aliases,
        compiler_params=params(),
        cost_estimate=cost(1),
        name="residuals",
    )(*args)


def gradient_part(n, features, residual, start, rows):
    at = slice(start, start + rows) if isinstance(start, int) else pl.ds(pl.multiple_of(start, rows), rows)
    value = None
    for j in range(n):
        term = jnp.dot(residual[j][...], features[j][:, at], preferred_element_type=f32)
        value = term if value is None else value + term
    return value


def first_part_kernel(n, *refs):
    features, residual, master = refs[:n], refs[n : 2 * n], refs[2 * n]
    out = refs[-2]
    rows = min(512, out.shape[0])
    for start in range(0, out.shape[0], rows):
        value = gradient_part(n, features, residual, start, rows).T
        out[start : start + rows, :] = value + master[0, start : start + rows, :]


def first_part(features, residual, master, deps):
    n = len(features)
    owned, k = master.shape[1:]
    return pl.pallas_call(
        functools.partial(first_part_kernel, n),
        in_specs=[IN_VMEM] * (2 * n + 1) + [ANYWHERE] * len(deps),
        out_specs=[IN_VMEM, ANYWHERE],
        out_shape=[jax.ShapeDtypeStruct((owned, k), f32), TOKEN],
        compiler_params=params(),
        cost_estimate=cost(0.3),
        name="first_part",
    )(*features, *residual, master, *deps)


def update_kernel(n, begin, *refs):
    features, residual = refs[:n], refs[n : 2 * n]
    begun, cov, master, first, second = refs[2 * n : 2 * n + 5]
    new_master, new_first, new_second, sent = refs[-4:]
    rows = new_master.shape[1]
    step = pl.program_id(0)
    start = pl.multiple_of((begin + step) * rows, rows)
    at = pl.ds(start, rows)
    gradient = gradient_part(n, features, residual, start, rows).T + begun[at, :]
    conditioned = jnp.dot(gradient.astype(bf16), cov[...], preferred_element_type=f32)
    moved_first = beta_one * first[0, at, :] + (1.0 - beta_one) * conditioned
    moved_second = beta_two * second[0, at, :] + (1.0 - beta_two) * conditioned * conditioned
    correction_one = 1.0 - beta_one**STEP
    correction_two = 1.0 - beta_two**STEP
    moved = master[0, at, :] - (learn_rate / correction_one) * moved_first / (
        jnp.sqrt(moved_second * (1.0 / correction_two)) + 1e-08
    )
    new_first[0] = moved_first
    new_second[0] = moved_second
    new_master[0] = moved
    sent[pl.ds(pl.multiple_of(step * rows, rows), rows), :] = moved.astype(bf16)


def update(features, residual, begun, cov, master, first, second, at, steps, before, deps):
    n = len(features)
    owned, k = master.shape[1:]
    rows = min(256, owned)
    state = pl.BlockSpec((1, rows, k), lambda i: (0, at + i, 0))
    args = [*features, *residual, begun, cov, master, first, second]
    specs = [IN_VMEM] * (2 * n + 5)
    aliases = {}
    if before is not None:
        aliases = {len(args) + j: j for j in range(3)}
        args += list(before)
        specs += [ANYWHERE] * 3
    args += deps
    specs += [ANYWHERE] * len(deps)
    return pl.pallas_call(
        functools.partial(update_kernel, n, at),
        grid=(steps,),
        in_specs=specs,
        out_specs=[state, state, state, IN_VMEM],
        out_shape=[jax.ShapeDtypeStruct(master.shape, f32)] * 3
        + [jax.ShapeDtypeStruct((steps * rows, k), bf16)],
        input_output_aliases=aliases,
        compiler_params=params(),
        cost_estimate=cost(4),
        name="update",
    )(*args)


def put_kernel(blocks, owned, n_pts, p, *refs):
    n = len(blocks)
    pieces, out, sems = refs[:n], refs[-2], refs[-1]
    me = p[0]
    copies = []
    for j, (distance, other, start) in enumerate(blocks):
        rows = pieces[j].shape[0]
        home = lax.rem(me + n_pts - distance * CORES, n_pts)
        home = home + other * (1 - 2 * lax.rem(home, 2))
        at = pl.ds(pl.multiple_of(home * owned + start, rows), rows)
        copies.append(pltpu.make_async_copy(pieces[j], out.at[at, :], sems.at[j]))
    for copy in copies:
        copy.start()
    for copy in copies:
        copy.wait()


def put(p, pieces, blocks, owned, n_pts, before):
    n = len(pieces)
    k = pieces[0].shape[1]
    return pl.pallas_call(
        functools.partial(put_kernel, blocks, owned, n_pts),
        grid_spec=pltpu.PrefetchScalarGridSpec(
            num_scalar_prefetch=1,
            grid=(1,),
            in_specs=[IN_VMEM] * n + [ANYWHERE] * (before is not None),
            out_specs=ANYWHERE,
            scratch_shapes=[pltpu.SemaphoreType.DMA((n,))],
        ),
        out_shape=jax.ShapeDtypeStruct((owned * n_pts, k), bf16),
        input_output_aliases={} if before is None else {n + 1: 0},
        compiler_params=params(),
        cost_estimate=cost(0.01),
        name="put_rows",
    )(p, *pieces, *([] if before is None else [before]))


def ring(x, axis, n, distance):
    return lax.ppermute(x, axis, [(i, (i + distance) % n) for i in range(n)])


def mate(x, n):
    return lax.ppermute(x, "pts", [(i, i ^ 1) for i in range(n)])


def across(x, n, distance):
    return ring(x, "pts", n, distance * CORES)


def swap(x, n, bit):
    return lax.ppermute(x, "feat", [(i, i ^ 2**bit) for i in range(n)])


def spread(x, n):
    got = [x if d == 0 else across(x, n, d) for d in range(n // CORES)]
    return [y for g in got for y in (g, mate(g, n))]


def body(n_feat, n_pts, points, picks, omega, phase, weights, counts, master, first, second, cov):
    f = lax.axis_index("feat").astype(jnp.int32).reshape(1)
    p = lax.axis_index("pts").astype(jnp.int32).reshape(1)
    owned, k = master.shape[1:]
    points_here = 2 * picks.shape[1]
    size_one = points_here * 3 // 8
    parts = [(0, points_here - size_one), (points_here - size_one, size_one)]
    bits = n_feat.bit_length() - 1
    points, picks, omega, weights = map(in_hbm, (points, picks, omega, weights))
    phase = in_hbm(phase[None, :])
    outer = counts.shape
    counts = counts.reshape(points_here, k)

    chosen, token = gather(picks, points)
    everyone = spread(chosen, n_pts)

    def some_rates(m, blocks, before, keep, ends, token):
        return rates(
            f, p, chosen, omega, phase, weights, *parts[m], owned, blocks, before, keep, ends, [token]
        )

    def add_up(kept, got, bit, token):
        last = bit == bits - 1
        *out, token = total(f, kept, got, bit, not last, [token])
        kept, sent = (out[0], out[0]) if last else out
        return kept, swap(sent, n_feat, bit), token

    def give_back(chunk):
        rows, masks = [chunk], [0]
        for bit in reversed(range(bits - 1)):
            rows = rows + [swap(r, n_feat, bit) for r in rows]
            masks = masks + [q ^ 2**bit for q in masks]
        return rows, masks

    feats_zero, own_omega, own_turns, kept_zero, sent, token = some_rates(
        0, (0, 2), None, True, True, token
    )
    got_zero = swap(sent, n_feat, 0)
    feats_one, begun, token = some_rates(1, (0, 1), None, False, False, token)
    for bit in range(1, bits):
        kept_zero, got_zero, token = add_up(kept_zero, got_zero, bit, token)
    kept_one, sent, token = some_rates(1, (1, 2), begun, False, True, token)
    got_one = swap(sent, n_feat, 0)
    features = [[feats_zero], [feats_one]]

    todo = [(m, j) for m in range(2) for j in range(1, n_pts)]
    share = len(todo) // 6

    def some(token, pieces, weight=1.0):
        for _ in range(pieces * share):
            m, j = todo.pop(0)
            feats, token = owned_features(
                everyone[j], own_omega, own_turns, *parts[m], weight, [token]
            )
            features[m].append(feats)
        return token

    token = some(token, 1)
    for bit in range(1, bits):
        kept_one, got_one, token = add_up(kept_one, got_one, bit, token)
    chunk, token = total(f, kept_zero, got_zero, 0, False, [token])
    rows_zero, masks = give_back(chunk)
    token = some(token, 1)
    chunk, token = total(f, kept_one, got_one, 0, False, [token])
    rows_one, masks = give_back(chunk)
    out_rates, res_zero, token = residuals(f, rows_zero, masks, counts, *parts[0], None, [token])
    far_zero = [across(res_zero, n_pts, d) for d in range(1, n_pts // CORES)]
    token = some(token, 1)
    out_rates, res_one, token = residuals(
        f, rows_one, masks, counts, *parts[1], out_rates, [token]
    )
    far_one = [across(res_one, n_pts, d) for d in range(1, n_pts // CORES)]
    token = some(token, 2, 0.1)
    *far_zero, token = lax.optimization_barrier((*far_zero, token))
    res_zero = [y for g in [res_zero] + far_zero for y in (g, mate(g, n_pts))]
    token = some(token, 1, 0.1)
    *far_one, token = lax.optimization_barrier((*far_one, token))
    res_one = [y for g in [res_one] + far_one for y in (g, mate(g, n_pts))]
    begun, token = first_part(features[0], res_zero, master, [token])

    steps = max(1, owned // 256)
    sizes = [1, 2, 2, 3] if steps == 8 else [1] * steps
    chips = n_pts // CORES
    state = None
    at = 0
    sent, come, starts = [], [], []
    for c, size in enumerate(sizes):
        *state, rows = update(
            features[1], res_one, begun, cov, master, first, second, at, size, state, [token] + (come[c - 2] if c > 1 else [])
        )
        sent.append([rows, mate(rows, n_pts)])
        come.append([across(rows, n_pts, d) for d in range(1, chips)])
        starts.append(at * (owned // steps))
        at += size
    working = None
    for group in [range(len(sizes) - 1), [len(sizes) - 1]]:
        pieces, blocks = [], []
        for c in group:
            got = come[c]
            if c and got:
                fence = sent[-1][0] if working is None else working
                *got, fence = lax.optimization_barrier((*got, fence))
                working = None if working is None else fence
            pieces += sent[c] + got + [mate(y, n_pts) for y in got]
            blocks += [(0, other, starts[c]) for other in (0, 1)]
            blocks += [(d, other, starts[c]) for other in (0, 1) for d in range(1, chips)]
        if pieces:
            working = put(p, pieces, blocks, owned, n_pts, working)
    return out_rates.reshape(outer), *state, working


def solution(mesh):
    placed = (
        P(("groups", "pts"), None),
        P(None, ("groups", "pts")),
        P(None, "feat"),
        P("feat"),
        P(("groups", "feat"), None),
        P(None, ("groups", "pts"), None),
        P(("groups", "feat"), "pts", None),
        P(("groups", "feat"), "pts", None),
        P(("groups", "feat"), "pts", None),
        P(),
    )
    return jax.shard_map(
        functools.partial(body, mesh.shape["feat"], mesh.shape["pts"]),
        mesh=mesh,
        in_specs=placed,
        out_specs=(
            P(None, ("groups", "pts"), None),
            P(("groups", "feat"), "pts", None),
            P(("groups", "feat"), "pts", None),
            P(("groups", "feat"), "pts", None),
            P(("groups", "feat"), None),
        ),
        check_vma=False,
    )
```

```python
import functools
import math

import jax
import jax.numpy as jnp
from jax import lax
from jax.experimental import pallas as pl
from jax.experimental.pallas import tpu as pltpu
from jax.sharding import PartitionSpec as P

F = 32768
STEP = 20
CORES = 2

beta_one = 0.9
beta_two = 0.999
learn_rate = 0.2

SINE = tuple(
    c * math.sqrt(2.0 / F) for c in (6.2825055774072665, -41.16644056159234, 74.4523919857074)
)
ROUNDER = 12582912.0
TURN = 1.0 / (2.0 * math.pi)
VMEM = 24 * 1024 * 1024

f32 = jnp.float32
bf16 = jnp.bfloat16
IN_VMEM = pl.BlockSpec(memory_space=pltpu.VMEM)
ANYWHERE = pl.BlockSpec(memory_space=pl.ANY)
TOKEN = jax.ShapeDtypeStruct((8, 128), f32)


def scaled_cos(product, phase_turns):
    turns = product * TURN + phase_turns
    v = 0.25 - jnp.abs(turns - ((turns + ROUNDER) - ROUNDER))
    s = v * v
    return (((SINE[2] * s + SINE[1]) * s + SINE[0]) * v).astype(bf16)


def cost(microseconds):
    return pl.CostEstimate(
        flops=int(microseconds * 1.0e9), bytes_accessed=1 << 10, transcendentals=0
    )


def params():
    return pltpu.CompilerParams(vmem_limit_bytes=VMEM)


def in_hbm(x):
    return pltpu.with_memory_space_constraint(x, pltpu.HBM)


def gather_kernel(picks, points, chosen, token):
    batch, pool = picks.shape[1], points.shape[0]
    lane = lax.broadcasted_iota(jnp.int32, (batch, 128), 1)
    for m in range(2):
        wanted = jnp.broadcast_to(picks[m : m + 1, :], (128, batch)).T
        hot = [
            jnp.where(wanted == lane + 128 * j, 1.0, 0.0).astype(bf16) for j in range(pool // 128)
        ]
        chosen[m * batch : (m + 1) * batch, :] = jnp.dot(
            jnp.concatenate(hot, axis=1), points[...], preferred_element_type=f32
        ).astype(bf16)


def gather(picks, points):
    batch = picks.shape[1]
    pool, ins = points.shape
    return pl.pallas_call(
        gather_kernel,
        grid=(1,),
        in_specs=[
            pl.BlockSpec(picks.shape, lambda i: (0, 0)),
            pl.BlockSpec((pool, ins), lambda i: (0, 0)),
        ],
        out_specs=[IN_VMEM, ANYWHERE],
        out_shape=[jax.ShapeDtypeStruct((2 * batch, ins), bf16), TOKEN],
        compiler_params=params(),
        cost_estimate=cost(3),
        name="chosen_points",
    )(picks, points)


def cosines(chosen, omega, phase, base, width, store, between=None):
    tile = min(256, width)
    count = width // tile
    group = min(512, width)

    def part(start, size):
        if isinstance(base, int):
            return slice(base + start, base + start + size)
        return pl.ds(pl.multiple_of(base + start, tile), size)

    def product(c):
        return jnp.dot(chosen, omega[:, part(c * tile, tile)], preferred_element_type=f32)

    ready = product(0)
    for c in range(count):
        coming = product(c + 1) if c + 1 < count else None
        if between is not None and c > 0 and c * tile % group == 0:
            between(c * tile - group, part(c * tile - group, group), group)
        turns = phase[:, part(c * tile, tile)] * TURN
        store(slice(c * tile, (c + 1) * tile), scaled_cos(ready, turns))
        ready = coming
    if between is not None:
        between(width - group, part(width - group, group), group)


def rates_kernel(start, size, low, high, width, own, begun, keep, ends, f, p, chosen, omega, phase, weights, *refs):
    refs = list(refs)
    total, feats = refs.pop(), refs.pop()
    before = refs.pop(0) if begun else None
    refs.pop()
    owned = None if begun else refs.pop(0)
    count = omega.shape[1] // width
    total[...] = before[...] if begun else jnp.zeros_like(total)

    def block(place, into, offset):
        parts = []

        def store(cols, value):
            into[:, offset + cols.start : offset + cols.stop] = value

        def between(at, rows, group):
            done = into[:, offset + at : offset + at + group]
            parts.append(jnp.dot(done, weights[rows, :], preferred_element_type=f32))

        cosines(
            chosen[start : start + size, :], omega, phase, place * width, width, store, between
        )
        part = parts[0]
        for q in parts[1:]:
            part = part + q
        total[...] += part

    if not begun:
        for step in range(own):
            block(p[0] * own + step, owned, step * width)

    def turn(step, _):
        block(lax.rem(step + p[0] * own, count), feats, 0)
        return _

    lax.fori_loop(low if begun else own, high, turn, 0)
    if keep:
        at = pl.ds(pl.multiple_of(p[0] * own * width, width), own * width)
        refs[0][...] = omega[:, at]
        refs[1][...] = phase[:, at]
    if ends:
        split(total, f[0], 0, *refs[-2:])
    else:
        refs[-1][...] = total[...]


def split(value, f, bit, kept, sent):
    rows = kept.shape[0]
    side = lax.rem(f // 2**bit, 2)
    kept[...] = value[pl.ds(pl.multiple_of(side * rows, rows), rows), :]
    sent[...] = value[pl.ds(pl.multiple_of((1 - side) * rows, rows), rows), :].astype(bf16)


def rates(f, p, chosen, omega, phase, weights, start, size, owned, blocks, before, keep, ends, deps):
    ins, feat_dev = omega.shape
    k = weights.shape[1]
    width = min(2048, owned)
    count = feat_dev // width
    own = owned // width
    low, high = blocks[0] * count // 2, blocks[1] * count // 2

    begun = before is not None
    outs = []
    if not begun:
        outs.append(jax.ShapeDtypeStruct((size, owned), bf16))
    if keep:
        outs += [jax.ShapeDtypeStruct((ins, owned), bf16), jax.ShapeDtypeStruct((1, owned), f32)]
    if ends:
        outs += [jax.ShapeDtypeStruct((size // 2, k), t) for t in (f32, bf16)]
    else:
        outs.append(jax.ShapeDtypeStruct((size, k), f32))
    args = [f, p, chosen, omega, phase, weights] + ([before] if begun else []) + deps

    def kernel(*refs):
        inputs = len(args) - len(deps)
        rates_kernel(
            start, size, low, high, width, own, begun, keep, ends, *refs[:inputs], *refs[inputs + len(deps) :]
        )

    return pl.pallas_call(
        kernel,
        grid_spec=pltpu.PrefetchScalarGridSpec(
            num_scalar_prefetch=2,
            grid=(1,),
            in_specs=[IN_VMEM] * (4 + begun) + [ANYWHERE] * len(deps),
            out_specs=[IN_VMEM] * len(outs) + [ANYWHERE],
            scratch_shapes=[pltpu.VMEM((size, width), bf16), pltpu.VMEM((size, k), f32)],
        ),
        out_shape=[*outs, TOKEN],
        compiler_params=params(),
        cost_estimate=cost(12 * (high - low) / count),
        name="partial_log_rates",
    )(*args)


def features_kernel(start, size, chosen, omega, phase, *refs):
    out = refs[-2]

    def store(cols, value):
        out[:, cols] = value

    cosines(chosen[start : start + size, :], omega, phase, 0, omega.shape[1], store)


def owned_features(chosen, omega, phase, start, size, weight, deps):
    owned = omega.shape[1]
    return pl.pallas_call(
        functools.partial(features_kernel, start, size),
        in_specs=[IN_VMEM] * 3 + [ANYWHERE] * len(deps),
        out_specs=[IN_VMEM, ANYWHERE],
        out_shape=[jax.ShapeDtypeStruct((size, owned), bf16), TOKEN],
        compiler_params=params(),
        cost_estimate=cost(weight),
        name="owned_features",
    )(chosen, omega, phase, *deps)


def total_kernel(bit, halves, f, a, b, *refs):
    value = a[...].astype(f32) + b[...].astype(f32)
    if halves:
        kept, sent, token, held = refs[-4:]
        held[...] = value
        split(held, f[0], bit, kept, sent)
    else:
        out, token = refs[-2:]
        out[...] = value.astype(bf16)


def total(f, a, b, bit, halves, deps):
    rows, k = a.shape
    if halves:
        outs = [
            jax.ShapeDtypeStruct((rows // 2, k), f32),
            jax.ShapeDtypeStruct((rows // 2, k), bf16),
        ]
    else:
        outs = [jax.ShapeDtypeStruct((rows, k), bf16)]
    return pl.pallas_call(
        functools.partial(total_kernel, bit, halves),
        grid_spec=pltpu.PrefetchScalarGridSpec(
            num_scalar_prefetch=1,
            grid=(1,),
            in_specs=[IN_VMEM] * 2 + [ANYWHERE] * len(deps),
            out_specs=[IN_VMEM] * len(outs) + [ANYWHERE],
            scratch_shapes=[pltpu.VMEM((rows, k), f32)] if halves else [],
        ),
        out_shape=[*outs, TOKEN],
        compiler_params=params(),
        cost_estimate=cost(0.5),
        name="total_rates",
    )(f, a, b, *deps)


def residual_kernel(masks, start, f, *refs):
    chunks, observed = refs[: len(masks)], refs[len(masks)]
    rate_out, residual_out, token, rates, held, sem = refs[-6:]
    size = held.shape[0]
    for j, mask in enumerate(masks):
        rows = chunks[j].shape[0]
        first, bit = 0, 0
        while size >> (bit + 1) >= rows:
            side = lax.rem(f[0] // 2**bit, 2)
            side = 1 - side if mask >> bit & 1 else side
            first = first + side * (size >> (bit + 1))
            bit += 1
        at = pl.ds(pl.multiple_of(first, rows), rows) if bit else slice(None)
        rates[at, :] = chunks[j][...].astype(f32)
    copy = pltpu.make_async_copy(rates, rate_out.at[pl.ds(start, size), :], sem)
    copy.start()
    held[...] = jnp.exp(rates[...]) - observed[start : start + size, :].astype(f32)
    residual_out[...] = held[...].T.astype(bf16)
    copy.wait()


def residuals(f, chunks, masks, counts, start, size, before, deps):
    n = len(chunks)
    k = counts.shape[1]
    args = [f, *chunks, counts, *deps]
    specs = [IN_VMEM] * (n + 1) + [ANYWHERE] * len(deps)
    aliases = {}
    if before is not None:
        aliases = {len(args): 0}
        args.append(before)
        specs.append(ANYWHERE)
    return pl.pallas_call(
        functools.partial(residual_kernel, masks, start),
        grid_spec=pltpu.PrefetchScalarGridSpec(
            num_scalar_prefetch=1,
            grid=(1,),
            in_specs=specs,
            out_specs=[ANYWHERE, IN_VMEM, ANYWHERE],
            scratch_shapes=[pltpu.VMEM((size, k), f32)] * 2 + [pltpu.SemaphoreType.DMA],
        ),
        out_shape=[
            jax.ShapeDtypeStruct(counts.shape, f32),
            jax.ShapeDtypeStruct((k, size), bf16),
            TOKEN,
        ],
        input_output_aliases=aliases,
        compiler_params=params(),
        cost_estimate=cost(1),
        name="residuals",
    )(*args)


def gradient_part(n, features, residual, start, rows):
    at = slice(start, start + rows) if isinstance(start, int) else pl.ds(pl.multiple_of(start, rows), rows)
    value = None
    for j in range(n):
        term = jnp.dot(residual[j][...], features[j][:, at], preferred_element_type=f32)
        value = term if value is None else value + term
    return value


def first_part_kernel(n, *refs):
    features, residual, master = refs[:n], refs[n : 2 * n], refs[2 * n]
    out = refs[-2]
    rows = min(512, out.shape[0])
    for start in range(0, out.shape[0], rows):
        value = gradient_part(n, features, residual, start, rows).T
        out[start : start + rows, :] = value + master[0, start : start + rows, :]


def first_part(features, residual, master, deps):
    n = len(features)
    owned, k = master.shape[1:]
    return pl.pallas_call(
        functools.partial(first_part_kernel, n),
        in_specs=[IN_VMEM] * (2 * n + 1) + [ANYWHERE] * len(deps),
        out_specs=[IN_VMEM, ANYWHERE],
        out_shape=[jax.ShapeDtypeStruct((owned, k), f32), TOKEN],
        compiler_params=params(),
        cost_estimate=cost(0.3),
        name="first_part",
    )(*features, *residual, master, *deps)


def update_kernel(n, begin, *refs):
    features, residual = refs[:n], refs[n : 2 * n]
    begun, cov, master, first, second = refs[2 * n : 2 * n + 5]
    new_master, new_first, new_second, sent = refs[-4:]
    rows = new_master.shape[1]
    step = pl.program_id(0)
    start = pl.multiple_of((begin + step) * rows, rows)
    at = pl.ds(start, rows)
    gradient = gradient_part(n, features, residual, start, rows).T + begun[at, :]
    conditioned = jnp.dot(gradient.astype(bf16), cov[...], preferred_element_type=f32)
    moved_first = beta_one * first[0, at, :] + (1.0 - beta_one) * conditioned
    moved_second = beta_two * second[0, at, :] + (1.0 - beta_two) * conditioned * conditioned
    correction_one = 1.0 - beta_one**STEP
    correction_two = 1.0 - beta_two**STEP
    moved = master[0, at, :] - (learn_rate / correction_one) * moved_first / (
        jnp.sqrt(moved_second * (1.0 / correction_two)) + 1e-08
    )
    new_first[0] = moved_first
    new_second[0] = moved_second
    new_master[0] = moved
    sent[pl.ds(pl.multiple_of(step * rows, rows), rows), :] = moved.astype(bf16)


def update(features, residual, begun, cov, master, first, second, at, steps, before, deps):
    n = len(features)
    owned, k = master.shape[1:]
    rows = min(256, owned)
    state = pl.BlockSpec((1, rows, k), lambda i: (0, at + i, 0))
    args = [*features, *residual, begun, cov, master, first, second]
    specs = [IN_VMEM] * (2 * n + 5)
    aliases = {}
    if before is not None:
        aliases = {len(args) + j: j for j in range(3)}
        args += list(before)
        specs += [ANYWHERE] * 3
    args += deps
    specs += [ANYWHERE] * len(deps)
    return pl.pallas_call(
        functools.partial(update_kernel, n, at),
        grid=(steps,),
        in_specs=specs,
        out_specs=[state, state, state, IN_VMEM],
        out_shape=[jax.ShapeDtypeStruct(master.shape, f32)] * 3
        + [jax.ShapeDtypeStruct((steps * rows, k), bf16)],
        input_output_aliases=aliases,
        compiler_params=params(),
        cost_estimate=cost(4),
        name="update",
    )(*args)


def put_kernel(blocks, owned, n_pts, p, *refs):
    n = len(blocks)
    pieces, out, sems = refs[:n], refs[-2], refs[-1]
    me = p[0]
    copies = []
    for j, (distance, other, start) in enumerate(blocks):
        rows = pieces[j].shape[0]
        home = lax.rem(me + n_pts - distance * CORES, n_pts)
        home = home + other * (1 - 2 * lax.rem(home, 2))
        at = pl.ds(pl.multiple_of(home * owned + start, rows), rows)
        copies.append(pltpu.make_async_copy(pieces[j], out.at[at, :], sems.at[j]))
    for copy in copies:
        copy.start()
    for copy in copies:
        copy.wait()


def put(p, pieces, blocks, owned, n_pts, before):
    n = len(pieces)
    k = pieces[0].shape[1]
    return pl.pallas_call(
        functools.partial(put_kernel, blocks, owned, n_pts),
        grid_spec=pltpu.PrefetchScalarGridSpec(
            num_scalar_prefetch=1,
            grid=(1,),
            in_specs=[IN_VMEM] * n + [ANYWHERE] * (before is not None),
            out_specs=ANYWHERE,
            scratch_shapes=[pltpu.SemaphoreType.DMA((n,))],
        ),
        out_shape=jax.ShapeDtypeStruct((owned * n_pts, k), bf16),
        input_output_aliases={} if before is None else {n + 1: 0},
        compiler_params=params(),
        cost_estimate=cost(0.01),
        name="put_rows",
    )(p, *pieces, *([] if before is None else [before]))


def ring(x, axis, n, distance):
    return lax.ppermute(x, axis, [(i, (i + distance) % n) for i in range(n)])


def mate(x, n):
    return lax.ppermute(x, "pts", [(i, i ^ 1) for i in range(n)])


def across(x, n, distance):
    return ring(x, "pts", n, distance * CORES)


def swap(x, n, bit):
    return lax.ppermute(x, "feat", [(i, i ^ 2**bit) for i in range(n)])


def spread(x, n):
    got = [x if d == 0 else across(x, n, d) for d in range(n // CORES)]
    return [y for g in got for y in (g, mate(g, n))]


def body(n_feat, n_pts, points, picks, omega, phase, weights, counts, master, first, second, cov):
    f = lax.axis_index("feat").astype(jnp.int32).reshape(1)
    p = lax.axis_index("pts").astype(jnp.int32).reshape(1)
    owned, k = master.shape[1:]
    points_here = 2 * picks.shape[1]
    size_one = points_here * 3 // 8
    parts = [(0, points_here - size_one), (points_here - size_one, size_one)]
    bits = n_feat.bit_length() - 1
    points, picks, phase = in_hbm(points), in_hbm(picks), phase[None, :]
    outer = counts.shape
    counts = counts.reshape(points_here, k)

    chosen, token = gather(picks, points)
    everyone = spread(chosen, n_pts)

    def some_rates(m, blocks, before, keep, ends, token):
        return rates(
            f, p, chosen, omega, phase, weights, *parts[m], owned, blocks, before, keep, ends, [token]
        )

    def add_up(kept, got, bit, token):
        last = bit == bits - 1
        *out, token = total(f, kept, got, bit, not last, [token])
        kept, sent = (out[0], out[0]) if last else out
        return kept, swap(sent, n_feat, bit), token

    def give_back(chunk):
        rows, masks = [chunk], [0]
        for bit in reversed(range(bits - 1)):
            rows = rows + [swap(r, n_feat, bit) for r in rows]
            masks = masks + [q ^ 2**bit for q in masks]
        return rows, masks

    feats_zero, own_omega, own_phase, kept_zero, sent, token = some_rates(
        0, (0, 2), None, True, True, token
    )
    got_zero = swap(sent, n_feat, 0)
    feats_one, begun, token = some_rates(1, (0, 1), None, False, False, token)
    for bit in range(1, bits):
        kept_zero, got_zero, token = add_up(kept_zero, got_zero, bit, token)
    kept_one, sent, token = some_rates(1, (1, 2), begun, False, True, token)
    got_one = swap(sent, n_feat, 0)
    features = [[feats_zero], [feats_one]]

    todo = [(m, j) for m in range(2) for j in range(1, n_pts)]
    share = len(todo) // 6

    def some(token, pieces, weight=1.0):
        for _ in range(pieces * share):
            m, j = todo.pop(0)
            feats, token = owned_features(
                everyone[j], own_omega, own_phase, *parts[m], weight, [token]
            )
            features[m].append(feats)
        return token

    token = some(token, 1)
    for bit in range(1, bits):
        kept_one, got_one, token = add_up(kept_one, got_one, bit, token)
    chunk, token = total(f, kept_zero, got_zero, 0, False, [token])
    rows_zero, masks = give_back(chunk)
    token = some(token, 1)
    chunk, token = total(f, kept_one, got_one, 0, False, [token])
    rows_one, masks = give_back(chunk)
    out_rates, res_zero, token = residuals(f, rows_zero, masks, counts, *parts[0], None, [token])
    far_zero = [across(res_zero, n_pts, d) for d in range(1, n_pts // CORES)]
    token = some(token, 1)
    out_rates, res_one, token = residuals(
        f, rows_one, masks, counts, *parts[1], out_rates, [token]
    )
    far_one = [across(res_one, n_pts, d) for d in range(1, n_pts // CORES)]
    token = some(token, 2, 0.1)
    *far_zero, token = lax.optimization_barrier((*far_zero, token))
    res_zero = [y for g in [res_zero] + far_zero for y in (g, mate(g, n_pts))]
    token = some(token, 1, 0.1)
    *far_one, token = lax.optimization_barrier((*far_one, token))
    res_one = [y for g in [res_one] + far_one for y in (g, mate(g, n_pts))]
    begun, token = first_part(features[0], res_zero, master, [token])

    steps = max(1, owned // 256)
    sizes = [1, 2, 2, 3] if steps == 8 else [1] * steps
    chips = n_pts // CORES
    state = None
    at = 0
    sent, come, starts = [], [], []
    for c, size in enumerate(sizes):
        *state, rows = update(
            features[1], res_one, begun, cov, master, first, second, at, size, state, [token] + (come[c - 2] if c > 1 else [])
        )
        sent.append([rows, mate(rows, n_pts)])
        come.append([across(rows, n_pts, d) for d in range(1, chips)])
        starts.append(at * (owned // steps))
        at += size
    working = None
    for group in [range(len(sizes) - 1), [len(sizes) - 1]]:
        pieces, blocks = [], []
        for c in group:
            got = come[c]
            if c and got:
                fence = sent[-1][0] if working is None else working
                *got, fence = lax.optimization_barrier((*got, fence))
                working = None if working is None else fence
            pieces += sent[c] + got + [mate(y, n_pts) for y in got]
            blocks += [(0, other, starts[c]) for other in (0, 1)]
            blocks += [(d, other, starts[c]) for other in (0, 1) for d in range(1, chips)]
        if pieces:
            working = put(p, pieces, blocks, owned, n_pts, working)
    return out_rates.reshape(outer), *state, working


def solution(mesh):
    placed = (
        P(("groups", "pts"), None),
        P(None, ("groups", "pts")),
        P(None, "feat"),
        P("feat"),
        P(("groups", "feat"), None),
        P(None, ("groups", "pts"), None),
        P(("groups", "feat"), "pts", None),
        P(("groups", "feat"), "pts", None),
        P(("groups", "feat"), "pts", None),
        P(),
    )
    return jax.shard_map(
        functools.partial(body, mesh.shape["feat"], mesh.shape["pts"]),
        mesh=mesh,
        in_specs=placed,
        out_specs=(
            P(None, ("groups", "pts"), None),
            P(("groups", "feat"), "pts", None),
            P(("groups", "feat"), "pts", None),
            P(("groups", "feat"), "pts", None),
            P(("groups", "feat"), None),
        ),
        check_vma=False,
    )
```

```python
import functools
import math

import jax
import jax.numpy as jnp
from jax import lax
from jax.experimental import pallas as pl
from jax.experimental.pallas import tpu as pltpu
from jax.sharding import PartitionSpec as P

F = 32768
STEP = 20
CORES = 2

beta_one = 0.9
beta_two = 0.999
learn_rate = 0.2

SINE = tuple(
    c * math.sqrt(2.0 / F) for c in (6.2825055774072665, -41.16644056159234, 74.4523919857074)
)
ROUNDER = 12582912.0
TURN = 1.0 / (2.0 * math.pi)
VMEM = 24 * 1024 * 1024

f32 = jnp.float32
bf16 = jnp.bfloat16
IN_VMEM = pl.BlockSpec(memory_space=pltpu.VMEM)
ANYWHERE = pl.BlockSpec(memory_space=pl.ANY)
TOKEN = jax.ShapeDtypeStruct((8, 128), f32)


def scaled_cos(product, phase_turns):
    turns = product * TURN + phase_turns
    v = 0.25 - jnp.abs(turns - ((turns + ROUNDER) - ROUNDER))
    s = v * v
    return (((SINE[2] * s + SINE[1]) * s + SINE[0]) * v).astype(bf16)


def cost(microseconds):
    return pl.CostEstimate(
        flops=int(microseconds * 1.0e9), bytes_accessed=1 << 10, transcendentals=0
    )


def params():
    return pltpu.CompilerParams(vmem_limit_bytes=VMEM)


def in_hbm(x):
    return pltpu.with_memory_space_constraint(x, pltpu.HBM)


def gather_kernel(picks, points, omega, chosen, omega_here, token, sems):
    batch, pool = picks.shape[1], points.shape[0]
    rows = omega.shape[0] // sems.shape[0]
    copies = [
        pltpu.make_async_copy(omega.at[at, :], omega_here.at[at, :], sems.at[j])
        for j, at in enumerate(pl.ds(j * rows, rows) for j in range(sems.shape[0]))
    ]
    for copy in copies:
        copy.start()
    lane = lax.broadcasted_iota(jnp.int32, (batch, 128), 1)
    for m in range(2):
        wanted = jnp.broadcast_to(picks[m : m + 1, :], (128, batch)).T
        hot = [
            jnp.where(wanted == lane + 128 * j, 1.0, 0.0).astype(bf16) for j in range(pool // 128)
        ]
        chosen[m * batch : (m + 1) * batch, :] = jnp.dot(
            jnp.concatenate(hot, axis=1), points[...], preferred_element_type=f32
        ).astype(bf16)
    for copy in copies:
        copy.wait()


def gather(picks, points, omega):
    batch = picks.shape[1]
    pool, ins = points.shape
    return pl.pallas_call(
        gather_kernel,
        grid=(1,),
        in_specs=[
            pl.BlockSpec(picks.shape, lambda i: (0, 0)),
            pl.BlockSpec((pool, ins), lambda i: (0, 0)),
            ANYWHERE,
        ],
        out_specs=[IN_VMEM, IN_VMEM, ANYWHERE],
        out_shape=[
            jax.ShapeDtypeStruct((2 * batch, ins), bf16),
            jax.ShapeDtypeStruct(omega.shape, bf16),
            TOKEN,
        ],
        scratch_shapes=[pltpu.SemaphoreType.DMA((4,))],
        compiler_params=params(),
        cost_estimate=cost(3),
        name="chosen_points",
    )(picks, points, omega)


def cosines(chosen, omega, phase, base, width, store, between=None):
    tile = min(256, width)
    count = width // tile
    group = min(512, width)

    def part(start, size):
        if isinstance(base, int):
            return slice(base + start, base + start + size)
        return pl.ds(pl.multiple_of(base + start, tile), size)

    def product(c):
        return jnp.dot(chosen, omega[:, part(c * tile, tile)], preferred_element_type=f32)

    ready = product(0)
    for c in range(count):
        coming = product(c + 1) if c + 1 < count else None
        if between is not None and c > 0 and c * tile % group == 0:
            between(c * tile - group, part(c * tile - group, group), group)
        turns = phase[:, part(c * tile, tile)] * TURN
        store(slice(c * tile, (c + 1) * tile), scaled_cos(ready, turns))
        ready = coming
    if between is not None:
        between(width - group, part(width - group, group), group)


def rates_kernel(start, size, low, high, width, own, begun, keep, ends, f, p, chosen, omega, phase, weights, *refs):
    refs = list(refs)
    sems = refs.pop() if keep else None
    total, feats = refs.pop(), refs.pop()
    before = refs.pop(0) if begun else None
    refs.pop()
    owned = None if begun else refs.pop(0)
    count = omega.shape[1] // width
    if keep:
        weights_far, weights = weights, refs[2]

        def coming(step):
            at = pl.ds(pl.multiple_of(lax.rem(step + p[0] * own, count) * width, width), width)
            return pltpu.make_async_copy(weights_far.at[at, :], weights.at[at, :], sems.at[step])

        for step in range(count):
            coming(step).start()
    total[...] = before[...] if begun else jnp.zeros_like(total)

    def block(place, into, offset, step):
        parts = []

        def store(cols, value):
            into[:, offset + cols.start : offset + cols.stop] = value

        def between(at, rows, group):
            if keep and at == 0:
                coming(step).wait()
            done = into[:, offset + at : offset + at + group]
            parts.append(jnp.dot(done, weights[rows, :], preferred_element_type=f32))

        cosines(
            chosen[start : start + size, :], omega, phase, place * width, width, store, between
        )
        part = parts[0]
        for q in parts[1:]:
            part = part + q
        total[...] += part

    if not begun:
        for step in range(own):
            block(p[0] * own + step, owned, step * width, step)

    def turn(step, _):
        block(lax.rem(step + p[0] * own, count), feats, 0, step)
        return _

    lax.fori_loop(low if begun else own, high, turn, 0)
    if keep:
        at = pl.ds(pl.multiple_of(p[0] * own * width, width), own * width)
        refs[0][...] = omega[:, at]
        refs[1][...] = phase[:, at]
    if ends:
        split(total, f[0], 0, *refs[-2:])
    else:
        refs[-1][...] = total[...]


def split(value, f, bit, kept, sent):
    rows = kept.shape[0]
    side = lax.rem(f // 2**bit, 2)
    kept[...] = value[pl.ds(pl.multiple_of(side * rows, rows), rows), :]
    sent[...] = value[pl.ds(pl.multiple_of((1 - side) * rows, rows), rows), :].astype(bf16)


def rates(f, p, chosen, omega, phase, weights, start, size, owned, blocks, before, keep, ends, deps):
    ins, feat_dev = omega.shape
    k = weights.shape[1]
    width = min(2048, owned)
    count = feat_dev // width
    own = owned // width
    low, high = blocks[0] * count // 2, blocks[1] * count // 2

    begun = before is not None
    outs = []
    if not begun:
        outs.append(jax.ShapeDtypeStruct((size, owned), bf16))
    if keep:
        outs += [jax.ShapeDtypeStruct((ins, owned), bf16), jax.ShapeDtypeStruct((1, owned), f32)]
        outs.append(jax.ShapeDtypeStruct(weights.shape, bf16))
    if ends:
        outs += [jax.ShapeDtypeStruct((size // 2, k), t) for t in (f32, bf16)]
    else:
        outs.append(jax.ShapeDtypeStruct((size, k), f32))
    args = [f, p, chosen, omega, phase, weights] + ([before] if begun else []) + deps

    def kernel(*refs):
        inputs = len(args) - len(deps)
        rates_kernel(
            start, size, low, high, width, own, begun, keep, ends, *refs[:inputs], *refs[inputs + len(deps) :]
        )

    return pl.pallas_call(
        kernel,
        grid_spec=pltpu.PrefetchScalarGridSpec(
            num_scalar_prefetch=2,
            grid=(1,),
            in_specs=[IN_VMEM] * 3 + [ANYWHERE if keep else IN_VMEM] + [IN_VMEM] * begun + [ANYWHERE] * len(deps),
            out_specs=[IN_VMEM] * len(outs) + [ANYWHERE],
            scratch_shapes=[pltpu.VMEM((size, width), bf16), pltpu.VMEM((size, k), f32)]
            + [pltpu.SemaphoreType.DMA((count,))] * keep,
        ),
        out_shape=[*outs, TOKEN],
        compiler_params=params(),
        cost_estimate=cost(12 * (high - low) / count),
        name="partial_log_rates",
    )(*args)


def features_kernel(start, size, chosen, omega, phase, *refs):
    out = refs[-2]

    def store(cols, value):
        out[:, cols] = value

    cosines(chosen[start : start + size, :], omega, phase, 0, omega.shape[1], store)


def owned_features(chosen, omega, phase, start, size, weight, deps):
    owned = omega.shape[1]
    return pl.pallas_call(
        functools.partial(features_kernel, start, size),
        in_specs=[IN_VMEM] * 3 + [ANYWHERE] * len(deps),
        out_specs=[IN_VMEM, ANYWHERE],
        out_shape=[jax.ShapeDtypeStruct((size, owned), bf16), TOKEN],
        compiler_params=params(),
        cost_estimate=cost(weight),
        name="owned_features",
    )(chosen, omega, phase, *deps)


def total_kernel(bit, halves, f, a, b, *refs):
    value = a[...].astype(f32) + b[...].astype(f32)
    if halves:
        kept, sent, token, held = refs[-4:]
        held[...] = value
        split(held, f[0], bit, kept, sent)
    else:
        out, token = refs[-2:]
        out[...] = value.astype(bf16)


def total(f, a, b, bit, halves, deps):
    rows, k = a.shape
    if halves:
        outs = [
            jax.ShapeDtypeStruct((rows // 2, k), f32),
            jax.ShapeDtypeStruct((rows // 2, k), bf16),
        ]
    else:
        outs = [jax.ShapeDtypeStruct((rows, k), bf16)]
    return pl.pallas_call(
        functools.partial(total_kernel, bit, halves),
        grid_spec=pltpu.PrefetchScalarGridSpec(
            num_scalar_prefetch=1,
            grid=(1,),
            in_specs=[IN_VMEM] * 2 + [ANYWHERE] * len(deps),
            out_specs=[IN_VMEM] * len(outs) + [ANYWHERE],
            scratch_shapes=[pltpu.VMEM((rows, k), f32)] if halves else [],
        ),
        out_shape=[*outs, TOKEN],
        compiler_params=params(),
        cost_estimate=cost(0.5),
        name="total_rates",
    )(f, a, b, *deps)


def residual_kernel(masks, start, f, *refs):
    chunks, observed = refs[: len(masks)], refs[len(masks)]
    rate_out, residual_out, token, rates, held, sem = refs[-6:]
    size = held.shape[0]
    for j, mask in enumerate(masks):
        rows = chunks[j].shape[0]
        first, bit = 0, 0
        while size >> (bit + 1) >= rows:
            side = lax.rem(f[0] // 2**bit, 2)
            side = 1 - side if mask >> bit & 1 else side
            first = first + side * (size >> (bit + 1))
            bit += 1
        at = pl.ds(pl.multiple_of(first, rows), rows) if bit else slice(None)
        rates[at, :] = chunks[j][...].astype(f32)
    copy = pltpu.make_async_copy(rates, rate_out.at[pl.ds(start, size), :], sem)
    copy.start()
    held[...] = jnp.exp(rates[...]) - observed[start : start + size, :].astype(f32)
    residual_out[...] = held[...].T.astype(bf16)
    copy.wait()


def residuals(f, chunks, masks, counts, start, size, before, deps):
    n = len(chunks)
    k = counts.shape[1]
    args = [f, *chunks, counts, *deps]
    specs = [IN_VMEM] * (n + 1) + [ANYWHERE] * len(deps)
    aliases = {}
    if before is not None:
        aliases = {len(args): 0}
        args.append(before)
        specs.append(ANYWHERE)
    return pl.pallas_call(
        functools.partial(residual_kernel, masks, start),
        grid_spec=pltpu.PrefetchScalarGridSpec(
            num_scalar_prefetch=1,
            grid=(1,),
            in_specs=specs,
            out_specs=[ANYWHERE, IN_VMEM, ANYWHERE],
            scratch_shapes=[pltpu.VMEM((size, k), f32)] * 2 + [pltpu.SemaphoreType.DMA],
        ),
        out_shape=[
            jax.ShapeDtypeStruct(counts.shape, f32),
            jax.ShapeDtypeStruct((k, size), bf16),
            TOKEN,
        ],
        input_output_aliases=aliases,
        compiler_params=params(),
        cost_estimate=cost(1),
        name="residuals",
    )(*args)


def gradient_part(n, features, residual, start, rows):
    at = slice(start, start + rows) if isinstance(start, int) else pl.ds(pl.multiple_of(start, rows), rows)
    value = None
    for j in range(n):
        term = jnp.dot(residual[j][...], features[j][:, at], preferred_element_type=f32)
        value = term if value is None else value + term
    return value


def first_part_kernel(n, *refs):
    features, residual, master = refs[:n], refs[n : 2 * n], refs[2 * n]
    out = refs[-2]
    rows = min(512, out.shape[0])
    for start in range(0, out.shape[0], rows):
        value = gradient_part(n, features, residual, start, rows).T
        out[start : start + rows, :] = value + master[0, start : start + rows, :]


def first_part(features, residual, master, deps):
    n = len(features)
    owned, k = master.shape[1:]
    return pl.pallas_call(
        functools.partial(first_part_kernel, n),
        in_specs=[IN_VMEM] * (2 * n + 1) + [ANYWHERE] * len(deps),
        out_specs=[IN_VMEM, ANYWHERE],
        out_shape=[jax.ShapeDtypeStruct((owned, k), f32), TOKEN],
        compiler_params=params(),
        cost_estimate=cost(0.3),
        name="first_part",
    )(*features, *residual, master, *deps)


def update_kernel(n, begin, *refs):
    features, residual = refs[:n], refs[n : 2 * n]
    begun, cov, master, first, second = refs[2 * n : 2 * n + 5]
    new_master, new_first, new_second, sent = refs[-4:]
    rows = new_master.shape[1]
    step = pl.program_id(0)
    start = pl.multiple_of((begin + step) * rows, rows)
    at = pl.ds(start, rows)
    gradient = gradient_part(n, features, residual, start, rows).T + begun[at, :]
    conditioned = jnp.dot(gradient.astype(bf16), cov[...], preferred_element_type=f32)
    moved_first = beta_one * first[0, at, :] + (1.0 - beta_one) * conditioned
    moved_second = beta_two * second[0, at, :] + (1.0 - beta_two) * conditioned * conditioned
    correction_one = 1.0 - beta_one**STEP
    correction_two = 1.0 - beta_two**STEP
    moved = master[0, at, :] - (learn_rate / correction_one) * moved_first / (
        jnp.sqrt(moved_second * (1.0 / correction_two)) + 1e-08
    )
    new_first[0] = moved_first
    new_second[0] = moved_second
    new_master[0] = moved
    sent[pl.ds(pl.multiple_of(step * rows, rows), rows), :] = moved.astype(bf16)


def update(features, residual, begun, cov, master, first, second, at, steps, before, deps):
    n = len(features)
    owned, k = master.shape[1:]
    rows = min(256, owned)
    state = pl.BlockSpec((1, rows, k), lambda i: (0, at + i, 0))
    args = [*features, *residual, begun, cov, master, first, second]
    specs = [IN_VMEM] * (2 * n + 5)
    aliases = {}
    if before is not None:
        aliases = {len(args) + j: j for j in range(3)}
        args += list(before)
        specs += [ANYWHERE] * 3
    args += deps
    specs += [ANYWHERE] * len(deps)
    return pl.pallas_call(
        functools.partial(update_kernel, n, at),
        grid=(steps,),
        in_specs=specs,
        out_specs=[state, state, state, IN_VMEM],
        out_shape=[jax.ShapeDtypeStruct(master.shape, f32)] * 3
        + [jax.ShapeDtypeStruct((steps * rows, k), bf16)],
        input_output_aliases=aliases,
        compiler_params=params(),
        cost_estimate=cost(4),
        name="update",
    )(*args)


def put_kernel(blocks, owned, n_pts, p, *refs):
    n = len(blocks)
    pieces, out, sems = refs[:n], refs[-2], refs[-1]
    me = p[0]
    copies = []
    for j, (distance, other, start) in enumerate(blocks):
        rows = pieces[j].shape[0]
        home = lax.rem(me + n_pts - distance * CORES, n_pts)
        home = home + other * (1 - 2 * lax.rem(home, 2))
        at = pl.ds(pl.multiple_of(home * owned + start, rows), rows)
        copies.append(pltpu.make_async_copy(pieces[j], out.at[at, :], sems.at[j]))
    for copy in copies:
        copy.start()
    for copy in copies:
        copy.wait()


def put(p, pieces, blocks, owned, n_pts, before):
    n = len(pieces)
    k = pieces[0].shape[1]
    return pl.pallas_call(
        functools.partial(put_kernel, blocks, owned, n_pts),
        grid_spec=pltpu.PrefetchScalarGridSpec(
            num_scalar_prefetch=1,
            grid=(1,),
            in_specs=[IN_VMEM] * n + [ANYWHERE] * (before is not None),
            out_specs=ANYWHERE,
            scratch_shapes=[pltpu.SemaphoreType.DMA((n,))],
        ),
        out_shape=jax.ShapeDtypeStruct((owned * n_pts, k), bf16),
        input_output_aliases={} if before is None else {n + 1: 0},
        compiler_params=params(),
        cost_estimate=cost(0.01),
        name="put_rows",
    )(p, *pieces, *([] if before is None else [before]))


def ring(x, axis, n, distance):
    return lax.ppermute(x, axis, [(i, (i + distance) % n) for i in range(n)])


def mate(x, n):
    return lax.ppermute(x, "pts", [(i, i ^ 1) for i in range(n)])


def across(x, n, distance):
    return ring(x, "pts", n, distance * CORES)


def swap(x, n, bit):
    return lax.ppermute(x, "feat", [(i, i ^ 2**bit) for i in range(n)])


def spread(x, n):
    got = [x if d == 0 else across(x, n, d) for d in range(n // CORES)]
    return [y for g in got for y in (g, mate(g, n))]


def body(n_feat, n_pts, points, picks, omega, phase, weights, counts, master, first, second, cov):
    f = lax.axis_index("feat").astype(jnp.int32).reshape(1)
    p = lax.axis_index("pts").astype(jnp.int32).reshape(1)
    owned, k = master.shape[1:]
    points_here = 2 * picks.shape[1]
    size_one = points_here // 2
    parts = [(0, points_here - size_one), (points_here - size_one, size_one)]
    bits = n_feat.bit_length() - 1
    points, picks, omega, weights = map(in_hbm, (points, picks, omega, weights))
    phase = phase[None, :]
    outer = counts.shape
    counts = counts.reshape(points_here, k)

    chosen, omega, token = gather(picks, points, omega)
    everyone = spread(chosen, n_pts)

    def some_rates(m, blocks, before, keep, ends, token):
        return rates(
            f, p, chosen, omega, phase, weights, *parts[m], owned, blocks, before, keep, ends, [token]
        )

    def add_up(kept, got, bit, token):
        last = bit == bits - 1
        *out, token = total(f, kept, got, bit, not last, [token])
        kept, sent = (out[0], out[0]) if last else out
        return kept, swap(sent, n_feat, bit), token

    def give_back(chunk):
        rows, masks = [chunk], [0]
        for bit in reversed(range(bits - 1)):
            rows = rows + [swap(r, n_feat, bit) for r in rows]
            masks = masks + [q ^ 2**bit for q in masks]
        return rows, masks

    feats_zero, own_omega, own_phase, weights, kept_zero, sent, token = some_rates(
        0, (0, 2), None, True, True, token
    )
    got_zero = swap(sent, n_feat, 0)
    feats_one, begun, token = some_rates(1, (0, 1), None, False, False, token)
    features = [[feats_zero], [feats_one]]
    todo = [(m, j) for m in range(2) for j in range(1, n_pts)]
    share = len(todo) // 6

    def some(token, pieces, weight=1.0):
        for _ in range(pieces * share):
            m, j = todo.pop(0)
            feats, token = owned_features(
                everyone[j], own_omega, own_phase, *parts[m], weight, [token]
            )
            features[m].append(feats)
        return token

    for bit in range(1, bits):
        kept_zero, got_zero, token = add_up(kept_zero, got_zero, bit, token)
    token = some(token, 1)
    kept_one, sent, token = some_rates(1, (1, 2), begun, False, True, token)
    got_one = swap(sent, n_feat, 0)
    chunk, token = total(f, kept_zero, got_zero, 0, False, [token])
    rows_zero, masks = give_back(chunk)
    token = some(token, 1)
    for bit in range(1, bits):
        kept_one, got_one, token = add_up(kept_one, got_one, bit, token)
    token = some(token, 1)
    chunk, token = total(f, kept_one, got_one, 0, False, [token])
    rows_one, masks = give_back(chunk)
    out_rates, res_zero, token = residuals(f, rows_zero, masks, counts, *parts[0], None, [token])
    far_zero = [across(res_zero, n_pts, d) for d in range(1, n_pts // CORES)]
    token = some(token, 1)
    out_rates, res_one, token = residuals(
        f, rows_one, masks, counts, *parts[1], out_rates, [token]
    )
    far_one = [across(res_one, n_pts, d) for d in range(1, n_pts // CORES)]
    token = some(token, 2, 0.1)
    *far_zero, token = lax.optimization_barrier((*far_zero, token))
    res_zero = [y for g in [res_zero] + far_zero for y in (g, mate(g, n_pts))]
    *far_one, token = lax.optimization_barrier((*far_one, token))
    res_one = [y for g in [res_one] + far_one for y in (g, mate(g, n_pts))]
    begun, token = first_part(features[0], res_zero, master, [token])

    steps = max(1, owned // 256)
    sizes = [1, 2, 2, 3] if steps == 8 else [1] * steps
    chips = n_pts // CORES
    state = None
    at = 0
    sent, come, starts = [], [], []
    for c, size in enumerate(sizes):
        *state, rows = update(
            features[1], res_one, begun, cov, master, first, second, at, size, state, [token] + (come[c - 2] if c > 1 else [])
        )
        sent.append([rows, mate(rows, n_pts)])
        come.append([across(rows, n_pts, d) for d in range(1, chips)])
        starts.append(at * (owned // steps))
        at += size
    working = None
    for group in [range(len(sizes) - 1), [len(sizes) - 1]]:
        pieces, blocks = [], []
        for c in group:
            got = come[c]
            if c and got:
                fence = sent[-1][0] if working is None else working
                *got, fence = lax.optimization_barrier((*got, fence))
                working = None if working is None else fence
            pieces += sent[c] + got + [mate(y, n_pts) for y in got]
            blocks += [(0, other, starts[c]) for other in (0, 1)]
            blocks += [(d, other, starts[c]) for other in (0, 1) for d in range(1, chips)]
        if pieces:
            working = put(p, pieces, blocks, owned, n_pts, working)
    return out_rates.reshape(outer), *state, working


def solution(mesh):
    placed = (
        P(("groups", "pts"), None),
        P(None, ("groups", "pts")),
        P(None, "feat"),
        P("feat"),
        P(("groups", "feat"), None),
        P(None, ("groups", "pts"), None),
        P(("groups", "feat"), "pts", None),
        P(("groups", "feat"), "pts", None),
        P(("groups", "feat"), "pts", None),
        P(),
    )
    return jax.shard_map(
        functools.partial(body, mesh.shape["feat"], mesh.shape["pts"]),
        mesh=mesh,
        in_specs=placed,
        out_specs=(
            P(None, ("groups", "pts"), None),
            P(("groups", "feat"), "pts", None),
            P(("groups", "feat"), "pts", None),
            P(("groups", "feat"), "pts", None),
            P(("groups", "feat"), None),
        ),
        check_vma=False,
    )
```

```python
import functools
import math

import jax
import jax.numpy as jnp
from jax import lax
from jax.experimental import pallas as pl
from jax.experimental.pallas import tpu as pltpu
from jax.sharding import PartitionSpec as P

F = 32768
STEP = 20
CORES = 2

beta_one = 0.9
beta_two = 0.999
learn_rate = 0.2

SINE = tuple(
    c * math.sqrt(2.0 / F) for c in (6.2825055774072665, -41.16644056159234, 74.4523919857074)
)
ROUNDER = 12582912.0
TURN = 1.0 / (2.0 * math.pi)
VMEM = 24 * 1024 * 1024

f32 = jnp.float32
bf16 = jnp.bfloat16
IN_VMEM = pl.BlockSpec(memory_space=pltpu.VMEM)
ANYWHERE = pl.BlockSpec(memory_space=pl.ANY)
TOKEN = jax.ShapeDtypeStruct((8, 128), f32)


def scaled_cos(product, phase_turns):
    turns = product * TURN + phase_turns
    v = 0.25 - jnp.abs(turns - ((turns + ROUNDER) - ROUNDER))
    s = v * v
    return (((SINE[2] * s + SINE[1]) * s + SINE[0]) * v).astype(bf16)


def cost(microseconds):
    return pl.CostEstimate(
        flops=int(microseconds * 1.0e9), bytes_accessed=1 << 10, transcendentals=0
    )


def params():
    return pltpu.CompilerParams(vmem_limit_bytes=VMEM)


def in_hbm(x):
    return pltpu.with_memory_space_constraint(x, pltpu.HBM)


def gather_kernel(picks, points, chosen, token):
    batch, pool = picks.shape[1], points.shape[0]
    lane = lax.broadcasted_iota(jnp.int32, (batch, 128), 1)
    for m in range(2):
        wanted = jnp.broadcast_to(picks[m : m + 1, :], (128, batch)).T
        hot = [
            jnp.where(wanted == lane + 128 * j, 1.0, 0.0).astype(bf16) for j in range(pool // 128)
        ]
        chosen[m * batch : (m + 1) * batch, :] = jnp.dot(
            jnp.concatenate(hot, axis=1), points[...], preferred_element_type=f32
        ).astype(bf16)


def gather(picks, points):
    batch = picks.shape[1]
    pool, ins = points.shape
    return pl.pallas_call(
        gather_kernel,
        grid=(1,),
        in_specs=[
            pl.BlockSpec(picks.shape, lambda i: (0, 0)),
            pl.BlockSpec((pool, ins), lambda i: (0, 0)),
        ],
        out_specs=[IN_VMEM, ANYWHERE],
        out_shape=[jax.ShapeDtypeStruct((2 * batch, ins), bf16), TOKEN],
        compiler_params=params(),
        cost_estimate=cost(3),
        name="chosen_points",
    )(picks, points)


def cosines(chosen, omega, phase, base, width, store, between=None, ahead=None):
    tile = min(256, width)
    count = width // tile
    group = min(512, width)

    def part(start, size):
        if isinstance(base, int):
            return slice(base + start, base + start + size)
        return pl.ds(pl.multiple_of(base + start, tile), size)

    def product(c):
        if ahead is not None and c * tile % group == 0:
            ahead(c * tile // group)
        return jnp.dot(chosen, omega[:, part(c * tile, tile)], preferred_element_type=f32)

    ready = product(0)
    for c in range(count):
        coming = product(c + 1) if c + 1 < count else None
        if between is not None and c > 0 and c * tile % group == 0:
            between(c * tile - group, part(c * tile - group, group), group)
        turns = phase[:, part(c * tile, tile)] * TURN
        store(slice(c * tile, (c + 1) * tile), scaled_cos(ready, turns))
        ready = coming
    if between is not None:
        between(width - group, part(width - group, group), group)


def rates_kernel(start, size, low, high, width, own, begun, keep, ends, f, p, chosen, omega, phase, weights, *refs):
    refs = list(refs)
    sems = refs.pop() if keep else None
    total, feats = refs.pop(), refs.pop()
    before = refs.pop(0) if begun else None
    refs.pop()
    owned = None if begun else refs.pop(0)
    count = omega.shape[1] // width
    group = min(512, width)
    if keep:
        sources, (omega, weights) = (omega, weights), refs[2:4]

        def coming(step, piece):
            first = lax.rem(step + p[0] * own, count) * width + piece * group
            at = pl.ds(pl.multiple_of(first, group), group)
            n = step * (width // group) + piece
            return (
                pltpu.make_async_copy(sources[0].at[:, at], omega.at[:, at], sems.at[0, n]),
                pltpu.make_async_copy(sources[1].at[at, :], weights.at[at, :], sems.at[1, n]),
            )

        for step in range(count):
            for piece in range(width // group):
                for copy in coming(step, piece):
                    copy.start()
    total[...] = before[...] if begun else jnp.zeros_like(total)

    def block(place, into, offset, step):
        parts = []

        def ahead(piece):
            for copy in coming(step, piece):
                copy.wait()

        def store(cols, value):
            into[:, offset + cols.start : offset + cols.stop] = value

        def between(at, rows, group):
            done = into[:, offset + at : offset + at + group]
            parts.append(jnp.dot(done, weights[rows, :], preferred_element_type=f32))

        cosines(
            chosen[start : start + size, :],
            omega,
            phase,
            place * width,
            width,
            store,
            between,
            ahead if keep else None,
        )
        part = parts[0]
        for q in parts[1:]:
            part = part + q
        total[...] += part

    if not begun:
        for step in range(own):
            block(p[0] * own + step, owned, step * width, step)

    def turn(step, _):
        block(lax.rem(step + p[0] * own, count), feats, 0, step)
        return _

    lax.fori_loop(low if begun else own, high, turn, 0)
    if keep:
        at = pl.ds(pl.multiple_of(p[0] * own * width, width), own * width)
        refs[0][...] = omega[:, at]
        refs[1][...] = phase[:, at]
    if ends:
        split(total, f[0], 0, *refs[-2:])
    else:
        refs[-1][...] = total[...]


def split(value, f, bit, kept, sent):
    rows = kept.shape[0]
    side = lax.rem(f // 2**bit, 2)
    kept[...] = value[pl.ds(pl.multiple_of(side * rows, rows), rows), :]
    sent[...] = value[pl.ds(pl.multiple_of((1 - side) * rows, rows), rows), :].astype(bf16)


def rates(f, p, chosen, omega, phase, weights, start, size, owned, blocks, before, keep, ends, deps):
    ins, feat_dev = omega.shape
    k = weights.shape[1]
    width = min(2048, owned)
    count = feat_dev // width
    own = owned // width
    low, high = blocks[0] * count // 2, blocks[1] * count // 2

    begun = before is not None
    outs = []
    if not begun:
        outs.append(jax.ShapeDtypeStruct((size, owned), bf16))
    if keep:
        outs += [jax.ShapeDtypeStruct((ins, owned), bf16), jax.ShapeDtypeStruct((1, owned), f32)]
        outs += [jax.ShapeDtypeStruct(x.shape, bf16) for x in (omega, weights)]
    if ends:
        outs += [jax.ShapeDtypeStruct((size // 2, k), t) for t in (f32, bf16)]
    else:
        outs.append(jax.ShapeDtypeStruct((size, k), f32))
    args = [f, p, chosen, omega, phase, weights] + ([before] if begun else []) + deps

    def kernel(*refs):
        inputs = len(args) - len(deps)
        rates_kernel(
            start, size, low, high, width, own, begun, keep, ends, *refs[:inputs], *refs[inputs + len(deps) :]
        )

    return pl.pallas_call(
        kernel,
        grid_spec=pltpu.PrefetchScalarGridSpec(
            num_scalar_prefetch=2,
            grid=(1,),
            in_specs=(
                [IN_VMEM, ANYWHERE, IN_VMEM, ANYWHERE] if keep else [IN_VMEM] * (4 + begun)
            )
            + [ANYWHERE] * len(deps),
            out_specs=[IN_VMEM] * len(outs) + [ANYWHERE],
            scratch_shapes=[pltpu.VMEM((size, width), bf16), pltpu.VMEM((size, k), f32)]
            + [pltpu.SemaphoreType.DMA((2, feat_dev // min(512, width)))] * keep,
        ),
        out_shape=[*outs, TOKEN],
        compiler_params=params(),
        cost_estimate=cost(12 * (high - low) / count),
        name="partial_log_rates",
    )(*args)


def features_kernel(start, size, chosen, omega, phase, *refs):
    out = refs[-2]

    def store(cols, value):
        out[:, cols] = value

    cosines(chosen[start : start + size, :], omega, phase, 0, omega.shape[1], store)


def owned_features(chosen, omega, phase, start, size, weight, deps):
    owned = omega.shape[1]
    return pl.pallas_call(
        functools.partial(features_kernel, start, size),
        in_specs=[IN_VMEM] * 3 + [ANYWHERE] * len(deps),
        out_specs=[IN_VMEM, ANYWHERE],
        out_shape=[jax.ShapeDtypeStruct((size, owned), bf16), TOKEN],
        compiler_params=params(),
        cost_estimate=cost(weight),
        name="owned_features",
    )(chosen, omega, phase, *deps)


def total_kernel(bit, halves, f, a, b, *refs):
    value = a[...].astype(f32) + b[...].astype(f32)
    if halves:
        kept, sent, token, held = refs[-4:]
        held[...] = value
        split(held, f[0], bit, kept, sent)
    else:
        out, token = refs[-2:]
        out[...] = value.astype(bf16)


def total(f, a, b, bit, halves, deps):
    rows, k = a.shape
    if halves:
        outs = [
            jax.ShapeDtypeStruct((rows // 2, k), f32),
            jax.ShapeDtypeStruct((rows // 2, k), bf16),
        ]
    else:
        outs = [jax.ShapeDtypeStruct((rows, k), bf16)]
    return pl.pallas_call(
        functools.partial(total_kernel, bit, halves),
        grid_spec=pltpu.PrefetchScalarGridSpec(
            num_scalar_prefetch=1,
            grid=(1,),
            in_specs=[IN_VMEM] * 2 + [ANYWHERE] * len(deps),
            out_specs=[IN_VMEM] * len(outs) + [ANYWHERE],
            scratch_shapes=[pltpu.VMEM((rows, k), f32)] if halves else [],
        ),
        out_shape=[*outs, TOKEN],
        compiler_params=params(),
        cost_estimate=cost(0.5),
        name="total_rates",
    )(f, a, b, *deps)


def residual_kernel(masks, start, f, *refs):
    chunks, observed = refs[: len(masks)], refs[len(masks)]
    rate_out, residual_out, token, rates, held, sem = refs[-6:]
    size = held.shape[0]
    for j, mask in enumerate(masks):
        rows = chunks[j].shape[0]
        first, bit = 0, 0
        while size >> (bit + 1) >= rows:
            side = lax.rem(f[0] // 2**bit, 2)
            side = 1 - side if mask >> bit & 1 else side
            first = first + side * (size >> (bit + 1))
            bit += 1
        at = pl.ds(pl.multiple_of(first, rows), rows) if bit else slice(None)
        rates[at, :] = chunks[j][...].astype(f32)
    copy = pltpu.make_async_copy(rates, rate_out.at[pl.ds(start, size), :], sem)
    copy.start()
    held[...] = jnp.exp(rates[...]) - observed[start : start + size, :].astype(f32)
    residual_out[...] = held[...].T.astype(bf16)
    copy.wait()


def residuals(f, chunks, masks, counts, start, size, before, deps):
    n = len(chunks)
    k = counts.shape[1]
    args = [f, *chunks, counts, *deps]
    specs = [IN_VMEM] * (n + 1) + [ANYWHERE] * len(deps)
    aliases = {}
    if before is not None:
        aliases = {len(args): 0}
        args.append(before)
        specs.append(ANYWHERE)
    return pl.pallas_call(
        functools.partial(residual_kernel, masks, start),
        grid_spec=pltpu.PrefetchScalarGridSpec(
            num_scalar_prefetch=1,
            grid=(1,),
            in_specs=specs,
            out_specs=[ANYWHERE, IN_VMEM, ANYWHERE],
            scratch_shapes=[pltpu.VMEM((size, k), f32)] * 2 + [pltpu.SemaphoreType.DMA],
        ),
        out_shape=[
            jax.ShapeDtypeStruct(counts.shape, f32),
            jax.ShapeDtypeStruct((k, size), bf16),
            TOKEN,
        ],
        input_output_aliases=aliases,
        compiler_params=params(),
        cost_estimate=cost(1),
        name="residuals",
    )(*args)


def gradient_part(n, features, residual, start, rows):
    at = slice(start, start + rows) if isinstance(start, int) else pl.ds(pl.multiple_of(start, rows), rows)
    value = None
    for j in range(n):
        term = jnp.dot(residual[j][...], features[j][:, at], preferred_element_type=f32)
        value = term if value is None else value + term
    return value


def first_part_kernel(n, *refs):
    features, residual, master = refs[:n], refs[n : 2 * n], refs[2 * n]
    out = refs[-2]
    rows = min(512, out.shape[0])
    for start in range(0, out.shape[0], rows):
        value = gradient_part(n, features, residual, start, rows).T
        out[start : start + rows, :] = value + master[0, start : start + rows, :]


def first_part(features, residual, master, deps):
    n = len(features)
    owned, k = master.shape[1:]
    return pl.pallas_call(
        functools.partial(first_part_kernel, n),
        in_specs=[IN_VMEM] * (2 * n + 1) + [ANYWHERE] * len(deps),
        out_specs=[IN_VMEM, ANYWHERE],
        out_shape=[jax.ShapeDtypeStruct((owned, k), f32), TOKEN],
        compiler_params=params(),
        cost_estimate=cost(0.3),
        name="first_part",
    )(*features, *residual, master, *deps)


def update_kernel(n, begin, *refs):
    features, residual = refs[:n], refs[n : 2 * n]
    begun, cov, master, first, second = refs[2 * n : 2 * n + 5]
    new_master, new_first, new_second, sent = refs[-4:]
    rows = new_master.shape[1]
    step = pl.program_id(0)
    start = pl.multiple_of((begin + step) * rows, rows)
    at = pl.ds(start, rows)
    gradient = gradient_part(n, features, residual, start, rows).T + begun[at, :]
    conditioned = jnp.dot(gradient.astype(bf16), cov[...], preferred_element_type=f32)
    moved_first = beta_one * first[0, at, :] + (1.0 - beta_one) * conditioned
    moved_second = beta_two * second[0, at, :] + (1.0 - beta_two) * conditioned * conditioned
    correction_one = 1.0 - beta_one**STEP
    correction_two = 1.0 - beta_two**STEP
    moved = master[0, at, :] - (learn_rate / correction_one) * moved_first / (
        jnp.sqrt(moved_second * (1.0 / correction_two)) + 1e-08
    )
    new_first[0] = moved_first
    new_second[0] = moved_second
    new_master[0] = moved
    sent[pl.ds(pl.multiple_of(step * rows, rows), rows), :] = moved.astype(bf16)


def update(features, residual, begun, cov, master, first, second, at, steps, before, deps):
    n = len(features)
    owned, k = master.shape[1:]
    rows = min(256, owned)
    state = pl.BlockSpec((1, rows, k), lambda i: (0, at + i, 0))
    args = [*features, *residual, begun, cov, master, first, second]
    specs = [IN_VMEM] * (2 * n + 5)
    aliases = {}
    if before is not None:
        aliases = {len(args) + j: j for j in range(3)}
        args += list(before)
        specs += [ANYWHERE] * 3
    args += deps
    specs += [ANYWHERE] * len(deps)
    return pl.pallas_call(
        functools.partial(update_kernel, n, at),
        grid=(steps,),
        in_specs=specs,
        out_specs=[state, state, state, IN_VMEM],
        out_shape=[jax.ShapeDtypeStruct(master.shape, f32)] * 3
        + [jax.ShapeDtypeStruct((steps * rows, k), bf16)],
        input_output_aliases=aliases,
        compiler_params=params(),
        cost_estimate=cost(4),
        name="update",
    )(*args)


def put_kernel(blocks, owned, n_pts, p, *refs):
    n = len(blocks)
    pieces, out, sems = refs[:n], refs[-2], refs[-1]
    me = p[0]
    copies = []
    for j, (distance, other, start) in enumerate(blocks):
        rows = pieces[j].shape[0]
        home = lax.rem(me + n_pts - distance * CORES, n_pts)
        home = home + other * (1 - 2 * lax.rem(home, 2))
        at = pl.ds(pl.multiple_of(home * owned + start, rows), rows)
        copies.append(pltpu.make_async_copy(pieces[j], out.at[at, :], sems.at[j]))
    for copy in copies:
        copy.start()
    for copy in copies:
        copy.wait()


def put(p, pieces, blocks, owned, n_pts, before):
    n = len(pieces)
    k = pieces[0].shape[1]
    return pl.pallas_call(
        functools.partial(put_kernel, blocks, owned, n_pts),
        grid_spec=pltpu.PrefetchScalarGridSpec(
            num_scalar_prefetch=1,
            grid=(1,),
            in_specs=[IN_VMEM] * n + [ANYWHERE] * (before is not None),
            out_specs=ANYWHERE,
            scratch_shapes=[pltpu.SemaphoreType.DMA((n,))],
        ),
        out_shape=jax.ShapeDtypeStruct((owned * n_pts, k), bf16),
        input_output_aliases={} if before is None else {n + 1: 0},
        compiler_params=params(),
        cost_estimate=cost(0.01),
        name="put_rows",
    )(p, *pieces, *([] if before is None else [before]))


def ring(x, axis, n, distance):
    return lax.ppermute(x, axis, [(i, (i + distance) % n) for i in range(n)])


def mate(x, n):
    return lax.ppermute(x, "pts", [(i, i ^ 1) for i in range(n)])


def across(x, n, distance):
    return ring(x, "pts", n, distance * CORES)


def swap(x, n, bit):
    return lax.ppermute(x, "feat", [(i, i ^ 2**bit) for i in range(n)])


def spread(x, n):
    got = [x if d == 0 else across(x, n, d) for d in range(n // CORES)]
    return [y for g in got for y in (g, mate(g, n))]


def body(n_feat, n_pts, points, picks, omega, phase, weights, counts, master, first, second, cov):
    f = lax.axis_index("feat").astype(jnp.int32).reshape(1)
    p = lax.axis_index("pts").astype(jnp.int32).reshape(1)
    owned, k = master.shape[1:]
    points_here = 2 * picks.shape[1]
    size_one = points_here * 3 // 8
    parts = [(0, points_here - size_one), (points_here - size_one, size_one)]
    bits = n_feat.bit_length() - 1
    points, picks, omega, weights = map(in_hbm, (points, picks, omega, weights))
    phase = phase[None, :]
    outer = counts.shape
    counts = counts.reshape(points_here, k)

    chosen, token = gather(picks, points)
    everyone = spread(chosen, n_pts)

    def some_rates(m, blocks, before, keep, ends, token):
        return rates(
            f, p, chosen, omega, phase, weights, *parts[m], owned, blocks, before, keep, ends, [token]
        )

    def add_up(kept, got, bit, token):
        last = bit == bits - 1
        *out, token = total(f, kept, got, bit, not last, [token])
        kept, sent = (out[0], out[0]) if last else out
        return kept, swap(sent, n_feat, bit), token

    def give_back(chunk):
        rows, masks = [chunk], [0]
        for bit in reversed(range(bits - 1)):
            rows = rows + [swap(r, n_feat, bit) for r in rows]
            masks = masks + [q ^ 2**bit for q in masks]
        return rows, masks

    feats_zero, own_omega, own_phase, omega, weights, kept_zero, sent, token = some_rates(
        0, (0, 2), None, True, True, token
    )
    got_zero = swap(sent, n_feat, 0)
    feats_one, begun, token = some_rates(1, (0, 1), None, False, False, token)
    for bit in range(1, bits):
        kept_zero, got_zero, token = add_up(kept_zero, got_zero, bit, token)
    kept_one, sent, token = some_rates(1, (1, 2), begun, False, True, token)
    got_one = swap(sent, n_feat, 0)
    features = [[feats_zero], [feats_one]]

    todo = [(m, j) for m in range(2) for j in range(1, n_pts)]
    share = len(todo) // 6

    def some(token, pieces, weight=1.0):
        for _ in range(pieces * share):
            m, j = todo.pop(0)
            feats, token = owned_features(
                everyone[j], own_omega, own_phase, *parts[m], weight, [token]
            )
            features[m].append(feats)
        return token

    token = some(token, 1)
    for bit in range(1, bits):
        kept_one, got_one, token = add_up(kept_one, got_one, bit, token)
    chunk, token = total(f, kept_zero, got_zero, 0, False, [token])
    rows_zero, masks = give_back(chunk)
    token = some(token, 1)
    chunk, token = total(f, kept_one, got_one, 0, False, [token])
    rows_one, masks = give_back(chunk)
    out_rates, res_zero, token = residuals(f, rows_zero, masks, counts, *parts[0], None, [token])
    far_zero = [across(res_zero, n_pts, d) for d in range(1, n_pts // CORES)]
    token = some(token, 1)
    out_rates, res_one, token = residuals(
        f, rows_one, masks, counts, *parts[1], out_rates, [token]
    )
    far_one = [across(res_one, n_pts, d) for d in range(1, n_pts // CORES)]
    token = some(token, 2, 0.1)
    *far_zero, token = lax.optimization_barrier((*far_zero, token))
    res_zero = [y for g in [res_zero] + far_zero for y in (g, mate(g, n_pts))]
    token = some(token, 1, 0.1)
    *far_one, token = lax.optimization_barrier((*far_one, token))
    res_one = [y for g in [res_one] + far_one for y in (g, mate(g, n_pts))]
    begun, token = first_part(features[0], res_zero, master, [token])

    steps = max(1, owned // 256)
    sizes = [1, 2, 2, 3] if steps == 8 else [1] * steps
    chips = n_pts // CORES
    state = None
    at = 0
    sent, come, starts = [], [], []
    for c, size in enumerate(sizes):
        *state, rows = update(
            features[1], res_one, begun, cov, master, first, second, at, size, state, [token] + (come[c - 2] if c > 1 else [])
        )
        sent.append([rows, mate(rows, n_pts)])
        come.append([across(rows, n_pts, d) for d in range(1, chips)])
        starts.append(at * (owned // steps))
        at += size
    working = None
    for group in [range(len(sizes) - 1), [len(sizes) - 1]]:
        pieces, blocks = [], []
        for c in group:
            got = come[c]
            if c and got:
                fence = sent[-1][0] if working is None else working
                *got, fence = lax.optimization_barrier((*got, fence))
                working = None if working is None else fence
            pieces += sent[c] + got + [mate(y, n_pts) for y in got]
            blocks += [(0, other, starts[c]) for other in (0, 1)]
            blocks += [(d, other, starts[c]) for other in (0, 1) for d in range(1, chips)]
        if pieces:
            working = put(p, pieces, blocks, owned, n_pts, working)
    return out_rates.reshape(outer), *state, working


def solution(mesh):
    placed = (
        P(("groups", "pts"), None),
        P(None, ("groups", "pts")),
        P(None, "feat"),
        P("feat"),
        P(("groups", "feat"), None),
        P(None, ("groups", "pts"), None),
        P(("groups", "feat"), "pts", None),
        P(("groups", "feat"), "pts", None),
        P(("groups", "feat"), "pts", None),
        P(),
    )
    return jax.shard_map(
        functools.partial(body, mesh.shape["feat"], mesh.shape["pts"]),
        mesh=mesh,
        in_specs=placed,
        out_specs=(
            P(None, ("groups", "pts"), None),
            P(("groups", "feat"), "pts", None),
            P(("groups", "feat"), "pts", None),
            P(("groups", "feat"), "pts", None),
            P(("groups", "feat"), None),
        ),
        check_vma=False,
    )
```

```python
import functools
import math

import jax
import jax.numpy as jnp
from jax import lax
from jax.experimental import pallas as pl
from jax.experimental.pallas import tpu as pltpu
from jax.sharding import PartitionSpec as P

F = 32768
STEP = 20
CORES = 2

beta_one = 0.9
beta_two = 0.999
learn_rate = 0.2

SINE = tuple(
    c * math.sqrt(2.0 / F) for c in (6.2825055774072665, -41.16644056159234, 74.4523919857074)
)
ROUNDER = 12582912.0
TURN = 1.0 / (2.0 * math.pi)
VMEM = 24 * 1024 * 1024

f32 = jnp.float32
bf16 = jnp.bfloat16
IN_VMEM = pl.BlockSpec(memory_space=pltpu.VMEM)
ANYWHERE = pl.BlockSpec(memory_space=pl.ANY)
TOKEN = jax.ShapeDtypeStruct((8, 128), f32)


def scaled_cos(product, phase_turns):
    turns = product * TURN + phase_turns
    v = 0.25 - jnp.abs(turns - ((turns + ROUNDER) - ROUNDER))
    s = v * v
    return (((SINE[2] * s + SINE[1]) * s + SINE[0]) * v).astype(bf16)


def cost(microseconds):
    return pl.CostEstimate(
        flops=int(microseconds * 1.0e9), bytes_accessed=1 << 10, transcendentals=0
    )


def params():
    return pltpu.CompilerParams(vmem_limit_bytes=VMEM)


def in_hbm(x):
    return pltpu.with_memory_space_constraint(x, pltpu.HBM)


def gather_kernel(picks, points, chosen, token):
    batch, pool = picks.shape[1], points.shape[0]
    lane = lax.broadcasted_iota(jnp.int32, (batch, 128), 1)
    for m in range(2):
        wanted = jnp.broadcast_to(picks[m : m + 1, :], (128, batch)).T
        hot = [
            jnp.where(wanted == lane + 128 * j, 1.0, 0.0).astype(bf16) for j in range(pool // 128)
        ]
        chosen[m * batch : (m + 1) * batch, :] = jnp.dot(
            jnp.concatenate(hot, axis=1), points[...], preferred_element_type=f32
        ).astype(bf16)


def gather(picks, points):
    batch = picks.shape[1]
    pool, ins = points.shape
    return pl.pallas_call(
        gather_kernel,
        grid=(1,),
        in_specs=[
            pl.BlockSpec(picks.shape, lambda i: (0, 0)),
            pl.BlockSpec((pool, ins), lambda i: (0, 0)),
        ],
        out_specs=[IN_VMEM, ANYWHERE],
        out_shape=[jax.ShapeDtypeStruct((2 * batch, ins), bf16), TOKEN],
        compiler_params=params(),
        cost_estimate=cost(3),
        name="chosen_points",
    )(picks, points)


def cosines(chosen, omega, phase, base, width, store, between=None):
    tile = min(256, width)
    count = width // tile
    group = min(512, width)

    def part(start, size):
        if isinstance(base, int):
            return slice(base + start, base + start + size)
        return pl.ds(pl.multiple_of(base + start, tile), size)

    def product(c):
        return jnp.dot(chosen, omega[:, part(c * tile, tile)], preferred_element_type=f32)

    ready = product(0)
    for c in range(count):
        coming = product(c + 1) if c + 1 < count else None
        if between is not None and c > 0 and c * tile % group == 0:
            between(c * tile - group, part(c * tile - group, group), group)
        turns = phase[:, part(c * tile, tile)] * TURN
        store(slice(c * tile, (c + 1) * tile), scaled_cos(ready, turns))
        ready = coming
    if between is not None:
        between(width - group, part(width - group, group), group)


def rates_kernel(start, size, low, high, width, own, begun, keep, ends, f, p, chosen, omega, phase, weights, *refs):
    refs = list(refs)
    total, feats = refs.pop(), refs.pop()
    before = refs.pop(0) if begun else None
    refs.pop()
    owned = None if begun else refs.pop(0)
    count = omega.shape[1] // width
    total[...] = before[...] if begun else jnp.zeros_like(total)

    def block(place, into, offset):
        parts = []

        def store(cols, value):
            into[:, offset + cols.start : offset + cols.stop] = value

        def between(at, rows, group):
            done = into[:, offset + at : offset + at + group]
            parts.append(jnp.dot(done, weights[rows, :], preferred_element_type=f32))

        cosines(
            chosen[start : start + size, :], omega, phase, place * width, width, store, between
        )
        part = parts[0]
        for q in parts[1:]:
            part = part + q
        total[...] += part

    if not begun:
        for step in range(own):
            block(p[0] * own + step, owned, step * width)

    def turn(step, _):
        block(lax.rem(step + p[0] * own, count), feats, 0)
        return _

    lax.fori_loop(low if begun else own, high, turn, 0)
    if keep:
        at = pl.ds(pl.multiple_of(p[0] * own * width, width), own * width)
        refs[0][...] = omega[:, at]
        refs[1][...] = phase[:, at]
    if ends:
        split(total, f[0], 0, *refs[-2:])
    else:
        refs[-1][...] = total[...]


def split(value, f, bit, kept, sent):
    rows = kept.shape[0]
    side = lax.rem(f // 2**bit, 2)
    kept[...] = value[pl.ds(pl.multiple_of(side * rows, rows), rows), :]
    sent[...] = value[pl.ds(pl.multiple_of((1 - side) * rows, rows), rows), :].astype(bf16)


def rates(f, p, chosen, omega, phase, weights, start, size, owned, blocks, before, keep, ends, deps):
    ins, feat_dev = omega.shape
    k = weights.shape[1]
    width = min(2048, owned)
    count = feat_dev // width
    own = owned // width
    low, high = blocks[0] * count // 2, blocks[1] * count // 2

    begun = before is not None
    outs = []
    if not begun:
        outs.append(jax.ShapeDtypeStruct((size, owned), bf16))
    if keep:
        outs += [jax.ShapeDtypeStruct((ins, owned), bf16), jax.ShapeDtypeStruct((1, owned), f32)]
    if ends:
        outs += [jax.ShapeDtypeStruct((size // 2, k), t) for t in (f32, bf16)]
    else:
        outs.append(jax.ShapeDtypeStruct((size, k), f32))
    args = [f, p, chosen, omega, phase, weights] + ([before] if begun else []) + deps

    def kernel(*refs):
        inputs = len(args) - len(deps)
        rates_kernel(
            start, size, low, high, width, own, begun, keep, ends, *refs[:inputs], *refs[inputs + len(deps) :]
        )

    return pl.pallas_call(
        kernel,
        grid_spec=pltpu.PrefetchScalarGridSpec(
            num_scalar_prefetch=2,
            grid=(1,),
            in_specs=[IN_VMEM] * (4 + begun) + [ANYWHERE] * len(deps),
            out_specs=[IN_VMEM] * len(outs) + [ANYWHERE],
            scratch_shapes=[pltpu.VMEM((size, width), bf16), pltpu.VMEM((size, k), f32)],
        ),
        out_shape=[*outs, TOKEN],
        compiler_params=params(),
        cost_estimate=cost(12 * (high - low) / count),
        name="partial_log_rates",
    )(*args)


def first_rates_kernel(start, size, own, f, p, chosen, omega, phase, weights, *refs):
    owned, own_omega, own_phase, kept, sent, _, feats, total = refs
    step = pl.program_id(0)
    width = omega.shape[1]
    parts = []

    @pl.when(step == 0)
    def _():
        total[...] = jnp.zeros_like(total)

    def store(cols, value):
        feats[:, cols] = value

    def between(at, rows, group):
        done = feats[:, at : at + group]
        parts.append(jnp.dot(done, weights[rows, :], preferred_element_type=f32))

    cosines(chosen[start : start + size, :], omega, phase, 0, width, store, between)
    part = parts[0]
    for q in parts[1:]:
        part = part + q
    total[...] += part

    @pl.when(step < own)
    def _():
        at = pl.ds(pl.multiple_of(step * width, width), width)
        owned[:, at] = feats[...]
        own_omega[:, at] = omega[...]
        own_phase[:, at] = phase[...]

    @pl.when(step == pl.num_programs(0) - 1)
    def _():
        split(total, f[0], 0, kept, sent)


def first_rates(f, p, chosen, omega, phase, weights, start, size, owned, deps):
    ins, feat_dev = omega.shape
    k = weights.shape[1]
    width = min(2048, owned)
    count = feat_dev // width
    own = owned // width

    def turned(i, p):
        return lax.rem(i + p[0] * own, count)

    def kernel(*refs):
        first_rates_kernel(start, size, own, *refs[:6], *refs[6 + len(deps) :])

    return pl.pallas_call(
        kernel,
        grid_spec=pltpu.PrefetchScalarGridSpec(
            num_scalar_prefetch=2,
            grid=(count,),
            in_specs=[
                IN_VMEM,
                pl.BlockSpec((ins, width), lambda i, f, p: (0, turned(i, p))),
                pl.BlockSpec((1, width), lambda i, f, p: (0, turned(i, p))),
                pl.BlockSpec((width, k), lambda i, f, p: (turned(i, p), 0)),
            ]
            + [ANYWHERE] * len(deps),
            out_specs=[IN_VMEM] * 5 + [ANYWHERE],
            scratch_shapes=[pltpu.VMEM((size, width), bf16), pltpu.VMEM((size, k), f32)],
        ),
        out_shape=[
            jax.ShapeDtypeStruct((size, owned), bf16),
            jax.ShapeDtypeStruct((ins, owned), bf16),
            jax.ShapeDtypeStruct((1, owned), f32),
            jax.ShapeDtypeStruct((size // 2, k), f32),
            jax.ShapeDtypeStruct((size // 2, k), bf16),
            TOKEN,
        ],
        compiler_params=params(),
        cost_estimate=cost(12),
        name="first_log_rates",
    )(f, p, chosen, omega, phase, weights, *deps)


def features_kernel(start, size, chosen, omega, phase, *refs):
    out = refs[-2]

    def store(cols, value):
        out[:, cols] = value

    cosines(chosen[start : start + size, :], omega, phase, 0, omega.shape[1], store)


def owned_features(chosen, omega, phase, start, size, weight, deps):
    owned = omega.shape[1]
    return pl.pallas_call(
        functools.partial(features_kernel, start, size),
        in_specs=[IN_VMEM] * 3 + [ANYWHERE] * len(deps),
        out_specs=[IN_VMEM, ANYWHERE],
        out_shape=[jax.ShapeDtypeStruct((size, owned), bf16), TOKEN],
        compiler_params=params(),
        cost_estimate=cost(weight),
        name="owned_features",
    )(chosen, omega, phase, *deps)


def total_kernel(bit, halves, f, a, b, *refs):
    value = a[...].astype(f32) + b[...].astype(f32)
    if halves:
        kept, sent, token, held = refs[-4:]
        held[...] = value
        split(held, f[0], bit, kept, sent)
    else:
        out, token = refs[-2:]
        out[...] = value.astype(bf16)


def total(f, a, b, bit, halves, deps):
    rows, k = a.shape
    if halves:
        outs = [
            jax.ShapeDtypeStruct((rows // 2, k), f32),
            jax.ShapeDtypeStruct((rows // 2, k), bf16),
        ]
    else:
        outs = [jax.ShapeDtypeStruct((rows, k), bf16)]
    return pl.pallas_call(
        functools.partial(total_kernel, bit, halves),
        grid_spec=pltpu.PrefetchScalarGridSpec(
            num_scalar_prefetch=1,
            grid=(1,),
            in_specs=[IN_VMEM] * 2 + [ANYWHERE] * len(deps),
            out_specs=[IN_VMEM] * len(outs) + [ANYWHERE],
            scratch_shapes=[pltpu.VMEM((rows, k), f32)] if halves else [],
        ),
        out_shape=[*outs, TOKEN],
        compiler_params=params(),
        cost_estimate=cost(0.5),
        name="total_rates",
    )(f, a, b, *deps)


def residual_kernel(masks, start, f, *refs):
    chunks, observed = refs[: len(masks)], refs[len(masks)]
    rate_out, residual_out, token, rates, held, sem = refs[-6:]
    size = held.shape[0]
    for j, mask in enumerate(masks):
        rows = chunks[j].shape[0]
        first, bit = 0, 0
        while size >> (bit + 1) >= rows:
            side = lax.rem(f[0] // 2**bit, 2)
            side = 1 - side if mask >> bit & 1 else side
            first = first + side * (size >> (bit + 1))
            bit += 1
        at = pl.ds(pl.multiple_of(first, rows), rows) if bit else slice(None)
        rates[at, :] = chunks[j][...].astype(f32)
    copy = pltpu.make_async_copy(rates, rate_out.at[pl.ds(start, size), :], sem)
    copy.start()
    held[...] = jnp.exp(rates[...]) - observed[start : start + size, :].astype(f32)
    residual_out[...] = held[...].T.astype(bf16)
    copy.wait()


def residuals(f, chunks, masks, counts, start, size, before, deps):
    n = len(chunks)
    k = counts.shape[1]
    args = [f, *chunks, counts, *deps]
    specs = [IN_VMEM] * (n + 1) + [ANYWHERE] * len(deps)
    aliases = {}
    if before is not None:
        aliases = {len(args): 0}
        args.append(before)
        specs.append(ANYWHERE)
    return pl.pallas_call(
        functools.partial(residual_kernel, masks, start),
        grid_spec=pltpu.PrefetchScalarGridSpec(
            num_scalar_prefetch=1,
            grid=(1,),
            in_specs=specs,
            out_specs=[ANYWHERE, IN_VMEM, ANYWHERE],
            scratch_shapes=[pltpu.VMEM((size, k), f32)] * 2 + [pltpu.SemaphoreType.DMA],
        ),
        out_shape=[
            jax.ShapeDtypeStruct(counts.shape, f32),
            jax.ShapeDtypeStruct((k, size), bf16),
            TOKEN,
        ],
        input_output_aliases=aliases,
        compiler_params=params(),
        cost_estimate=cost(1),
        name="residuals",
    )(*args)


def gradient_part(n, features, residual, start, rows):
    at = slice(start, start + rows) if isinstance(start, int) else pl.ds(pl.multiple_of(start, rows), rows)
    value = None
    for j in range(n):
        term = jnp.dot(residual[j][...], features[j][:, at], preferred_element_type=f32)
        value = term if value is None else value + term
    return value


def first_part_kernel(n, *refs):
    features, residual, master = refs[:n], refs[n : 2 * n], refs[2 * n]
    out = refs[-2]
    rows = min(512, out.shape[0])
    for start in range(0, out.shape[0], rows):
        value = gradient_part(n, features, residual, start, rows).T
        out[start : start + rows, :] = value + master[0, start : start + rows, :]


def first_part(features, residual, master, deps):
    n = len(features)
    owned, k = master.shape[1:]
    return pl.pallas_call(
        functools.partial(first_part_kernel, n),
        in_specs=[IN_VMEM] * (2 * n + 1) + [ANYWHERE] * len(deps),
        out_specs=[IN_VMEM, ANYWHERE],
        out_shape=[jax.ShapeDtypeStruct((owned, k), f32), TOKEN],
        compiler_params=params(),
        cost_estimate=cost(0.3),
        name="first_part",
    )(*features, *residual, master, *deps)


def update_kernel(n, begin, *refs):
    features, residual = refs[:n], refs[n : 2 * n]
    begun, cov, master, first, second = refs[2 * n : 2 * n + 5]
    new_master, new_first, new_second, sent = refs[-4:]
    rows = new_master.shape[1]
    step = pl.program_id(0)
    start = pl.multiple_of((begin + step) * rows, rows)
    at = pl.ds(start, rows)
    gradient = gradient_part(n, features, residual, start, rows).T + begun[at, :]
    conditioned = jnp.dot(gradient.astype(bf16), cov[...], preferred_element_type=f32)
    moved_first = beta_one * first[0, at, :] + (1.0 - beta_one) * conditioned
    moved_second = beta_two * second[0, at, :] + (1.0 - beta_two) * conditioned * conditioned
    correction_one = 1.0 - beta_one**STEP
    correction_two = 1.0 - beta_two**STEP
    moved = master[0, at, :] - (learn_rate / correction_one) * moved_first / (
        jnp.sqrt(moved_second * (1.0 / correction_two)) + 1e-08
    )
    new_first[0] = moved_first
    new_second[0] = moved_second
    new_master[0] = moved
    sent[pl.ds(pl.multiple_of(step * rows, rows), rows), :] = moved.astype(bf16)


def update(features, residual, begun, cov, master, first, second, at, steps, before, deps):
    n = len(features)
    owned, k = master.shape[1:]
    rows = min(256, owned)
    state = pl.BlockSpec((1, rows, k), lambda i: (0, at + i, 0))
    args = [*features, *residual, begun, cov, master, first, second]
    specs = [IN_VMEM] * (2 * n + 5)
    aliases = {}
    if before is not None:
        aliases = {len(args) + j: j for j in range(3)}
        args += list(before)
        specs += [ANYWHERE] * 3
    args += deps
    specs += [ANYWHERE] * len(deps)
    return pl.pallas_call(
        functools.partial(update_kernel, n, at),
        grid=(steps,),
        in_specs=specs,
        out_specs=[state, state, state, IN_VMEM],
        out_shape=[jax.ShapeDtypeStruct(master.shape, f32)] * 3
        + [jax.ShapeDtypeStruct((steps * rows, k), bf16)],
        input_output_aliases=aliases,
        compiler_params=params(),
        cost_estimate=cost(4),
        name="update",
    )(*args)


def put_kernel(blocks, owned, n_pts, p, *refs):
    n = len(blocks)
    pieces, out, sems = refs[:n], refs[-2], refs[-1]
    me = p[0]
    copies = []
    for j, (distance, other, start) in enumerate(blocks):
        rows = pieces[j].shape[0]
        home = lax.rem(me + n_pts - distance * CORES, n_pts)
        home = home + other * (1 - 2 * lax.rem(home, 2))
        at = pl.ds(pl.multiple_of(home * owned + start, rows), rows)
        copies.append(pltpu.make_async_copy(pieces[j], out.at[at, :], sems.at[j]))
    for copy in copies:
        copy.start()
    for copy in copies:
        copy.wait()


def put(p, pieces, blocks, owned, n_pts, before):
    n = len(pieces)
    k = pieces[0].shape[1]
    return pl.pallas_call(
        functools.partial(put_kernel, blocks, owned, n_pts),
        grid_spec=pltpu.PrefetchScalarGridSpec(
            num_scalar_prefetch=1,
            grid=(1,),
            in_specs=[IN_VMEM] * n + [ANYWHERE] * (before is not None),
            out_specs=ANYWHERE,
            scratch_shapes=[pltpu.SemaphoreType.DMA((n,))],
        ),
        out_shape=jax.ShapeDtypeStruct((owned * n_pts, k), bf16),
        input_output_aliases={} if before is None else {n + 1: 0},
        compiler_params=params(),
        cost_estimate=cost(0.01),
        name="put_rows",
    )(p, *pieces, *([] if before is None else [before]))


def ring(x, axis, n, distance):
    return lax.ppermute(x, axis, [(i, (i + distance) % n) for i in range(n)])


def mate(x, n):
    return lax.ppermute(x, "pts", [(i, i ^ 1) for i in range(n)])


def across(x, n, distance):
    return ring(x, "pts", n, distance * CORES)


def swap(x, n, bit):
    return lax.ppermute(x, "feat", [(i, i ^ 2**bit) for i in range(n)])


def spread(x, n):
    got = [x if d == 0 else across(x, n, d) for d in range(n // CORES)]
    return [y for g in got for y in (g, mate(g, n))]


def body(n_feat, n_pts, points, picks, omega, phase, weights, counts, master, first, second, cov):
    f = lax.axis_index("feat").astype(jnp.int32).reshape(1)
    p = lax.axis_index("pts").astype(jnp.int32).reshape(1)
    owned, k = master.shape[1:]
    points_here = 2 * picks.shape[1]
    size_one = points_here * 3 // 8
    parts = [(0, points_here - size_one), (points_here - size_one, size_one)]
    bits = n_feat.bit_length() - 1
    points, picks, phase = in_hbm(points), in_hbm(picks), phase[None, :]
    outer = counts.shape
    counts = counts.reshape(points_here, k)

    chosen, token = gather(picks, points)
    everyone = spread(chosen, n_pts)

    def some_rates(m, blocks, before, keep, ends, token):
        return rates(
            f, p, chosen, omega, phase, weights, *parts[m], owned, blocks, before, keep, ends, [token]
        )

    def add_up(kept, got, bit, token):
        last = bit == bits - 1
        *out, token = total(f, kept, got, bit, not last, [token])
        kept, sent = (out[0], out[0]) if last else out
        return kept, swap(sent, n_feat, bit), token

    def give_back(chunk):
        rows, masks = [chunk], [0]
        for bit in reversed(range(bits - 1)):
            rows = rows + [swap(r, n_feat, bit) for r in rows]
            masks = masks + [q ^ 2**bit for q in masks]
        return rows, masks

    feats_zero, own_omega, own_phase, kept_zero, sent, token = first_rates(
        f, p, chosen, in_hbm(omega), phase, in_hbm(weights), *parts[0], owned, [token]
    )
    got_zero = swap(sent, n_feat, 0)
    feats_one, begun, token = some_rates(1, (0, 1), None, False, False, token)
    for bit in range(1, bits):
        kept_zero, got_zero, token = add_up(kept_zero, got_zero, bit, token)
    kept_one, sent, token = some_rates(1, (1, 2), begun, False, True, token)
    got_one = swap(sent, n_feat, 0)
    features = [[feats_zero], [feats_one]]

    todo = [(m, j) for m in range(2) for j in range(1, n_pts)]
    share = len(todo) // 6

    def some(token, pieces, weight=1.0):
        for _ in range(pieces * share):
            m, j = todo.pop(0)
            feats, token = owned_features(
                everyone[j], own_omega, own_phase, *parts[m], weight, [token]
            )
            features[m].append(feats)
        return token

    token = some(token, 1)
    for bit in range(1, bits):
        kept_one, got_one, token = add_up(kept_one, got_one, bit, token)
    chunk, token = total(f, kept_zero, got_zero, 0, False, [token])
    rows_zero, masks = give_back(chunk)
    token = some(token, 1)
    chunk, token = total(f, kept_one, got_one, 0, False, [token])
    rows_one, masks = give_back(chunk)
    out_rates, res_zero, token = residuals(f, rows_zero, masks, counts, *parts[0], None, [token])
    far_zero = [across(res_zero, n_pts, d) for d in range(1, n_pts // CORES)]
    token = some(token, 1)
    out_rates, res_one, token = residuals(
        f, rows_one, masks, counts, *parts[1], out_rates, [token]
    )
    far_one = [across(res_one, n_pts, d) for d in range(1, n_pts // CORES)]
    token = some(token, 2, 0.1)
    *far_zero, token = lax.optimization_barrier((*far_zero, token))
    res_zero = [y for g in [res_zero] + far_zero for y in (g, mate(g, n_pts))]
    token = some(token, 1, 0.1)
    *far_one, token = lax.optimization_barrier((*far_one, token))
    res_one = [y for g in [res_one] + far_one for y in (g, mate(g, n_pts))]
    begun, token = first_part(features[0], res_zero, master, [token])

    steps = max(1, owned // 256)
    sizes = [1, 2, 2, 3] if steps == 8 else [1] * steps
    chips = n_pts // CORES
    state = None
    at = 0
    sent, come, starts = [], [], []
    for c, size in enumerate(sizes):
        *state, rows = update(
            features[1], res_one, begun, cov, master, first, second, at, size, state, [token] + (come[c - 2] if c > 1 else [])
        )
        sent.append([rows, mate(rows, n_pts)])
        come.append([across(rows, n_pts, d) for d in range(1, chips)])
        starts.append(at * (owned // steps))
        at += size
    working = None
    for group in [range(len(sizes) - 1), [len(sizes) - 1]]:
        pieces, blocks = [], []
        for c in group:
            got = come[c]
            if c and got:
                fence = sent[-1][0] if working is None else working
                *got, fence = lax.optimization_barrier((*got, fence))
                working = None if working is None else fence
            pieces += sent[c] + got + [mate(y, n_pts) for y in got]
            blocks += [(0, other, starts[c]) for other in (0, 1)]
            blocks += [(d, other, starts[c]) for other in (0, 1) for d in range(1, chips)]
        if pieces:
            working = put(p, pieces, blocks, owned, n_pts, working)
    return out_rates.reshape(outer), *state, working


def solution(mesh):
    placed = (
        P(("groups", "pts"), None),
        P(None, ("groups", "pts")),
        P(None, "feat"),
        P("feat"),
        P(("groups", "feat"), None),
        P(None, ("groups", "pts"), None),
        P(("groups", "feat"), "pts", None),
        P(("groups", "feat"), "pts", None),
        P(("groups", "feat"), "pts", None),
        P(),
    )
    return jax.shard_map(
        functools.partial(body, mesh.shape["feat"], mesh.shape["pts"]),
        mesh=mesh,
        in_specs=placed,
        out_specs=(
            P(None, ("groups", "pts"), None),
            P(("groups", "feat"), "pts", None),
            P(("groups", "feat"), "pts", None),
            P(("groups", "feat"), "pts", None),
            P(("groups", "feat"), None),
        ),
        check_vma=False,
    )
```

```python
import functools
import math

import jax
import jax.numpy as jnp
from jax import lax
from jax.experimental import pallas as pl
from jax.experimental.pallas import tpu as pltpu
from jax.sharding import PartitionSpec as P

F = 32768
STEP = 20
CORES = 2

beta_one = 0.9
beta_two = 0.999
learn_rate = 0.2

SINE = tuple(
    c * math.sqrt(2.0 / F) for c in (6.2825055774072665, -41.16644056159234, 74.4523919857074)
)
ROUNDER = 12582912.0
TURN = 1.0 / (2.0 * math.pi)
VMEM = 24 * 1024 * 1024

f32 = jnp.float32
bf16 = jnp.bfloat16
IN_VMEM = pl.BlockSpec(memory_space=pltpu.VMEM)
ANYWHERE = pl.BlockSpec(memory_space=pl.ANY)
TOKEN = jax.ShapeDtypeStruct((8, 128), f32)


def scaled_cos(product, phase_turns):
    turns = product * TURN + phase_turns
    v = 0.25 - jnp.abs(turns - ((turns + ROUNDER) - ROUNDER))
    s = v * v
    return (((SINE[2] * s + SINE[1]) * s + SINE[0]) * v).astype(bf16)


def cost(microseconds):
    return pl.CostEstimate(
        flops=int(microseconds * 1.0e9), bytes_accessed=1 << 10, transcendentals=0
    )


def params():
    return pltpu.CompilerParams(vmem_limit_bytes=VMEM)


def in_hbm(x):
    return pltpu.with_memory_space_constraint(x, pltpu.HBM)


def gather_kernel(picks, points, chosen, token):
    batch, pool = picks.shape[1], points.shape[0]
    lane = lax.broadcasted_iota(jnp.int32, (batch, 128), 1)
    for m in range(2):
        wanted = jnp.broadcast_to(picks[m : m + 1, :], (128, batch)).T
        hot = [
            jnp.where(wanted == lane + 128 * j, 1.0, 0.0).astype(bf16) for j in range(pool // 128)
        ]
        chosen[m * batch : (m + 1) * batch, :] = jnp.dot(
            jnp.concatenate(hot, axis=1), points[...], preferred_element_type=f32
        ).astype(bf16)


def gather(picks, points):
    batch = picks.shape[1]
    pool, ins = points.shape
    return pl.pallas_call(
        gather_kernel,
        grid=(1,),
        in_specs=[
            pl.BlockSpec(picks.shape, lambda i: (0, 0)),
            pl.BlockSpec((pool, ins), lambda i: (0, 0)),
        ],
        out_specs=[IN_VMEM, ANYWHERE],
        out_shape=[jax.ShapeDtypeStruct((2 * batch, ins), bf16), TOKEN],
        compiler_params=params(),
        cost_estimate=cost(3),
        name="chosen_points",
    )(picks, points)


def cosines(chosen, omega, phase, base, width, store, between=None):
    tile = min(256, width)
    count = width // tile
    group = min(512, width)

    def part(start, size):
        if isinstance(base, int):
            return slice(base + start, base + start + size)
        return pl.ds(pl.multiple_of(base + start, tile), size)

    def product(c):
        return jnp.dot(chosen, omega[:, part(c * tile, tile)], preferred_element_type=f32)

    ready = product(0)
    for c in range(count):
        coming = product(c + 1) if c + 1 < count else None
        if between is not None and c > 0 and c * tile % group == 0:
            between(c * tile - group, part(c * tile - group, group), group)
        turns = phase[:, part(c * tile, tile)] * TURN
        store(slice(c * tile, (c + 1) * tile), scaled_cos(ready, turns))
        ready = coming
    if between is not None:
        between(width - group, part(width - group, group), group)


def rates_kernel(start, size, low, high, width, own, begun, keep, ends, f, p, chosen, omega, phase, weights, *refs):
    refs = list(refs)
    total, feats = refs.pop(), refs.pop()
    before = refs.pop(0) if begun else None
    refs.pop()
    owned = None if begun else refs.pop(0)
    count = omega.shape[1] // width
    total[...] = before[...] if begun else jnp.zeros_like(total)

    def block(place, into, offset):
        parts = []

        def store(cols, value):
            into[:, offset + cols.start : offset + cols.stop] = value

        def between(at, rows, group):
            done = into[:, offset + at : offset + at + group]
            parts.append(jnp.dot(done, weights[rows, :], preferred_element_type=f32))

        cosines(
            chosen[start : start + size, :], omega, phase, place * width, width, store, between
        )
        part = parts[0]
        for q in parts[1:]:
            part = part + q
        total[...] += part

    if not begun:
        for step in range(own):
            block(p[0] * own + step, owned, step * width)

    def turn(step, _):
        block(lax.rem(step + p[0] * own, count), feats, 0)
        return _

    lax.fori_loop(low if begun else own, high, turn, 0)
    if keep:
        at = pl.ds(pl.multiple_of(p[0] * own * width, width), own * width)
        refs[0][...] = omega[:, at]
        refs[1][...] = phase[:, at]
    if ends:
        split(total, f[0], 0, *refs[-2:])
    else:
        refs[-1][...] = total[...]


def split(value, f, bit, kept, sent):
    rows = kept.shape[0]
    side = lax.rem(f // 2**bit, 2)
    kept[...] = value[pl.ds(pl.multiple_of(side * rows, rows), rows), :]
    sent[...] = value[pl.ds(pl.multiple_of((1 - side) * rows, rows), rows), :].astype(bf16)


def rates(f, p, chosen, omega, phase, weights, start, size, owned, blocks, before, keep, ends, deps):
    ins, feat_dev = omega.shape
    k = weights.shape[1]
    width = min(2048, owned)
    count = feat_dev // width
    own = owned // width
    low, high = blocks[0] * count // 2, blocks[1] * count // 2

    begun = before is not None
    outs = []
    if not begun:
        outs.append(jax.ShapeDtypeStruct((size, owned), bf16))
    if keep:
        outs += [jax.ShapeDtypeStruct((ins, owned), bf16), jax.ShapeDtypeStruct((1, owned), f32)]
    if ends:
        outs += [jax.ShapeDtypeStruct((size // 2, k), t) for t in (f32, bf16)]
    else:
        outs.append(jax.ShapeDtypeStruct((size, k), f32))
    args = [f, p, chosen, omega, phase, weights] + ([before] if begun else []) + deps

    def kernel(*refs):
        inputs = len(args) - len(deps)
        rates_kernel(
            start, size, low, high, width, own, begun, keep, ends, *refs[:inputs], *refs[inputs + len(deps) :]
        )

    return pl.pallas_call(
        kernel,
        grid_spec=pltpu.PrefetchScalarGridSpec(
            num_scalar_prefetch=2,
            grid=(1,),
            in_specs=[IN_VMEM] * (4 + begun) + [ANYWHERE] * len(deps),
            out_specs=[IN_VMEM] * len(outs) + [ANYWHERE],
            scratch_shapes=[pltpu.VMEM((size, width), bf16), pltpu.VMEM((size, k), f32)],
        ),
        out_shape=[*outs, TOKEN],
        compiler_params=params(),
        cost_estimate=cost(12 * (high - low) / count),
        name="partial_log_rates",
    )(*args)


def first_rates_kernel(start, size, own, f, p, chosen, omega, phase, weights, *refs):
    owned, own_omega, own_phase, kept, sent, _, feats, total = refs
    step = pl.program_id(0)
    width = omega.shape[1]
    parts = []

    @pl.when(step == 0)
    def _():
        total[...] = jnp.zeros_like(total)

    def store(cols, value):
        feats[:, cols] = value

    def between(at, rows, group):
        done = feats[:, at : at + group]
        parts.append(jnp.dot(done, weights[rows, :], preferred_element_type=f32))

    cosines(chosen[start : start + size, :], omega, phase, 0, width, store, between)
    part = parts[0]
    for q in parts[1:]:
        part = part + q
    total[...] += part

    @pl.when(step < own)
    def _():
        at = pl.ds(pl.multiple_of(step * width, width), width)
        owned[:, at] = feats[...]
        own_omega[:, at] = omega[...]
        own_phase[:, at] = phase[...]

    @pl.when(step == pl.num_programs(0) - 1)
    def _():
        split(total, f[0], 0, kept, sent)


def first_rates(f, p, chosen, omega, phase, weights, start, size, owned, deps):
    ins, feat_dev = omega.shape
    k = weights.shape[1]
    width = min(2048, owned)
    count = feat_dev // width
    own = owned // width

    def turned(i, p):
        return lax.rem(i + p[0] * own, count)

    def kernel(*refs):
        first_rates_kernel(start, size, own, *refs[:6], *refs[6 + len(deps) :])

    return pl.pallas_call(
        kernel,
        grid_spec=pltpu.PrefetchScalarGridSpec(
            num_scalar_prefetch=2,
            grid=(count,),
            in_specs=[
                IN_VMEM,
                pl.BlockSpec((ins, width), lambda i, f, p: (0, turned(i, p))),
                pl.BlockSpec((1, width), lambda i, f, p: (0, turned(i, p))),
                pl.BlockSpec((width, k), lambda i, f, p: (turned(i, p), 0)),
            ]
            + [ANYWHERE] * len(deps),
            out_specs=[IN_VMEM] * 5 + [ANYWHERE],
            scratch_shapes=[pltpu.VMEM((size, width), bf16), pltpu.VMEM((size, k), f32)],
        ),
        out_shape=[
            jax.ShapeDtypeStruct((size, owned), bf16),
            jax.ShapeDtypeStruct((ins, owned), bf16),
            jax.ShapeDtypeStruct((1, owned), f32),
            jax.ShapeDtypeStruct((size // 2, k), f32),
            jax.ShapeDtypeStruct((size // 2, k), bf16),
            TOKEN,
        ],
        compiler_params=params(),
        cost_estimate=cost(12),
        name="first_log_rates",
    )(f, p, chosen, omega, phase, weights, *deps)


def features_kernel(start, size, chosen, omega, phase, *refs):
    out = refs[-2]

    def store(cols, value):
        out[:, cols] = value

    cosines(chosen[start : start + size, :], omega, phase, 0, omega.shape[1], store)


def owned_features(chosen, omega, phase, start, size, weight, deps):
    owned = omega.shape[1]
    return pl.pallas_call(
        functools.partial(features_kernel, start, size),
        in_specs=[IN_VMEM] * 3 + [ANYWHERE] * len(deps),
        out_specs=[IN_VMEM, ANYWHERE],
        out_shape=[jax.ShapeDtypeStruct((size, owned), bf16), TOKEN],
        compiler_params=params(),
        cost_estimate=cost(weight),
        name="owned_features",
    )(chosen, omega, phase, *deps)


def total_kernel(bit, halves, f, a, b, *refs):
    value = a[...].astype(f32) + b[...].astype(f32)
    if halves:
        kept, sent, token, held = refs[-4:]
        held[...] = value
        split(held, f[0], bit, kept, sent)
    else:
        out, token = refs[-2:]
        out[...] = value.astype(bf16)


def total(f, a, b, bit, halves, deps):
    rows, k = a.shape
    if halves:
        outs = [
            jax.ShapeDtypeStruct((rows // 2, k), f32),
            jax.ShapeDtypeStruct((rows // 2, k), bf16),
        ]
    else:
        outs = [jax.ShapeDtypeStruct((rows, k), bf16)]
    return pl.pallas_call(
        functools.partial(total_kernel, bit, halves),
        grid_spec=pltpu.PrefetchScalarGridSpec(
            num_scalar_prefetch=1,
            grid=(1,),
            in_specs=[IN_VMEM] * 2 + [ANYWHERE] * len(deps),
            out_specs=[IN_VMEM] * len(outs) + [ANYWHERE],
            scratch_shapes=[pltpu.VMEM((rows, k), f32)] if halves else [],
        ),
        out_shape=[*outs, TOKEN],
        compiler_params=params(),
        cost_estimate=cost(0.5),
        name="total_rates",
    )(f, a, b, *deps)


def residual_kernel(masks, start, f, *refs):
    chunks, observed = refs[: len(masks)], refs[len(masks)]
    rate_out, residual_out, token, rates, held, sem = refs[-6:]
    size = held.shape[0]
    for j, mask in enumerate(masks):
        rows = chunks[j].shape[0]
        first, bit = 0, 0
        while size >> (bit + 1) >= rows:
            side = lax.rem(f[0] // 2**bit, 2)
            side = 1 - side if mask >> bit & 1 else side
            first = first + side * (size >> (bit + 1))
            bit += 1
        at = pl.ds(pl.multiple_of(first, rows), rows) if bit else slice(None)
        rates[at, :] = chunks[j][...].astype(f32)
    copy = pltpu.make_async_copy(rates, rate_out.at[pl.ds(start, size), :], sem)
    copy.start()
    held[...] = jnp.exp(rates[...]) - observed[start : start + size, :].astype(f32)
    residual_out[...] = held[...].T.astype(bf16)
    copy.wait()


def residuals(f, chunks, masks, counts, start, size, before, deps):
    n = len(chunks)
    k = counts.shape[1]
    args = [f, *chunks, counts, *deps]
    specs = [IN_VMEM] * (n + 1) + [ANYWHERE] * len(deps)
    aliases = {}
    if before is not None:
        aliases = {len(args): 0}
        args.append(before)
        specs.append(ANYWHERE)
    return pl.pallas_call(
        functools.partial(residual_kernel, masks, start),
        grid_spec=pltpu.PrefetchScalarGridSpec(
            num_scalar_prefetch=1,
            grid=(1,),
            in_specs=specs,
            out_specs=[ANYWHERE, IN_VMEM, ANYWHERE],
            scratch_shapes=[pltpu.VMEM((size, k), f32)] * 2 + [pltpu.SemaphoreType.DMA],
        ),
        out_shape=[
            jax.ShapeDtypeStruct(counts.shape, f32),
            jax.ShapeDtypeStruct((k, size), bf16),
            TOKEN,
        ],
        input_output_aliases=aliases,
        compiler_params=params(),
        cost_estimate=cost(1),
        name="residuals",
    )(*args)


def gradient_part(n, features, residual, start, rows):
    at = slice(start, start + rows) if isinstance(start, int) else pl.ds(pl.multiple_of(start, rows), rows)
    value = None
    for j in range(n):
        term = jnp.dot(residual[j][...], features[j][:, at], preferred_element_type=f32)
        value = term if value is None else value + term
    return value


def first_part_kernel(n, *refs):
    features, residual, master = refs[:n], refs[n : 2 * n], refs[2 * n]
    out = refs[-2]
    rows = min(512, out.shape[0])
    for start in range(0, out.shape[0], rows):
        value = gradient_part(n, features, residual, start, rows).T
        out[start : start + rows, :] = value + master[0, start : start + rows, :]


def first_part(features, residual, master, deps):
    n = len(features)
    owned, k = master.shape[1:]
    return pl.pallas_call(
        functools.partial(first_part_kernel, n),
        in_specs=[IN_VMEM] * (2 * n + 1) + [ANYWHERE] * len(deps),
        out_specs=[IN_VMEM, ANYWHERE],
        out_shape=[jax.ShapeDtypeStruct((owned, k), f32), TOKEN],
        compiler_params=params(),
        cost_estimate=cost(0.3),
        name="first_part",
    )(*features, *residual, master, *deps)


def update_kernel(n, begin, *refs):
    features, residual = refs[:n], refs[n : 2 * n]
    begun, cov, master, first, second = refs[2 * n : 2 * n + 5]
    new_master, new_first, new_second, sent = refs[-4:]
    rows = new_master.shape[1]
    step = pl.program_id(0)
    start = pl.multiple_of((begin + step) * rows, rows)
    at = pl.ds(start, rows)
    gradient = gradient_part(n, features, residual, start, rows).T + begun[at, :]
    conditioned = jnp.dot(gradient.astype(bf16), cov[...], preferred_element_type=f32)
    moved_first = beta_one * first[0, at, :] + (1.0 - beta_one) * conditioned
    moved_second = beta_two * second[0, at, :] + (1.0 - beta_two) * conditioned * conditioned
    correction_one = 1.0 - beta_one**STEP
    correction_two = 1.0 - beta_two**STEP
    moved = master[0, at, :] - (learn_rate / correction_one) * moved_first / (
        jnp.sqrt(moved_second * (1.0 / correction_two)) + 1e-08
    )
    new_first[0] = moved_first
    new_second[0] = moved_second
    new_master[0] = moved
    sent[pl.ds(pl.multiple_of(step * rows, rows), rows), :] = moved.astype(bf16)


def update(features, residual, begun, cov, master, first, second, at, steps, before, deps):
    n = len(features)
    owned, k = master.shape[1:]
    rows = min(256, owned)
    state = pl.BlockSpec((1, rows, k), lambda i: (0, at + i, 0))
    args = [*features, *residual, begun, cov, master, first, second]
    specs = [IN_VMEM] * (2 * n + 5)
    aliases = {}
    if before is not None:
        aliases = {len(args) + j: j for j in range(3)}
        args += list(before)
        specs += [ANYWHERE] * 3
    args += deps
    specs += [ANYWHERE] * len(deps)
    return pl.pallas_call(
        functools.partial(update_kernel, n, at),
        grid=(steps,),
        in_specs=specs,
        out_specs=[state, state, state, IN_VMEM],
        out_shape=[jax.ShapeDtypeStruct(master.shape, f32)] * 3
        + [jax.ShapeDtypeStruct((steps * rows, k), bf16)],
        input_output_aliases=aliases,
        compiler_params=params(),
        cost_estimate=cost(4),
        name="update",
    )(*args)


def put_kernel(blocks, owned, n_pts, p, *refs):
    n = len(blocks)
    pieces, out, sems = refs[:n], refs[-2], refs[-1]
    me = p[0]
    copies = []
    for j, (distance, other, start) in enumerate(blocks):
        rows = pieces[j].shape[0]
        home = lax.rem(me + n_pts - distance * CORES, n_pts)
        home = home + other * (1 - 2 * lax.rem(home, 2))
        at = pl.ds(pl.multiple_of(home * owned + start, rows), rows)
        copies.append(pltpu.make_async_copy(pieces[j], out.at[at, :], sems.at[j]))
    for copy in copies:
        copy.start()
    for copy in copies:
        copy.wait()


def put(p, pieces, blocks, owned, n_pts, before):
    n = len(pieces)
    k = pieces[0].shape[1]
    return pl.pallas_call(
        functools.partial(put_kernel, blocks, owned, n_pts),
        grid_spec=pltpu.PrefetchScalarGridSpec(
            num_scalar_prefetch=1,
            grid=(1,),
            in_specs=[IN_VMEM] * n + [ANYWHERE] * (before is not None),
            out_specs=ANYWHERE,
            scratch_shapes=[pltpu.SemaphoreType.DMA((n,))],
        ),
        out_shape=jax.ShapeDtypeStruct((owned * n_pts, k), bf16),
        input_output_aliases={} if before is None else {n + 1: 0},
        compiler_params=params(),
        cost_estimate=cost(0.01),
        name="put_rows",
    )(p, *pieces, *([] if before is None else [before]))


def ring(x, axis, n, distance):
    return lax.ppermute(x, axis, [(i, (i + distance) % n) for i in range(n)])


def mate(x, n):
    return lax.ppermute(x, "pts", [(i, i ^ 1) for i in range(n)])


def across(x, n, distance):
    return ring(x, "pts", n, distance * CORES)


def swap(x, n, bit):
    return lax.ppermute(x, "feat", [(i, i ^ 2**bit) for i in range(n)])


def spread(x, n):
    got = [x if d == 0 else across(x, n, d) for d in range(n // CORES)]
    return [y for g in got for y in (g, mate(g, n))]


def body(n_feat, n_pts, points, picks, omega, phase, weights, counts, master, first, second, cov):
    f = lax.axis_index("feat").astype(jnp.int32).reshape(1)
    p = lax.axis_index("pts").astype(jnp.int32).reshape(1)
    owned, k = master.shape[1:]
    points_here = 2 * picks.shape[1]
    size_one = points_here // 2
    parts = [(0, points_here - size_one), (points_here - size_one, size_one)]
    bits = n_feat.bit_length() - 1
    points, picks, phase = in_hbm(points), in_hbm(picks), phase[None, :]
    outer = counts.shape
    counts = counts.reshape(points_here, k)

    chosen, token = gather(picks, points)
    everyone = spread(chosen, n_pts)

    def some_rates(m, blocks, before, keep, ends, token):
        return rates(
            f, p, chosen, omega, phase, weights, *parts[m], owned, blocks, before, keep, ends, [token]
        )

    def add_up(kept, got, bit, token):
        last = bit == bits - 1
        *out, token = total(f, kept, got, bit, not last, [token])
        kept, sent = (out[0], out[0]) if last else out
        return kept, swap(sent, n_feat, bit), token

    def give_back(chunk):
        rows, masks = [chunk], [0]
        for bit in reversed(range(bits - 1)):
            rows = rows + [swap(r, n_feat, bit) for r in rows]
            masks = masks + [q ^ 2**bit for q in masks]
        return rows, masks

    feats_zero, own_omega, own_phase, kept_zero, sent, token = first_rates(
        f, p, chosen, in_hbm(omega), phase, in_hbm(weights), *parts[0], owned, [token]
    )
    got_zero = swap(sent, n_feat, 0)
    feats_one, begun, token = some_rates(1, (0, 1), None, False, False, token)
    for bit in range(1, bits):
        kept_zero, got_zero, token = add_up(kept_zero, got_zero, bit, token)
    kept_one, sent, token = some_rates(1, (1, 2), begun, False, True, token)
    got_one = swap(sent, n_feat, 0)
    features = [[feats_zero], [feats_one]]

    todo = [(m, j) for m in range(2) for j in range(1, n_pts)]
    share = len(todo) // 6

    def some(token, pieces, weight=1.0):
        for _ in range(pieces * share):
            m, j = todo.pop(0)
            feats, token = owned_features(
                everyone[j], own_omega, own_phase, *parts[m], weight, [token]
            )
            features[m].append(feats)
        return token

    chunk, token = total(f, kept_zero, got_zero, 0, False, [token])
    rows_zero, masks = give_back(chunk)
    token = some(token, 1)
    for bit in range(1, bits):
        kept_one, got_one, token = add_up(kept_one, got_one, bit, token)
    token = some(token, 1)
    chunk, token = total(f, kept_one, got_one, 0, False, [token])
    rows_one, masks = give_back(chunk)
    out_rates, res_zero, token = residuals(f, rows_zero, masks, counts, *parts[0], None, [token])
    far_zero = [across(res_zero, n_pts, d) for d in range(1, n_pts // CORES)]
    token = some(token, 1)
    out_rates, res_one, token = residuals(
        f, rows_one, masks, counts, *parts[1], out_rates, [token]
    )
    far_one = [across(res_one, n_pts, d) for d in range(1, n_pts // CORES)]
    token = some(token, 2, 0.1)
    *far_zero, token = lax.optimization_barrier((*far_zero, token))
    res_zero = [y for g in [res_zero] + far_zero for y in (g, mate(g, n_pts))]
    token = some(token, 1, 0.1)
    *far_one, token = lax.optimization_barrier((*far_one, token))
    res_one = [y for g in [res_one] + far_one for y in (g, mate(g, n_pts))]
    begun, token = first_part(features[0], res_zero, master, [token])

    steps = max(1, owned // 256)
    sizes = [1, 2, 2, 3] if steps == 8 else [1] * steps
    chips = n_pts // CORES
    state = None
    at = 0
    sent, come, starts = [], [], []
    for c, size in enumerate(sizes):
        *state, rows = update(
            features[1], res_one, begun, cov, master, first, second, at, size, state, [token] + (come[c - 2] if c > 1 else [])
        )
        sent.append([rows, mate(rows, n_pts)])
        come.append([across(rows, n_pts, d) for d in range(1, chips)])
        starts.append(at * (owned // steps))
        at += size
    working = None
    for group in [range(len(sizes) - 1), [len(sizes) - 1]]:
        pieces, blocks = [], []
        for c in group:
            got = come[c]
            if c and got:
                fence = sent[-1][0] if working is None else working
                *got, fence = lax.optimization_barrier((*got, fence))
                working = None if working is None else fence
            pieces += sent[c] + got + [mate(y, n_pts) for y in got]
            blocks += [(0, other, starts[c]) for other in (0, 1)]
            blocks += [(d, other, starts[c]) for other in (0, 1) for d in range(1, chips)]
        if pieces:
            working = put(p, pieces, blocks, owned, n_pts, working)
    return out_rates.reshape(outer), *state, working


def solution(mesh):
    placed = (
        P(("groups", "pts"), None),
        P(None, ("groups", "pts")),
        P(None, "feat"),
        P("feat"),
        P(("groups", "feat"), None),
        P(None, ("groups", "pts"), None),
        P(("groups", "feat"), "pts", None),
        P(("groups", "feat"), "pts", None),
        P(("groups", "feat"), "pts", None),
        P(),
    )
    return jax.shard_map(
        functools.partial(body, mesh.shape["feat"], mesh.shape["pts"]),
        mesh=mesh,
        in_specs=placed,
        out_specs=(
            P(None, ("groups", "pts"), None),
            P(("groups", "feat"), "pts", None),
            P(("groups", "feat"), "pts", None),
            P(("groups", "feat"), "pts", None),
            P(("groups", "feat"), None),
        ),
        check_vma=False,
    )
```
